32 devices in a mesh: rows: 8 (over z, x), heads: 4 (over y, core).
Axes of the slice: x: 2, y: 2, z: 4, core: 2. Of those that a mesh axis runs over, the one named last changes fastest.
Arguments:
- inputs: bfloat16 [4096, 512], P('rows'), may hold values from -6 to 6
- key_weight: bfloat16 [512, 1024], P(None, 'heads'), may hold values from -0.25 to 0.25
- value_weight: bfloat16 [512, 1024], P(None, 'heads'), may hold values from -0.25 to 0.25
- queries: bfloat16 [2, 1024, 1024], P(None, None, 'heads'), may hold values from -100 to 100
- out_grad: bfloat16 [2, 1024, 1024], P(None, None, 'heads'), may hold values from -3072 to 3072
Outputs:
- query_grad: float32 [2, 1024, 1024], P(None, 'rows', 'heads')
- key_weight_grad: float32 [512, 1024], P(None, 'heads')
- value_weight_grad: float32 [512, 1024], P(None, 'heads')
- input_grad: float32 [4096, 512], P('rows', 'heads')
The draws below stay inside these ranges and needn't reach their ends.
All inputs are finite; a program needn't handle non-finite values.
Results may differ from the reference program's by a relative error of at most 0.003.
The reference program's roundings to bfloat16 on the way count: a program that leaves them out, or rounds other values in their place, can miss the bound.
Values sent between devices are 32-bit elements; how exact they have to be, the bound alone decides.
No kernel may reach another device: no remote copies, remote signals or barrier semaphores. Data moves between devices by JAX's collectives and lax.ppermute only.
A program may use at most 64 MiB of HBM per device.

```python
import jax
import jax.numpy as jnp
from jax import lax

D_IN = 512
LAT = 1024
HEADS = 8
HD = 128
READS = 2
NROWS = 4096


def draw_queries(key, part):
    key = jax.random.fold_in(key, 11)
    first_key = jax.random.fold_in(key, 0)
    shape = (READS, LAT, HEADS * HD)
    base = jax.random.normal(first_key, shape, jnp.float32)
    return jnp.clip(base, -6.0, 6.0).astype(jnp.bfloat16)


def levels(own_key, shape, shards, smallest, high):
    factor_of, own = 1.0, jax.random.fold_in(own_key, 6)
    for position, shards_of in shards:
        draws = jnp.exp(jax.random.uniform(jax.random.fold_in(own, position), (shards_of,), jnp.float32, smallest / len(shards), high / len(shards)))
        factor_of = factor_of * jnp.repeat(draws, shape[position] // shards_of).reshape([-1 if axis == position else 1 for axis in range(len(shape))])
    return factor_of


def scatter_about(stream_key, dims, deviation, bound, cuts=(), held_as=jnp.bfloat16):
    gain = levels(stream_key, dims, cuts, -0.22, 0.18) if cuts else 1.0
    result = jax.random.normal(stream_key, dims, jnp.float32) * deviation * gain
    return jnp.minimum(jnp.maximum(result, -bound), bound).astype(held_as)


def setup_inputs(seed: int = 0) -> dict:
    arg_keys = jax.random.split(jax.random.key(seed), 6)
    inputs = scatter_about(arg_keys[0], (NROWS, D_IN), 1.0, 6.0, ((0, 8),))
    key_weight = scatter_about(arg_keys[1], (D_IN, HEADS * HD), D_IN ** -0.5, 0.25, ((1, 4),))
    value_weight = scatter_about(arg_keys[2], (D_IN, HEADS * HD), D_IN ** -0.5, 0.25, ((1, 4),))
    queries = draw_queries(jax.random.fold_in(arg_keys[5], 71), 0)
    out_grad = scatter_about(arg_keys[4], (READS, LAT, HEADS * HD), 512.0, 3072.0, ((2, 4),))
    return dict(inputs=inputs, key_weight=key_weight, value_weight=value_weight, queries=queries, out_grad=out_grad)


def reference(inputs, key_weight, value_weight, queries, out_grad):
    keys = jnp.dot(inputs, key_weight, preferred_element_type=jnp.float32).astype(jnp.bfloat16)
    values = jnp.dot(inputs, value_weight, preferred_element_type=jnp.float32).astype(jnp.bfloat16)
    factor = HD ** -0.5

    def one_head(head_index):
        start = (head_index * HD).astype(jnp.int32)
        key_block = lax.dynamic_slice_in_dim(keys, start, HD, 1)
        value_block = lax.dynamic_slice_in_dim(values, start, HD, 1)
        query_heads = lax.dynamic_slice_in_dim(queries, start, HD, 2)
        grad_heads = lax.dynamic_slice_in_dim(out_grad, start, HD, 2)

        def one_read(carry, pair):
            query_block, grad_block = pair
            scores = jnp.dot(query_block, key_block.T, preferred_element_type=jnp.float32) * factor
            probs = jax.nn.softmax(scores, axis=-1)
            weighted = jnp.dot(grad_block, value_block.T, preferred_element_type=jnp.float32)
            delta = jnp.sum(probs * weighted, axis=-1, keepdims=True)
            score_grad = (probs * (weighted - delta) * factor).astype(jnp.bfloat16)
            latent_grad = jnp.dot(score_grad, key_block, preferred_element_type=jnp.float32)
            key_acc = carry[0] + jnp.dot(score_grad.T, query_block, preferred_element_type=jnp.float32)
            value_acc = carry[1] + jnp.dot(probs.astype(jnp.bfloat16).T, grad_block, preferred_element_type=jnp.float32)
            return (key_acc, value_acc), latent_grad

        zeros = jnp.zeros((NROWS, HD), jnp.float32)
        (key_acc, value_acc), latent_grads = lax.scan(one_read, (zeros, zeros), (query_heads, grad_heads))
        return key_acc, value_acc, latent_grads

    key_parts, value_parts, latent_parts = lax.map(one_head, jnp.arange(HEADS, dtype=jnp.int32))
    key_grad = key_parts.transpose(1, 0, 2).reshape(NROWS, HEADS * HD).astype(jnp.bfloat16)
    value_grad = value_parts.transpose(1, 0, 2).reshape(NROWS, HEADS * HD).astype(jnp.bfloat16)
    query_grad = latent_parts.transpose(1, 2, 0, 3).reshape(READS, LAT, HEADS * HD)
    key_weight_grad = jnp.dot(inputs.T, key_grad, preferred_element_type=jnp.float32)
    value_weight_grad = jnp.dot(inputs.T, value_grad, preferred_element_type=jnp.float32)
    input_grad = (jnp.dot(key_grad, key_weight.T, preferred_element_type=jnp.float32)
                  + jnp.dot(value_grad, value_weight.T, preferred_element_type=jnp.float32))
    return query_grad, key_weight_grad, value_weight_grad, input_grad
```

```python
import jax
import jax.numpy as jnp
from jax import lax
from jax.sharding import PartitionSpec as P

HD = 128


def last_contract(left, right):
    return lax.dot_general(
        left, right, (((1,), (1,)), ((), ())), preferred_element_type=jnp.float32
    )


def rows_contract(left, right):
    return lax.dot_general(
        left, right, (((0,), (0,)), ((), ())), preferred_element_type=jnp.float32
    )


def swap(array, axis, count, bit):
    pairs = [(device, device ^ bit) for device in range(count)]
    return lax.ppermute(array, axis, pairs)


def bits_of(count):
    bit = 1
    while bit < count:
        yield bit
        bit *= 2


def scatter_sum(array, axis, count):
    for bit in bits_of(count):
        halves = array.reshape((array.shape[0] // 2, 2) + array.shape[1:])
        array = halves[:, 0] + swap(halves[:, 1], axis, count, bit)
    return array[0]


def gather_all(array, axis, count):
    array = array[None]
    for bit in reversed(list(bits_of(count))):
        theirs = swap(array, axis, count, bit)
        array = jnp.stack([array, theirs], axis=1).reshape((-1,) + array.shape[1:])
    return array


def on_device(row_devices, head_devices, inputs, key_weight, value_weight, queries, out_grad):
    me = lax.axis_index("rows")
    order = me ^ jnp.arange(row_devices, dtype=jnp.int32)
    reads, latents, columns = queries.shape
    piece = latents // row_devices

    def reorder(array):
        blocks = array.reshape(reads, row_devices, piece, columns)
        return jnp.take(blocks, order, axis=1).reshape(array.shape)

    queries = reorder(queries)
    out_grad = reorder(out_grad)
    keys = jnp.dot(inputs, key_weight, preferred_element_type=jnp.float32).astype(jnp.bfloat16)
    values = jnp.dot(inputs, value_weight, preferred_element_type=jnp.float32).astype(jnp.bfloat16)
    head_count = columns // HD
    factor = HD ** (-0.5)

    def block_terms(read_index, head_index):
        lower = head_index * HD
        upper = lower + HD
        query_block = queries[read_index, :, lower:upper]
        grad_block = out_grad[read_index, :, lower:upper]
        key_block = keys[:, lower:upper]
        scores = last_contract(query_block, key_block) * factor
        weighted = last_contract(grad_block, values[:, lower:upper])
        return (query_block, grad_block, key_block, scores, weighted)

    top_list = []
    total_list = []
    accum_list = []
    for read_index in range(reads):
        for head_index in range(head_count):
            terms = block_terms(read_index, head_index)
            scores = terms[3]
            local_top = jnp.max(scores, axis=1)
            expos = jnp.exp(scores - local_top[:, None])
            top_list.append(local_top)
            total_list.append(jnp.sum(expos, axis=1))
            accum_list.append(jnp.sum(expos * terms[4], axis=1))
    stats = jnp.stack([jnp.stack(top_list), jnp.stack(total_list), jnp.stack(accum_list)])
    for bit in bits_of(row_devices):
        shape = (3, reads * head_count, row_devices // (2 * bit), 2, bit * piece)
        theirs = swap(stats, "rows", row_devices, bit).reshape(shape)
        theirs = jnp.flip(theirs, axis=3).reshape(stats.shape)
        top = jnp.maximum(stats[0], theirs[0])
        mine_scale = jnp.exp(stats[0] - top)
        their_scale = jnp.exp(theirs[0] - top)
        stats = jnp.stack([
            top,
            stats[1] * mine_scale + theirs[1] * their_scale,
            stats[2] * mine_scale + theirs[2] * their_scale,
        ])
    global_top = stats[0]
    inverse = 1.0 / stats[1]
    delta = stats[2] * inverse
    row_count = inputs.shape[0]
    key_accs = [jnp.zeros((row_count, HD), jnp.float32) for head_index in range(head_count)]
    value_accs = [jnp.zeros((row_count, HD), jnp.float32) for head_index in range(head_count)]
    pieces = []
    for read_index in range(reads):
        latent_cols = []
        for head_index in range(head_count):
            position = read_index * head_count + head_index
            query_block, grad_block, key_block, scores, weighted = block_terms(
                read_index, head_index
            )
            probs = jnp.exp(scores - global_top[position][:, None]) * inverse[position][:, None]
            score_grad = (probs * (weighted - delta[position][:, None]) * factor).astype(
                jnp.bfloat16
            )
            latent_cols.append(jnp.dot(score_grad, key_block, preferred_element_type=jnp.float32))
            key_accs[head_index] = key_accs[head_index] + rows_contract(score_grad, query_block)
            value_accs[head_index] = value_accs[head_index] + rows_contract(
                probs.astype(jnp.bfloat16), grad_block
            )
        latent_grad = jnp.concatenate(latent_cols, axis=1)
        pieces.append(scatter_sum(latent_grad.reshape(row_devices, piece, columns), "rows", row_devices))
    query_grad = jnp.stack(pieces)
    key_grad = jnp.concatenate(key_accs, axis=1).astype(jnp.bfloat16)
    value_grad = jnp.concatenate(value_accs, axis=1).astype(jnp.bfloat16)

    weights = jnp.concatenate(
        [rows_contract(inputs, key_grad), rows_contract(inputs, value_grad)], axis=1
    )
    features = inputs.shape[1]
    blocks = weights.reshape(row_devices, features // row_devices, 2 * columns)
    mine = scatter_sum(jnp.take(blocks, order, axis=0), "rows", row_devices)
    gathered = jnp.take(gather_all(mine, "rows", row_devices), order, axis=0)
    gathered = gathered.reshape(features, 2 * columns)

    partial_input = last_contract(key_grad, key_weight) + last_contract(value_grad, value_weight)
    place = lax.axis_index("heads")
    head_order = place ^ jnp.arange(head_devices, dtype=jnp.int32)
    parts = partial_input.reshape(row_count, head_devices, features // head_devices)
    parts = jnp.take(parts.transpose(1, 0, 2), head_order, axis=0)
    input_grad = scatter_sum(parts, "heads", head_devices)
    return (query_grad, gathered[:, :columns], gathered[:, columns:], input_grad)


def solution(mesh):
    in_specs = (
        P("rows", None),
        P(None, "heads"),
        P(None, "heads"),
        P(None, None, "heads"),
        P(None, None, "heads"),
    )
    out_specs = (P(None, "rows", "heads"), P(None, "heads"), P(None, "heads"), P("rows", "heads"))

    def body(*args):
        return on_device(mesh.shape["rows"], mesh.shape["heads"], *args)

    return jax.shard_map(body, mesh=mesh, in_specs=in_specs, out_specs=out_specs, check_vma=False)
```

```python
import functools

import jax
import jax.numpy as jnp
from jax import lax
from jax.experimental import pallas as pl
from jax.experimental.pallas import tpu as pltpu
from jax.sharding import PartitionSpec as P

HD = 128
GROUPS = 8
FACTOR = HD ** (-0.5)
LOG2_E = 1.4426950408889634
VMEM = pl.BlockSpec(memory_space=pltpu.VMEM)
PARAMS = pltpu.CompilerParams(vmem_limit_bytes=48 * 1024 * 1024)


def last_contract(left, right):
    return lax.dot_general(
        left, right, (((1,), (1,)), ((), ())), preferred_element_type=jnp.float32
    )


def rows_contract(left, right):
    return lax.dot_general(
        left, right, (((0,), (0,)), ((), ())), preferred_element_type=jnp.float32
    )


def plain_dot(left, right):
    return jnp.dot(left, right, preferred_element_type=jnp.float32)


def swap(array, axis, count, bit):
    pairs = [(device, device ^ bit) for device in range(count)]
    return lax.ppermute(array, axis, pairs)


def bits_of(count):
    return [1 << place for place in range(count.bit_length() - 1)]


def project_kernel(tile, inputs, key_weight, value_weight, queries, out_grad, keys, values, stats):
    reads, latents, columns = queries.shape
    head_count = columns // HD
    rows = inputs[...]
    keys[...] = plain_dot(rows, key_weight[...]).astype(jnp.bfloat16)
    values[...] = plain_dot(rows, value_weight[...]).astype(jnp.bfloat16)
    for read_index in range(reads):
        for head_index in range(head_count):
            cols = slice(head_index * HD, (head_index + 1) * HD)
            position = read_index * head_count + head_index

            @pl.loop(0, latents // tile)
            def _(step):
                at = pl.ds(pl.multiple_of(step * tile, tile), tile)
                scores = last_contract(keys[:, cols], queries[read_index, at, cols])
                scores = scores * (FACTOR * LOG2_E)
                weighted = last_contract(values[:, cols], out_grad[read_index, at, cols])
                top = jnp.max(scores, axis=0, keepdims=True)
                expos = jnp.exp2(scores - top)
                total = jnp.sum(expos, axis=0, keepdims=True)
                accum = jnp.sum(expos * weighted, axis=0, keepdims=True)
                stats[position : position + 1, at] = top + jnp.log2(total)
                lower = reads * head_count + position
                stats[lower : lower + 1, at] = accum / total


def merge_kernel(mine, theirs, merged):
    blocks = mine.shape[0] // 2
    own, other = mine[:blocks], theirs[:blocks]
    top = jnp.maximum(own, other)
    own_share = jnp.exp2(own - top)
    other_share = jnp.exp2(other - top)
    total = own_share + other_share
    merged[:blocks] = top + jnp.log2(total)
    merged[blocks:] = (mine[blocks:] * own_share + theirs[blocks:] * other_share) / total


def head_kernel(head_index, row_axis, head_axis, low, last, *refs):
    (inputs, keys, values, queries, out_grad, stats) = refs[:6]
    if last:
        (key_weight, value_weight, other_grads) = refs[6:9]
        (grads, query_keep, query_send, weight_keep, weight_send, input_keep, input_send) = refs[9:16]
        key_acc, value_acc, tile_ref, weights_ref, input_ref = refs[16:]
    else:
        (grads, query_keep, query_send, weight_keep, weight_send) = refs[6:11]
        key_acc, value_acc, tile_ref, weights_ref = refs[11:]
    reads, latents, _ = queries.shape
    head_count = stats.shape[0] // (2 * reads)
    pairs = GROUPS // 2
    tile = latents // pairs
    half = tile // 2
    me = lax.axis_index(row_axis) // low
    side = lax.rem(me, 2)
    mine = pl.ds(pl.multiple_of(side * half, half), half)
    yours = pl.ds(pl.multiple_of((1 - side) * half, half), half)
    key_acc[...] = jnp.zeros_like(key_acc)
    value_acc[...] = jnp.zeros_like(value_acc)
    for read_index in range(reads):
        position = read_index * head_count + head_index
        lower = reads * head_count + position

        @pl.loop(0, pairs)
        def _(slot):
            relative = (slot // (pairs // 2)) + 2 * lax.rem(slot, pairs // 2)
            pair = (me // 2) ^ relative
            at = pl.ds(pl.multiple_of(pair * tile, tile), tile)
            query_block = queries[read_index, at, :]
            grad_block = out_grad[read_index, at, :]
            scores = last_contract(keys[...], query_block) * (FACTOR * LOG2_E)
            weighted = last_contract(values[...], grad_block)
            probs = jnp.exp2(scores - stats[position : position + 1, at])
            score_grad = (probs * (weighted - stats[lower : lower + 1, at]) * FACTOR).astype(
                jnp.bfloat16
            )
            key_acc[...] += plain_dot(score_grad, query_block)
            value_acc[...] += plain_dot(probs.astype(jnp.bfloat16), grad_block)
            tile_ref[...] = rows_contract(score_grad, keys[...])
            query_keep[slot, read_index] = tile_ref[mine, :]
            query_send[slot, read_index] = tile_ref[yours, :]

    grads[:, :HD] = key_acc[...].astype(jnp.bfloat16)
    grads[:, HD:] = value_acc[...].astype(jnp.bfloat16)
    weights_ref[...] = rows_contract(inputs[...], grads[...])
    features = inputs.shape[1]
    piece = features // GROUPS
    for slot in range(pairs):
        relative = (slot // (pairs // 2)) + 2 * (slot % (pairs // 2))
        base = 2 * ((me // 2) ^ relative)
        weight_keep[slot] = weights_ref[pl.ds(pl.multiple_of((base + side) * piece, piece), piece), :]
        weight_send[slot] = weights_ref[
            pl.ds(pl.multiple_of((base + 1 - side) * piece, piece), piece), :
        ]
    if last:
        total = last_contract(grads[:, :HD], key_weight[:, HD:])
        total += last_contract(grads[:, HD:], value_weight[:, HD:])
        total += last_contract(other_grads[:, :HD], key_weight[:, :HD])
        total += last_contract(other_grads[:, HD:], value_weight[:, :HD])
        input_ref[...] = total
        place = lax.axis_index(head_axis)
        width = features // (2 * input_keep.shape[0])
        for relative in range(2 * input_keep.shape[0]):
            ref = input_send if relative % 2 else input_keep
            start = pl.multiple_of((place ^ relative) * width, width)
            ref[relative // 2] = input_ref[:, pl.ds(start, width)]


def assemble_kernel(row_axis, low, *refs):
    key_out, value_out = refs[-2:]
    piece = key_out.shape[0] // GROUPS
    me = lax.axis_index(row_axis) // low
    for head_index in range((len(refs) - 2) // 2):
        near, far = refs[2 * head_index : 2 * head_index + 2]
        cols = slice(head_index * HD, (head_index + 1) * HD)
        for slot in range(GROUPS // 2):
            relative = 2 * (slot // (GROUPS // 4) + 2 * (slot % (GROUPS // 4)))
            start = pl.multiple_of((me ^ relative) * piece, piece)
            key_out[pl.ds(start, piece), cols] = near[slot, :, :HD]
            value_out[pl.ds(start, piece), cols] = near[slot, :, HD:]
            start = pl.multiple_of((me ^ (relative + 1)) * piece, piece)
            key_out[pl.ds(start, piece), cols] = far[slot, :, :HD]
            value_out[pl.ds(start, piece), cols] = far[slot, :, HD:]


def shape_of(shape, dtype=jnp.float32):
    return jax.ShapeDtypeStruct(shape, dtype)


def reduce_bits(keep, send, count, bits):
    for index, bit in enumerate(bits):
        theirs = swap(send, "rows", count, bit)
        if index + 1 == len(bits):
            return keep + theirs
        middle = keep.shape[0] // 2
        send = keep[middle:] + theirs[middle:]
        keep = keep[:middle] + theirs[:middle]


def on_device(row_devices, head_devices, inputs, key_weight, value_weight, queries, out_grad):
    reads, latents, columns = queries.shape
    head_count = columns // HD
    row_count, features = inputs.shape
    blocks = reads * head_count
    low = row_devices // GROUPS
    group_bits = [bit * low for bit in bits_of(GROUPS)]
    tile = latents // (GROUPS // 2)

    keys, values, stats = pl.pallas_call(
        functools.partial(project_kernel, tile),
        out_shape=(
            shape_of((row_count, columns), jnp.bfloat16),
            shape_of((row_count, columns), jnp.bfloat16),
            shape_of((2 * blocks, latents)),
        ),
        in_specs=[VMEM] * 5,
        out_specs=(VMEM,) * 3,
        compiler_params=PARAMS,
        name="project",
    )(inputs, key_weight, value_weight, queries, out_grad)

    for bit in bits_of(row_devices):
        theirs = swap(stats, "rows", row_devices, bit)
        stats = pl.pallas_call(
            merge_kernel,
            out_shape=shape_of(stats.shape),
            in_specs=[VMEM] * 2,
            out_specs=VMEM,
            name="merge",
        )(stats, theirs)

    half = GROUPS // 2
    piece = features // GROUPS
    heads_out = []
    other_grads = None
    for head_index in range(head_count):
        last = head_index + 1 == head_count
        column = pl.BlockSpec((row_count, HD), lambda _, at=head_index: (0, at))
        stack = pl.BlockSpec((reads, latents, HD), lambda _, at=head_index: (0, 0, at))
        whole = lambda shape: pl.BlockSpec(shape, lambda _, rank=len(shape): (0,) * rank)
        operands = [inputs, keys, values, queries, out_grad, stats]
        in_specs = [whole(inputs.shape), column, column, stack, stack, whole(stats.shape)]
        out_shape = [
            shape_of((row_count, 2 * HD), jnp.bfloat16),
            shape_of((half, reads, latents // GROUPS, HD)),
            shape_of((half, reads, latents // GROUPS, HD)),
            shape_of((half, piece, 2 * HD)),
            shape_of((half, piece, 2 * HD)),
        ]
        scratch = [
            pltpu.VMEM((row_count, HD), jnp.float32),
            pltpu.VMEM((row_count, HD), jnp.float32),
            pltpu.VMEM((tile, HD), jnp.float32),
            pltpu.VMEM((features, 2 * HD), jnp.float32),
        ]
        if last:
            operands += [key_weight, value_weight, other_grads]
            in_specs += [whole(key_weight.shape), whole(value_weight.shape), whole(other_grads.shape)]
            share = (head_devices // 2, row_count, features // head_devices)
            out_shape += [shape_of(share), shape_of(share)]
            scratch += [pltpu.VMEM((row_count, features), jnp.float32)]
        results = pl.pallas_call(
            functools.partial(head_kernel, head_index, "rows", "heads", low, last),
            grid=(1,),
            out_shape=out_shape,
            in_specs=in_specs,
            out_specs=[whole(item.shape) for item in out_shape],
            scratch_shapes=scratch,
            compiler_params=PARAMS,
            name="head",
        )(*operands)
        other_grads = results[0]
        heads_out.append(results[1:])

    input_keep, input_send = heads_out[-1][4:]
    order_low = (lax.axis_index("rows") % low) ^ jnp.arange(low, dtype=jnp.int32)
    low_bits = [bit for bit in bits_of(row_devices) if bit < low]

    def scatter_low(block, axis):
        if low == 1:
            return block
        parts = jnp.moveaxis(
            block.reshape(block.shape[:axis] + (low, -1) + block.shape[axis + 1 :]), axis, 0
        )
        parts = jnp.take(parts, order_low, axis=0)
        for bit in low_bits:
            parts = parts.reshape((-1, 2) + parts.shape[1:])
            parts = parts[:, 0] + swap(parts[:, 1], "rows", row_devices, bit)
        return parts[0]

    def gather_low(block):
        if low == 1:
            return block
        parts = block[None]
        for bit in reversed(low_bits):
            theirs = swap(parts, "rows", row_devices, bit)
            parts = jnp.stack([parts, theirs], axis=1).reshape((-1,) + parts.shape[1:])
        parts = jnp.take(parts, order_low, axis=0)
        return parts.reshape((low * block.shape[0],) + block.shape[1:])

    query_parts = []
    assembled = []
    for head_index in range(head_count):
        query_keep, query_send, weight_keep, weight_send = heads_out[head_index][:4]
        mine = reduce_bits(weight_keep, weight_send, row_devices, group_bits)
        block = gather_low(scatter_low(mine[0], 0))[None]
        for bit in reversed(group_bits[1:]):
            block = jnp.concatenate([block, swap(block, "rows", row_devices, bit)], axis=0)
        assembled += [block, swap(block, "rows", row_devices, group_bits[0])]
        mine = reduce_bits(query_keep, query_send, row_devices, group_bits)
        query_parts.append(scatter_low(mine[0], 1))
    query_grad = jnp.concatenate(query_parts, axis=2)

    key_weight_grad, value_weight_grad = pl.pallas_call(
        functools.partial(assemble_kernel, "rows", low),
        out_shape=(shape_of((features, columns)),) * 2,
        in_specs=[VMEM] * len(assembled),
        out_specs=(VMEM,) * 2,
        compiler_params=PARAMS,
        name="assemble",
    )(*assembled)

    total = input_keep + swap(input_send, "heads", head_devices, 1)
    for bit in bits_of(head_devices)[1:]:
        pairs = total.reshape((-1, 2) + total.shape[1:])
        total = pairs[:, 0] + swap(pairs[:, 1], "heads", head_devices, bit)
    return (query_grad, key_weight_grad, value_weight_grad, total[0])


def solution(mesh):
    in_specs = (
        P("rows", None),
        P(None, "heads"),
        P(None, "heads"),
        P(None, None, "heads"),
        P(None, None, "heads"),
    )
    out_specs = (P(None, "rows", "heads"), P(None, "heads"), P(None, "heads"), P("rows", "heads"))

    def body(*args):
        return on_device(mesh.shape["rows"], mesh.shape["heads"], *args)

    return jax.shard_map(body, mesh=mesh, in_specs=in_specs, out_specs=out_specs, check_vma=False)
```

```python
import functools

import jax
import jax.numpy as jnp
from jax import lax
from jax.experimental import pallas as pl
from jax.experimental.pallas import tpu as pltpu
from jax.sharding import PartitionSpec as P

HD = 128
GROUPS = 8
FACTOR = HD ** (-0.5)
LOG2_E = 1.4426950408889634
VMEM = pl.BlockSpec(memory_space=pltpu.VMEM)
HBM = pl.BlockSpec(memory_space=pltpu.HBM)
PARAMS = pltpu.CompilerParams(vmem_limit_bytes=24 * 1024 * 1024)


def last_contract(left, right):
    return lax.dot_general(
        left, right, (((1,), (1,)), ((), ())), preferred_element_type=jnp.float32
    )


def rows_contract(left, right):
    return lax.dot_general(
        left, right, (((0,), (0,)), ((), ())), preferred_element_type=jnp.float32
    )


def plain_dot(left, right):
    return jnp.dot(left, right, preferred_element_type=jnp.float32)


def swap(array, axis, count, bit):
    pairs = [(device, device ^ bit) for device in range(count)]
    return lax.ppermute(array, axis, pairs)


def bits_of(count):
    return [1 << place for place in range(count.bit_length() - 1)]


def project_kernel(
    tile, inputs_hbm, key_weight_hbm, value_weight_hbm, queries_hbm, out_grad_hbm,
    keys, values, stats, inputs, key_weight, value_weight, queries, out_grad, local, sems
):
    loads = [
        pltpu.make_async_copy(source, target, sems.at[index])
        for index, (source, target) in enumerate([
            (inputs_hbm, inputs),
            (key_weight_hbm, key_weight),
            (value_weight_hbm, value_weight),
            (queries_hbm, queries),
            (out_grad_hbm, out_grad),
        ])
    ]
    for load in loads:
        load.start()
    reads, latents, columns = queries.shape
    head_count = columns // HD
    for load in loads[:2]:
        load.wait()
    keys[...] = plain_dot(inputs[...], key_weight[...]).astype(jnp.bfloat16)
    loads[2].wait()
    values[...] = plain_dot(inputs[...], value_weight[...]).astype(jnp.bfloat16)
    for load in loads[3:]:
        load.wait()

    @pl.loop(0, latents // tile)
    def _(step):
        at = pl.ds(pl.multiple_of(step * tile, tile), tile)
        for read_index in range(reads):
            for head_index in range(head_count):
                cols = slice(head_index * HD, (head_index + 1) * HD)
                position = read_index * head_count + head_index
                scores = last_contract(keys[:, cols], queries[read_index, at, cols])
                scores = scores * (FACTOR * LOG2_E)
                weighted = last_contract(values[:, cols], out_grad[read_index, at, cols])
                top = jnp.max(scores, axis=0, keepdims=True)
                expos = jnp.exp2(scores - top)
                total = jnp.sum(expos, axis=0, keepdims=True)
                accum = jnp.sum(expos * weighted, axis=0, keepdims=True)
                local[position : position + 1, at] = top + jnp.log2(total)
                lower = reads * head_count + position
                local[lower : lower + 1, at] = accum / total

    for device in range(stats.shape[0]):
        stats[device] = local[...]


def merge(gathered):
    blocks = gathered.shape[1] // 2
    sums = gathered[:, :blocks]
    top = jnp.max(sums, axis=0)
    shares = jnp.exp2(sums - top)
    total = jnp.sum(shares, axis=0)
    return top + jnp.log2(total), jnp.sum(gathered[:, blocks:] * shares, axis=0) / total


def head_kernel(head_index, row_axis, head_axis, low, last, *refs):
    (inputs, keys, values, queries, out_grad, gathered) = refs[:6]
    if last:
        (key_weight, value_weight, other_grads) = refs[6:9]
        (grads, query_keep, query_send, weight_keep, weight_send, input_keep, input_send) = refs[9:16]
        key_acc, value_acc, tile_ref, weights_ref, stats, input_ref = refs[16:]
    else:
        (grads, query_keep, query_send, weight_keep, weight_send) = refs[6:11]
        key_acc, value_acc, tile_ref, weights_ref, stats = refs[11:]
    reads, latents, _ = queries.shape
    blocks = gathered.shape[1] // 2
    head_count = blocks // reads
    stats[:blocks], stats[blocks:] = merge(gathered)
    pairs = GROUPS // 2
    tile = latents // pairs
    half = tile // 2
    me = lax.axis_index(row_axis) // low
    side = lax.rem(me, 2)
    mine = pl.ds(pl.multiple_of(side * half, half), half)
    yours = pl.ds(pl.multiple_of((1 - side) * half, half), half)
    cols = slice(head_index * HD, (head_index + 1) * HD)
    key_acc[...] = jnp.zeros_like(key_acc)
    value_acc[...] = jnp.zeros_like(value_acc)

    @pl.loop(0, pairs)
    def _(slot):
        relative = (slot // (pairs // 2)) + 2 * lax.rem(slot, pairs // 2)
        pair = (me // 2) ^ relative
        at = pl.ds(pl.multiple_of(pair * tile, tile), tile)
        for read_index in range(reads):
            position = read_index * head_count + head_index
            lower = blocks + position
            query_block = queries[read_index, at, cols]
            grad_block = out_grad[read_index, at, cols]
            scores = last_contract(keys[:, cols], query_block) * (FACTOR * LOG2_E)
            weighted = last_contract(values[:, cols], grad_block)
            probs = jnp.exp2(scores - stats[position : position + 1, at])
            score_grad = (probs * (weighted - stats[lower : lower + 1, at]) * FACTOR).astype(
                jnp.bfloat16
            )
            key_acc[...] += plain_dot(score_grad, query_block)
            value_acc[...] += plain_dot(probs.astype(jnp.bfloat16), grad_block)
            tile_ref[read_index] = rows_contract(score_grad, keys[:, cols])
            query_keep[slot, read_index] = tile_ref[read_index, mine, :]
            query_send[slot, read_index] = tile_ref[read_index, yours, :]

    grads[:, :HD] = key_acc[...].astype(jnp.bfloat16)
    grads[:, HD:] = value_acc[...].astype(jnp.bfloat16)
    weights_ref[...] = rows_contract(inputs[...], grads[...])
    features = inputs.shape[1]
    piece = features // GROUPS
    for slot in range(pairs):
        relative = (slot // (pairs // 2)) + 2 * (slot % (pairs // 2))
        base = 2 * ((me // 2) ^ relative)
        weight_keep[slot] = weights_ref[pl.ds(pl.multiple_of((base + side) * piece, piece), piece), :]
        weight_send[slot] = weights_ref[
            pl.ds(pl.multiple_of((base + 1 - side) * piece, piece), piece), :
        ]
    if last:
        total = last_contract(grads[:, :HD], key_weight[:, HD:])
        total += last_contract(grads[:, HD:], value_weight[:, HD:])
        total += last_contract(other_grads[:, :HD], key_weight[:, :HD])
        total += last_contract(other_grads[:, HD:], value_weight[:, :HD])
        input_ref[...] = total
        place = lax.axis_index(head_axis)
        width = features // (2 * input_keep.shape[0])
        for relative in range(2 * input_keep.shape[0]):
            ref = input_send if relative % 2 else input_keep
            start = pl.multiple_of((place ^ relative) * width, width)
            ref[relative // 2] = input_ref[:, pl.ds(start, width)]


def assemble_kernel(row_axis, low, *refs):
    key_out, value_out = refs[-2:]
    piece = key_out.shape[0] // GROUPS
    me = lax.axis_index(row_axis) // low
    for head_index in range((len(refs) - 2) // 2):
        near, far = refs[2 * head_index : 2 * head_index + 2]
        cols = slice(head_index * HD, (head_index + 1) * HD)
        for slot in range(GROUPS // 2):
            relative = 2 * (slot // (GROUPS // 4) + 2 * (slot % (GROUPS // 4)))
            start = pl.multiple_of((me ^ relative) * piece, piece)
            key_out[pl.ds(start, piece), cols] = near[slot, :, :HD]
            value_out[pl.ds(start, piece), cols] = near[slot, :, HD:]
            start = pl.multiple_of((me ^ (relative + 1)) * piece, piece)
            key_out[pl.ds(start, piece), cols] = far[slot, :, :HD]
            value_out[pl.ds(start, piece), cols] = far[slot, :, HD:]


def shape_of(shape, dtype=jnp.float32):
    return jax.ShapeDtypeStruct(shape, dtype)


def reduce_bits(keep, send, count, bits):
    for index, bit in enumerate(bits):
        theirs = swap(send, "rows", count, bit)
        if index + 1 == len(bits):
            return keep + theirs
        middle = keep.shape[0] // 2
        send = keep[middle:] + theirs[middle:]
        keep = keep[:middle] + theirs[:middle]


def on_device(row_devices, head_devices, inputs, key_weight, value_weight, queries, out_grad):
    reads, latents, columns = queries.shape
    head_count = columns // HD
    row_count, features = inputs.shape
    blocks = reads * head_count
    low = row_devices // GROUPS
    group_bits = [bit * low for bit in bits_of(GROUPS)]
    tile = latents // (GROUPS // 2)

    operands = (inputs, key_weight, value_weight, queries, out_grad)
    keys, values, stats = pl.pallas_call(
        functools.partial(project_kernel, tile),
        out_shape=(
            shape_of((row_count, columns), jnp.bfloat16),
            shape_of((row_count, columns), jnp.bfloat16),
            shape_of((row_devices, 2 * blocks, latents)),
        ),
        in_specs=[HBM] * 5,
        out_specs=(VMEM,) * 3,
        scratch_shapes=[pltpu.VMEM(item.shape, item.dtype) for item in operands]
        + [
            pltpu.VMEM((2 * blocks, latents), jnp.float32),
            pltpu.SemaphoreType.DMA((5,)),
        ],
        compiler_params=pltpu.CompilerParams(vmem_limit_bytes=57 * 1024 * 1024),
        cost_estimate=pl.CostEstimate(
            flops=4 * row_count * columns * (features + reads * latents),
            bytes_accessed=8 * 2**20,
            transcendentals=blocks * row_count * latents,
        ),
        name="project",
    )(*operands)

    gathered = lax.all_to_all(stats, "rows", 0, 0, tiled=True)

    half = GROUPS // 2
    piece = features // GROUPS
    heads_out = []
    other_grads = None
    for head_index in range(head_count):
        last = head_index + 1 == head_count
        operands = [inputs, keys, values, queries, out_grad, gathered]
        out_shape = [
            shape_of((row_count, 2 * HD), jnp.bfloat16),
            shape_of((half, reads, latents // GROUPS, HD)),
            shape_of((half, reads, latents // GROUPS, HD)),
            shape_of((half, piece, 2 * HD)),
            shape_of((half, piece, 2 * HD)),
        ]
        scratch = [
            pltpu.VMEM((row_count, HD), jnp.float32),
            pltpu.VMEM((row_count, HD), jnp.float32),
            pltpu.VMEM((reads, tile, HD), jnp.float32),
            pltpu.VMEM((features, 2 * HD), jnp.float32),
            pltpu.VMEM((2 * blocks, latents), jnp.float32),
        ]
        if last:
            operands += [key_weight, value_weight, other_grads]
            share = (head_devices // 2, row_count, features // head_devices)
            out_shape += [shape_of(share), shape_of(share)]
            scratch += [pltpu.VMEM((row_count, features), jnp.float32)]
        results = pl.pallas_call(
            functools.partial(head_kernel, head_index, "rows", "heads", low, last),
            out_shape=out_shape,
            in_specs=[VMEM] * len(operands),
            out_specs=[VMEM] * len(out_shape),
            scratch_shapes=scratch,
            compiler_params=PARAMS,
            cost_estimate=pl.CostEstimate(
                flops=20 * reads * row_count * latents * HD,
                bytes_accessed=8 * 2**20,
                transcendentals=reads * row_count * latents,
            ),
            name="head",
        )(*operands)
        other_grads = results[0]
        heads_out.append(results[1:])

    input_keep, input_send = heads_out[-1][4:]
    order_low = (lax.axis_index("rows") % low) ^ jnp.arange(low, dtype=jnp.int32)
    low_bits = [bit for bit in bits_of(row_devices) if bit < low]

    def scatter_low(block, axis):
        if low == 1:
            return block
        parts = jnp.moveaxis(
            block.reshape(block.shape[:axis] + (low, -1) + block.shape[axis + 1 :]), axis, 0
        )
        parts = jnp.take(parts, order_low, axis=0)
        for bit in low_bits:
            parts = parts.reshape((-1, 2) + parts.shape[1:])
            parts = parts[:, 0] + swap(parts[:, 1], "rows", row_devices, bit)
        return parts[0]

    def gather_low(block):
        if low == 1:
            return block
        parts = block[None]
        for bit in reversed(low_bits):
            theirs = swap(parts, "rows", row_devices, bit)
            parts = jnp.stack([parts, theirs], axis=1).reshape((-1,) + parts.shape[1:])
        parts = jnp.take(parts, order_low, axis=0)
        return parts.reshape((low * block.shape[0],) + block.shape[1:])

    query_parts = []
    assembled = []
    for head_index in range(head_count):
        query_keep, query_send, weight_keep, weight_send = heads_out[head_index][:4]
        mine = reduce_bits(weight_keep, weight_send, row_devices, group_bits)
        block = gather_low(scatter_low(mine[0], 0))[None]
        for bit in reversed(group_bits[1:]):
            block = jnp.concatenate([block, swap(block, "rows", row_devices, bit)], axis=0)
        assembled += [block, swap(block, "rows", row_devices, group_bits[0])]
        mine = reduce_bits(query_keep, query_send, row_devices, group_bits)
        query_parts.append(scatter_low(mine[0], 1))
    query_grad = jnp.concatenate(query_parts, axis=2)

    key_weight_grad, value_weight_grad = pl.pallas_call(
        functools.partial(assemble_kernel, "rows", low),
        out_shape=(shape_of((features, columns)),) * 2,
        in_specs=[VMEM] * len(assembled),
        out_specs=(VMEM,) * 2,
        compiler_params=PARAMS,
        name="assemble",
    )(*assembled)

    total = input_keep + swap(input_send, "heads", head_devices, 1)
    for bit in bits_of(head_devices)[1:]:
        pairs = total.reshape((-1, 2) + total.shape[1:])
        total = pairs[:, 0] + swap(pairs[:, 1], "heads", head_devices, bit)
    return (query_grad, key_weight_grad, value_weight_grad, total[0])


def solution(mesh):
    in_specs = (
        P("rows", None),
        P(None, "heads"),
        P(None, "heads"),
        P(None, None, "heads"),
        P(None, None, "heads"),
    )
    out_specs = (P(None, "rows", "heads"), P(None, "heads"), P(None, "heads"), P("rows", "heads"))

    def body(*args):
        return on_device(mesh.shape["rows"], mesh.shape["heads"], *args)

    return jax.shard_map(body, mesh=mesh, in_specs=in_specs, out_specs=out_specs, check_vma=False)
```

```python
import functools

import jax
import jax.numpy as jnp
from jax import lax
from jax.experimental import pallas as pl
from jax.experimental.pallas import tpu as pltpu
from jax.sharding import PartitionSpec as P

HD = 128
GROUPS = 8
FACTOR = HD ** (-0.5)
LOG2_E = 1.4426950408889634
VMEM = pl.BlockSpec(memory_space=pltpu.VMEM)
HBM = pl.BlockSpec(memory_space=pltpu.HBM)


def params(mebibytes):
    return pltpu.CompilerParams(vmem_limit_bytes=mebibytes * 1024 * 1024)


def last_contract(left, right):
    return lax.dot_general(
        left, right, (((1,), (1,)), ((), ())), preferred_element_type=jnp.float32
    )


def rows_contract(left, right):
    return lax.dot_general(
        left, right, (((0,), (0,)), ((), ())), preferred_element_type=jnp.float32
    )


def plain_dot(left, right):
    return jnp.dot(left, right, preferred_element_type=jnp.float32)


def swap(array, axis, count, bit):
    pairs = [(device, device ^ bit) for device in range(count)]
    return lax.ppermute(array, axis, pairs)


def bits_of(count):
    return [1 << place for place in range(count.bit_length() - 1)]


def head_statistics(tile, cols, inputs, key_weight, value_weight, queries, out_grad, keys, values, stats):
    reads, latents, _ = queries.shape
    keys[...] = plain_dot(inputs[...], key_weight[:, cols]).astype(jnp.bfloat16)
    values[...] = plain_dot(inputs[...], value_weight[:, cols]).astype(jnp.bfloat16)

    @pl.loop(0, latents // tile)
    def _(step):
        at = pl.ds(pl.multiple_of(step * tile, tile), tile)
        for read_index in range(reads):
            scores = last_contract(keys[...], queries[read_index, at, cols])
            scores = scores * (FACTOR * LOG2_E)
            weighted = last_contract(values[...], out_grad[read_index, at, cols])
            top = jnp.max(scores, axis=0, keepdims=True)
            expos = jnp.exp2(scores - top)
            total = jnp.sum(expos, axis=0, keepdims=True)
            accum = jnp.sum(expos * weighted, axis=0, keepdims=True)
            stats[read_index : read_index + 1, at] = top + jnp.log2(total)
            stats[reads + read_index : reads + read_index + 1, at] = accum / total


def first_kernel(tile, *refs):
    sources, results, targets, sems = refs[:5], refs[5:8], refs[8:13], refs[13]
    loads = []
    for index, (source, target) in enumerate(zip(sources, targets)):
        if index:
            source = source.at[..., :HD]
        loads.append(pltpu.make_async_copy(source, target, sems.at[index]))
    for load in loads:
        load.start()
    for load in loads:
        load.wait()
    head_statistics(tile, slice(0, HD), *targets, *results)


def later_kernel(tile, head_index, *refs):
    head_statistics(tile, slice(head_index * HD, (head_index + 1) * HD), *refs)


def merged(mine, theirs):
    reads = mine.shape[0] // 2
    own, other = mine[:reads], theirs[:reads]
    top = jnp.maximum(own, other)
    own_share = jnp.exp2(own - top)
    other_share = jnp.exp2(other - top)
    total = own_share + other_share
    delta = (mine[reads:] * own_share + theirs[reads:] * other_share) / total
    return top + jnp.log2(total), delta


def merge_kernel(mine, theirs, result):
    reads = mine.shape[0] // 2
    result[:reads], result[reads:] = merged(mine, theirs)


def group_at(bits, relative, me):
    low = me % GROUPS
    group = 0
    for bit, flip in zip(bits, relative):
        group = group + ((low // bit) % 2 ^ flip) * bit
    return group


WEIGHT_BITS = (1, 2)
LAST_BIT = 4
QUERY_BITS = ((1, 2, 4), (2, 1, 4))


def grads_kernel(head_index, row_axis, head_axis, low, last, *refs):
    (inputs, keys, values, queries, out_grad, mine, theirs) = refs[:7]
    if last:
        (key_weight, value_weight, other_grads) = refs[7:10]
        refs = refs[10:]
        input_keep, input_send, input_ref = refs[4], refs[5], refs[-1]
    else:
        refs = refs[7:]
    grads, score_grads = refs[:2]
    weight_parts = refs[2:4]
    scratch = refs[6:] if last else refs[4:]
    key_acc, value_acc, weights_ref, stats = scratch[:4]
    reads, latents, _ = queries.shape
    tile = latents // (GROUPS // 2)
    cols = slice(head_index * HD, (head_index + 1) * HD)
    stats[:reads], stats[reads:] = merged(mine, theirs)
    key_acc[...] = jnp.zeros_like(key_acc)
    value_acc[...] = jnp.zeros_like(value_acc)

    @pl.loop(0, latents // tile)
    def _(step):
        at = pl.ds(pl.multiple_of(step * tile, tile), tile)
        for read_index in range(reads):
            query_block = queries[read_index, at, cols]
            grad_block = out_grad[read_index, at, cols]
            scores = last_contract(keys[...], query_block) * (FACTOR * LOG2_E)
            weighted = last_contract(values[...], grad_block)
            probs = jnp.exp2(scores - stats[read_index : read_index + 1, at])
            delta = stats[reads + read_index : reads + read_index + 1, at]
            score_grad = (probs * (weighted - delta) * FACTOR).astype(jnp.bfloat16)
            score_grads[read_index, :, at] = score_grad
            key_acc[...] += plain_dot(score_grad, query_block)
            value_acc[...] += plain_dot(probs.astype(jnp.bfloat16), grad_block)

    grads[:, :HD] = key_acc[...].astype(jnp.bfloat16)
    grads[:, HD:] = value_acc[...].astype(jnp.bfloat16)
    weights_ref[...] = rows_contract(inputs[...], grads[...])
    features = inputs.shape[1]
    piece = features // GROUPS
    me = lax.axis_index(row_axis) // low
    for first in range(2):
        for second in range(2):
            base = group_at(WEIGHT_BITS, (first, second), me)
            for high in range(2):
                start = pl.multiple_of((base + LAST_BIT * high) * piece, piece)
                weight_parts[first][second, high] = weights_ref[pl.ds(start, piece), :]
    if last:
        total = last_contract(grads[:, :HD], key_weight[:, HD:])
        total += last_contract(grads[:, HD:], value_weight[:, HD:])
        total += last_contract(other_grads[:, :HD], key_weight[:, :HD])
        total += last_contract(other_grads[:, HD:], value_weight[:, :HD])
        input_ref[...] = total
        place = lax.axis_index(head_axis)
        width = features // (2 * input_keep.shape[0])
        for relative in range(2 * input_keep.shape[0]):
            ref = input_send if relative % 2 else input_keep
            start = pl.multiple_of((place ^ relative) * width, width)
            ref[relative // 2] = input_ref[:, pl.ds(start, width)]


def query_kernel(bits, row_axis, low, score_grads, keys, query_keep, query_send, tile_ref):
    reads, _, latents = score_grads.shape
    piece = latents // GROUPS
    me = lax.axis_index(row_axis) // low
    side = lax.rem(me, 2)
    for upper in range(GROUPS // 2):
        pair = (me // 2) ^ upper
        at = pl.ds(pl.multiple_of(pair * 2 * piece, 2 * piece), 2 * piece)
        for read_index in range(reads):
            slot = upper * reads + read_index
            tile_ref[slot] = rows_contract(score_grads[read_index, :, at], keys[...])
            for flip in range(2):
                half = pl.ds(pl.multiple_of((side ^ flip) * piece, piece), piece)
                relative = 2 * upper + flip
                ref = query_send if relative & bits[0] else query_keep
                index = 2 * ((relative & bits[1]) // bits[1]) + (relative & bits[2]) // bits[2]
                ref[index, read_index] = tile_ref[slot, half, :]


def assemble_kernel(row_axis, low, *refs):
    key_out, value_out = refs[-2:]
    piece = key_out.shape[0] // GROUPS
    me = lax.axis_index(row_axis) // low
    for head_index in range(len(refs) // 2 - 1):
        cols = slice(head_index * HD, (head_index + 1) * HD)
        for first in range(2):
            source = refs[2 * head_index + first]
            for second in range(2):
                base = group_at(WEIGHT_BITS, (first, second), me)
                for high in range(2):
                    start = pl.multiple_of((base + LAST_BIT * high) * piece, piece)
                    key_out[pl.ds(start, piece), cols] = source[second, high, :, :HD]
                    value_out[pl.ds(start, piece), cols] = source[second, high, :, HD:]


def shape_of(shape, dtype=jnp.float32):
    return jax.ShapeDtypeStruct(shape, dtype)


def scatter_steps(keep, send, count, bits):
    for index, bit in enumerate(bits):
        theirs = swap(send, "rows", count, bit)
        if index + 1 == len(bits):
            return keep + theirs
        middle = keep.shape[0] // 2
        send = keep[middle:] + theirs[middle:]
        keep = keep[:middle] + theirs[:middle]


def on_device(row_devices, head_devices, inputs, key_weight, value_weight, queries, out_grad):
    reads, latents, columns = queries.shape
    head_count = columns // HD
    row_count, features = inputs.shape
    low = row_devices // GROUPS
    tile = latents // (GROUPS // 2)
    piece = features // GROUPS
    operands = (inputs, key_weight, value_weight, queries, out_grad)
    block_work = pl.CostEstimate(
        flops=8 * reads * row_count * latents * HD,
        bytes_accessed=4 * 2**20,
        transcendentals=reads * row_count * latents,
    )

    projected = []
    for head_index in range(head_count):
        first = head_index == 0
        loaded = [
            pltpu.VMEM(item.shape[:-1] + ((HD,) if place else item.shape[-1:]), item.dtype)
            for place, item in enumerate(operands)
        ]
        projected.append(
            pl.pallas_call(
                functools.partial(first_kernel, tile)
                if first
                else functools.partial(later_kernel, tile, head_index),
                out_shape=(
                    shape_of((row_count, HD), jnp.bfloat16),
                    shape_of((row_count, HD), jnp.bfloat16),
                    shape_of((2 * reads, latents)),
                ),
                in_specs=[HBM if first else VMEM] * 5,
                out_specs=(VMEM,) * 3,
                scratch_shapes=loaded + [pltpu.SemaphoreType.DMA((5,))] if first else [],
                compiler_params=params(57 if first else 16),
                cost_estimate=block_work,
                name="project",
            )(*operands)
        )

    stats_parts = []
    for head_index in range(head_count):
        stats = projected[head_index][2]
        for bit in bits_of(row_devices)[:-1]:
            theirs = swap(stats, "rows", row_devices, bit)
            stats = pl.pallas_call(
                merge_kernel,
                out_shape=shape_of(stats.shape),
                in_specs=[VMEM] * 2,
                out_specs=VMEM,
                compiler_params=params(2),
                name="merge",
            )(stats, theirs)
        stats_parts.append((stats, swap(stats, "rows", row_devices, bits_of(row_devices)[-1])))

    grads_out = []
    for head_index in range(head_count):
        last = head_index + 1 == head_count
        keys, values, _ = projected[head_index]
        operands = [inputs, keys, values, queries, out_grad, *stats_parts[head_index]]
        out_shape = [
            shape_of((row_count, 2 * HD), jnp.bfloat16),
            shape_of((reads, row_count, latents), jnp.bfloat16),
        ] + [shape_of((2, 2, piece, 2 * HD))] * 2
        scratch = [
            pltpu.VMEM((row_count, HD), jnp.float32),
            pltpu.VMEM((row_count, HD), jnp.float32),
            pltpu.VMEM((features, 2 * HD), jnp.float32),
            pltpu.VMEM((2 * reads, latents), jnp.float32),
        ]
        if last:
            operands += [key_weight, value_weight, grads_out[0][0]]
            share = (head_devices // 2, row_count, features // head_devices)
            out_shape += [shape_of(share), shape_of(share)]
            scratch += [pltpu.VMEM((row_count, features), jnp.float32)]
        grads_out.append(
            pl.pallas_call(
                functools.partial(grads_kernel, head_index, "rows", "heads", low, last),
                out_shape=out_shape,
                in_specs=[VMEM] * len(operands),
                out_specs=[VMEM] * len(out_shape),
                scratch_shapes=scratch,
                compiler_params=params(20),
                cost_estimate=block_work,
                name="grads",
            )(*operands)
        )

    query_out = []
    for head_index in range(head_count):
        share = (GROUPS // 2, reads, latents // GROUPS, HD)
        query_out.append(
            pl.pallas_call(
                functools.partial(query_kernel, QUERY_BITS[head_index % 2], "rows", low),
                out_shape=(shape_of(share), shape_of(share)),
                in_specs=[VMEM] * 2,
                out_specs=(VMEM,) * 2,
                scratch_shapes=[pltpu.VMEM((GROUPS // 2 * reads, tile, HD), jnp.float32)],
                compiler_params=params(16),
                cost_estimate=block_work,
                name="query",
            )(grads_out[head_index][1], projected[head_index][0])
        )

    order_low = (lax.axis_index("rows") % low) ^ jnp.arange(low, dtype=jnp.int32)
    low_bits = [bit for bit in bits_of(row_devices) if bit < low]

    def scatter_low(block, axis):
        if low == 1:
            return block
        parts = jnp.moveaxis(
            block.reshape(block.shape[:axis] + (low, -1) + block.shape[axis + 1 :]), axis, 0
        )
        parts = jnp.take(parts, order_low, axis=0)
        for bit in low_bits:
            parts = parts.reshape((-1, 2) + parts.shape[1:])
            parts = parts[:, 0] + swap(parts[:, 1], "rows", row_devices, bit)
        return parts[0]

    def sum_low(block):
        for bit in low_bits:
            block = block + swap(block, "rows", row_devices, bit)
        return block

    query_parts = []
    assembled = []
    for head_index in range(head_count):
        keep, send = grads_out[head_index][2:4]
        mine = scatter_steps(keep, send, row_devices, [bit * low for bit in WEIGHT_BITS])
        mine = mine + swap(mine, "rows", row_devices, LAST_BIT * low)
        mine = sum_low(mine)
        near = jnp.concatenate([mine, swap(mine, "rows", row_devices, WEIGHT_BITS[1] * low)], axis=0)
        assembled += [near, swap(near, "rows", row_devices, WEIGHT_BITS[0] * low)]
        keep, send = query_out[head_index]
        bits = [bit * low for bit in QUERY_BITS[head_index % 2]]
        mine = scatter_steps(keep, send, row_devices, bits)
        query_parts.append(scatter_low(mine[0], 1))
    query_grad = jnp.concatenate(query_parts, axis=2)

    key_weight_grad, value_weight_grad = pl.pallas_call(
        functools.partial(assemble_kernel, "rows", low),
        out_shape=(shape_of((features, columns)),) * 2,
        in_specs=[VMEM] * len(assembled),
        out_specs=(VMEM,) * 2,
        compiler_params=params(8),
        name="assemble",
    )(*assembled)

    input_keep, input_send = grads_out[-1][4:]
    total = input_keep + swap(input_send, "heads", head_devices, 1)
    for bit in bits_of(head_devices)[1:]:
        pairs = total.reshape((-1, 2) + total.shape[1:])
        total = pairs[:, 0] + swap(pairs[:, 1], "heads", head_devices, bit)
    return (query_grad, key_weight_grad, value_weight_grad, total[0])


def solution(mesh):
    in_specs = (
        P("rows", None),
        P(None, "heads"),
        P(None, "heads"),
        P(None, None, "heads"),
        P(None, None, "heads"),
    )
    out_specs = (P(None, "rows", "heads"), P(None, "heads"), P(None, "heads"), P("rows", "heads"))

    def body(*args):
        return on_device(mesh.shape["rows"], mesh.shape["heads"], *args)

    return jax.shard_map(body, mesh=mesh, in_specs=in_specs, out_specs=out_specs, check_vma=False)
```

```python
import functools

import jax
import jax.numpy as jnp
from jax import lax
from jax.experimental import pallas as pl
from jax.experimental.pallas import tpu as pltpu
from jax.sharding import PartitionSpec as P

HD = 128
GROUPS = 8
FACTOR = HD ** (-0.5)
LOG2_E = 1.4426950408889634
VMEM = pl.BlockSpec(memory_space=pltpu.VMEM)
HBM = pl.BlockSpec(memory_space=pltpu.HBM)


def params(mebibytes):
    return pltpu.CompilerParams(vmem_limit_bytes=mebibytes * 1024 * 1024)


def last_contract(left, right):
    return lax.dot_general(
        left, right, (((1,), (1,)), ((), ())), preferred_element_type=jnp.float32
    )


def rows_contract(left, right):
    return lax.dot_general(
        left, right, (((0,), (0,)), ((), ())), preferred_element_type=jnp.float32
    )


def plain_dot(left, right):
    return jnp.dot(left, right, preferred_element_type=jnp.float32)


def swap(array, axis, count, bit):
    pairs = [(device, device ^ bit) for device in range(count)]
    return lax.ppermute(array, axis, pairs)


def bits_of(count):
    return [1 << place for place in range(count.bit_length() - 1)]


def head_statistics(tile, cols, inputs, key_weight, value_weight, queries, out_grad, keys, values, stats):
    reads, latents, _ = queries.shape
    keys[...] = plain_dot(inputs[...], key_weight[:, cols]).astype(jnp.bfloat16)
    values[...] = plain_dot(inputs[...], value_weight[:, cols]).astype(jnp.bfloat16)

    @pl.loop(0, latents // tile, unroll=True)
    def _(step):
        at = pl.ds(pl.multiple_of(step * tile, tile), tile)
        for read_index in range(reads):
            scores = last_contract(keys[...], queries[read_index, at, cols])
            scores = scores * (FACTOR * LOG2_E)
            weighted = last_contract(values[...], out_grad[read_index, at, cols])
            top = jnp.max(scores, axis=0, keepdims=True)
            expos = jnp.exp2(scores - top)
            total = jnp.sum(expos, axis=0, keepdims=True)
            accum = jnp.sum(expos * weighted, axis=0, keepdims=True)
            stats[read_index : read_index + 1, at] = top + jnp.log2(total)
            stats[reads + read_index : reads + read_index + 1, at] = accum / total


def first_kernel(tile, *refs):
    sources, results, targets, sems = refs[:5], refs[5:8], refs[8:13], refs[13]
    loads = []
    for index, (source, target) in enumerate(zip(sources, targets)):
        if index:
            source = source.at[..., :HD]
        loads.append(pltpu.make_async_copy(source, target, sems.at[index]))
    for load in loads:
        load.start()
    for load in loads:
        load.wait()
    head_statistics(tile, slice(0, HD), *targets, *results)


def later_kernel(tile, head_index, *refs):
    head_statistics(tile, slice(head_index * HD, (head_index + 1) * HD), *refs)


def merged(mine, theirs):
    reads = mine.shape[0] // 2
    own, other = mine[:reads], theirs[:reads]
    top = jnp.maximum(own, other)
    own_share = jnp.exp2(own - top)
    other_share = jnp.exp2(other - top)
    total = own_share + other_share
    delta = (mine[reads:] * own_share + theirs[reads:] * other_share) / total
    return top + jnp.log2(total), delta


def merge_kernel(mine, theirs, result):
    reads = mine.shape[0] // 2
    result[:reads], result[reads:] = merged(mine, theirs)


def group_at(bits, relative, me):
    low = me % GROUPS
    group = 0
    for bit, flip in zip(bits, relative):
        group = group + ((low // bit) % 2 ^ flip) * bit
    return group


WEIGHT_BITS = (1, 2)
LAST_BIT = 4
QUERY_BITS = ((2, 1, 4), (1, 2, 4))


def grads_kernel(head_index, row_axis, head_axis, low, last, *refs):
    (inputs, keys, values, queries, out_grad, mine, theirs) = refs[:7]
    if last:
        (key_weight, value_weight, other_grads) = refs[7:10]
        refs = refs[10:]
        input_keep, input_send, input_ref = refs[4], refs[5], refs[-1]
    else:
        refs = refs[7:]
    grads, score_grads = refs[:2]
    weight_parts = refs[2:4]
    scratch = refs[6:] if last else refs[4:]
    key_acc, value_acc, weights_ref, stats = scratch[:4]
    reads, latents, _ = queries.shape
    tile = latents // (GROUPS // 2)
    cols = slice(head_index * HD, (head_index + 1) * HD)
    stats[:reads], stats[reads:] = merged(mine, theirs)
    key_acc[...] = jnp.zeros_like(key_acc)
    value_acc[...] = jnp.zeros_like(value_acc)

    @pl.loop(0, latents // tile, unroll=True)
    def _(step):
        at = pl.ds(pl.multiple_of(step * tile, tile), tile)
        for read_index in range(reads):
            query_block = queries[read_index, at, cols]
            grad_block = out_grad[read_index, at, cols]
            scores = last_contract(keys[...], query_block) * (FACTOR * LOG2_E)
            weighted = last_contract(values[...], grad_block)
            probs = jnp.exp2(scores - stats[read_index : read_index + 1, at])
            delta = stats[reads + read_index : reads + read_index + 1, at]
            score_grad = (probs * (weighted - delta) * FACTOR).astype(jnp.bfloat16)
            score_grads[read_index, :, at] = score_grad
            key_acc[...] += plain_dot(score_grad, query_block)
            value_acc[...] += plain_dot(probs.astype(jnp.bfloat16), grad_block)

    grads[:, :HD] = key_acc[...].astype(jnp.bfloat16)
    grads[:, HD:] = value_acc[...].astype(jnp.bfloat16)
    weights_ref[...] = rows_contract(inputs[...], grads[...])
    features = inputs.shape[1]
    piece = features // GROUPS
    me = lax.axis_index(row_axis) // low
    for first in range(2):
        for second in range(2):
            base = group_at(WEIGHT_BITS, (first, second), me)
            for high in range(2):
                start = pl.multiple_of((base + LAST_BIT * high) * piece, piece)
                weight_parts[first][second, high] = weights_ref[pl.ds(start, piece), :]
    if last:
        total = last_contract(grads[:, :HD], key_weight[:, HD:])
        total += last_contract(grads[:, HD:], value_weight[:, HD:])
        total += last_contract(other_grads[:, :HD], key_weight[:, :HD])
        total += last_contract(other_grads[:, HD:], value_weight[:, :HD])
        input_ref[...] = total
        place = lax.axis_index(head_axis)
        width = features // (2 * input_keep.shape[0])
        for relative in range(2 * input_keep.shape[0]):
            ref = input_send if relative % 2 else input_keep
            start = pl.multiple_of((place ^ relative) * width, width)
            ref[relative // 2] = input_ref[:, pl.ds(start, width)]


def query_kernel(bits, row_axis, low, score_grads, keys, query_keep, query_send, tile_ref):
    reads, _, latents = score_grads.shape
    piece = latents // GROUPS
    me = lax.axis_index(row_axis) // low
    side = lax.rem(me, 2)
    for upper in range(GROUPS // 2):
        pair = (me // 2) ^ upper
        at = pl.ds(pl.multiple_of(pair * 2 * piece, 2 * piece), 2 * piece)
        for read_index in range(reads):
            slot = upper * reads + read_index
            tile_ref[slot] = rows_contract(score_grads[read_index, :, at], keys[...])
            for flip in range(2):
                half = pl.ds(pl.multiple_of((side ^ flip) * piece, piece), piece)
                relative = 2 * upper + flip
                ref = query_send if relative & bits[0] else query_keep
                index = 2 * ((relative & bits[1]) // bits[1]) + (relative & bits[2]) // bits[2]
                ref[index, read_index] = tile_ref[slot, half, :]


def assemble_kernel(head_count, row_axis, low, *refs):
    query_out, key_out, value_out = refs[-3:]
    query_parts = refs[2 * head_count : -3]
    terms = len(query_parts) // head_count
    piece = key_out.shape[0] // GROUPS
    me = lax.axis_index(row_axis) // low
    for head_index in range(head_count):
        cols = slice(head_index * HD, (head_index + 1) * HD)
        parts = query_parts[head_index * terms : (head_index + 1) * terms]
        query_out[:, :, cols] = sum(part[0] for part in parts[1:]) + parts[0][0]
        for first in range(2):
            source = refs[2 * head_index + first]
            for second in range(2):
                base = group_at(WEIGHT_BITS, (first, second), me)
                for high in range(2):
                    start = pl.multiple_of((base + LAST_BIT * high) * piece, piece)
                    key_out[pl.ds(start, piece), cols] = source[second, high, :, :HD]
                    value_out[pl.ds(start, piece), cols] = source[second, high, :, HD:]


def shape_of(shape, dtype=jnp.float32):
    return jax.ShapeDtypeStruct(shape, dtype)


def scatter_steps(keep, send, count, bits):
    for index, bit in enumerate(bits):
        theirs = swap(send, "rows", count, bit)
        if index + 1 == len(bits):
            return keep, theirs
        middle = keep.shape[0] // 2
        send = keep[middle:] + theirs[middle:]
        keep = keep[:middle] + theirs[:middle]


def on_device(row_devices, head_devices, inputs, key_weight, value_weight, queries, out_grad):
    reads, latents, columns = queries.shape
    head_count = columns // HD
    row_count, features = inputs.shape
    low = row_devices // GROUPS
    tile = latents // (GROUPS // 2)
    piece = features // GROUPS
    operands = (inputs, key_weight, value_weight, queries, out_grad)
    block_work = pl.CostEstimate(
        flops=8 * reads * row_count * latents * HD,
        bytes_accessed=4 * 2**20,
        transcendentals=reads * row_count * latents,
    )

    projected = []
    for head_index in range(head_count):
        first = head_index == 0
        loaded = [
            pltpu.VMEM(item.shape[:-1] + ((HD,) if place else item.shape[-1:]), item.dtype)
            for place, item in enumerate(operands)
        ]
        projected.append(
            pl.pallas_call(
                functools.partial(first_kernel, tile)
                if first
                else functools.partial(later_kernel, tile, head_index),
                out_shape=(
                    shape_of((row_count, HD), jnp.bfloat16),
                    shape_of((row_count, HD), jnp.bfloat16),
                    shape_of((2 * reads, latents)),
                ),
                in_specs=[HBM if first else VMEM] * 5,
                out_specs=(VMEM,) * 3,
                scratch_shapes=loaded + [pltpu.SemaphoreType.DMA((5,))] if first else [],
                compiler_params=params(57 if first else 16),
                cost_estimate=block_work,
                name="project",
            )(*operands)
        )

    stats_parts = []
    for head_index in range(head_count):
        stats = projected[head_index][2]
        for bit in bits_of(row_devices)[:-1]:
            theirs = swap(stats, "rows", row_devices, bit)
            stats = pl.pallas_call(
                merge_kernel,
                out_shape=shape_of(stats.shape),
                in_specs=[VMEM] * 2,
                out_specs=VMEM,
                compiler_params=params(2),
                name="merge",
            )(stats, theirs)
        stats_parts.append((stats, swap(stats, "rows", row_devices, bits_of(row_devices)[-1])))

    grads_out = []
    for head_index in range(head_count):
        last = head_index + 1 == head_count
        keys, values, _ = projected[head_index]
        operands = [inputs, keys, values, queries, out_grad, *stats_parts[head_index]]
        out_shape = [
            shape_of((row_count, 2 * HD), jnp.bfloat16),
            shape_of((reads, row_count, latents), jnp.bfloat16),
        ] + [shape_of((2, 2, piece, 2 * HD))] * 2
        scratch = [
            pltpu.VMEM((row_count, HD), jnp.float32),
            pltpu.VMEM((row_count, HD), jnp.float32),
            pltpu.VMEM((features, 2 * HD), jnp.float32),
            pltpu.VMEM((2 * reads, latents), jnp.float32),
        ]
        if last:
            operands += [key_weight, value_weight, grads_out[0][0]]
            share = (head_devices // 2, row_count, features // head_devices)
            out_shape += [shape_of(share), shape_of(share)]
            scratch += [pltpu.VMEM((row_count, features), jnp.float32)]
        grads_out.append(
            pl.pallas_call(
                functools.partial(grads_kernel, head_index, "rows", "heads", low, last),
                out_shape=out_shape,
                in_specs=[VMEM] * len(operands),
                out_specs=[VMEM] * len(out_shape),
                scratch_shapes=scratch,
                compiler_params=params(20),
                cost_estimate=block_work,
                name="grads",
            )(*operands)
        )

    query_out = []
    for head_index in range(head_count):
        share = (GROUPS // 2, reads, latents // GROUPS, HD)
        query_out.append(
            pl.pallas_call(
                functools.partial(query_kernel, QUERY_BITS[head_index % 2], "rows", low),
                out_shape=(shape_of(share), shape_of(share)),
                in_specs=[VMEM] * 2,
                out_specs=(VMEM,) * 2,
                scratch_shapes=[pltpu.VMEM((GROUPS // 2 * reads, tile, HD), jnp.float32)],
                compiler_params=params(16),
                cost_estimate=block_work,
                name="query",
            )(grads_out[head_index][1], projected[head_index][0])
        )

    order_low = (lax.axis_index("rows") % low) ^ jnp.arange(low, dtype=jnp.int32)
    low_bits = [bit for bit in bits_of(row_devices) if bit < low]

    def scatter_low(block, axis):
        if low == 1:
            return block
        parts = jnp.moveaxis(
            block.reshape(block.shape[:axis] + (low, -1) + block.shape[axis + 1 :]), axis, 0
        )
        parts = jnp.take(parts, order_low, axis=0)
        for bit in low_bits:
            parts = parts.reshape((-1, 2) + parts.shape[1:])
            parts = parts[:, 0] + swap(parts[:, 1], "rows", row_devices, bit)
        return parts[0]

    def sum_low(block):
        for bit in low_bits:
            block = block + swap(block, "rows", row_devices, bit)
        return block

    query_parts = []
    assembled = []
    for head_index in range(head_count):
        keep, send = grads_out[head_index][2:4]
        mine, theirs = scatter_steps(keep, send, row_devices, [bit * low for bit in WEIGHT_BITS])
        mine = mine + theirs
        mine = mine + swap(mine, "rows", row_devices, LAST_BIT * low)
        mine = sum_low(mine)
        near = jnp.concatenate([mine, swap(mine, "rows", row_devices, WEIGHT_BITS[1] * low)], axis=0)
        assembled += [near, swap(near, "rows", row_devices, WEIGHT_BITS[0] * low)]
        keep, send = query_out[head_index]
        bits = [bit * low for bit in QUERY_BITS[head_index % 2]]
        mine, theirs = scatter_steps(keep, send, row_devices, bits)
        if low == 1:
            query_parts += [mine, theirs]
        else:
            query_parts.append(scatter_low((mine + theirs)[0], 1)[None])

    query_grad, key_weight_grad, value_weight_grad = pl.pallas_call(
        functools.partial(assemble_kernel, head_count, "rows", low),
        out_shape=(shape_of((reads, latents // row_devices, columns)),)
        + (shape_of((features, columns)),) * 2,
        in_specs=[VMEM] * (len(assembled) + len(query_parts)),
        out_specs=(VMEM,) * 3,
        compiler_params=params(8),
        name="assemble",
    )(*assembled, *query_parts)

    input_keep, input_send = grads_out[-1][4:]
    total = input_keep + swap(input_send, "heads", head_devices, 1)
    for bit in bits_of(head_devices)[1:]:
        pairs = total.reshape((-1, 2) + total.shape[1:])
        total = pairs[:, 0] + swap(pairs[:, 1], "heads", head_devices, bit)
    return (query_grad, key_weight_grad, value_weight_grad, total[0])


def solution(mesh):
    in_specs = (
        P("rows", None),
        P(None, "heads"),
        P(None, "heads"),
        P(None, None, "heads"),
        P(None, None, "heads"),
    )
    out_specs = (P(None, "rows", "heads"), P(None, "heads"), P(None, "heads"), P("rows", "heads"))

    def body(*args):
        return on_device(mesh.shape["rows"], mesh.shape["heads"], *args)

    return jax.shard_map(body, mesh=mesh, in_specs=in_specs, out_specs=out_specs, check_vma=False)
```

```python
import functools

import jax
import jax.numpy as jnp
from jax import lax
from jax.experimental import pallas as pl
from jax.experimental.pallas import tpu as pltpu
from jax.sharding import PartitionSpec as P

HD = 128
GROUPS = 8
FACTOR = HD ** (-0.5)
LOG2_E = 1.4426950408889634
VMEM = pl.BlockSpec(memory_space=pltpu.VMEM)
HBM = pl.BlockSpec(memory_space=pltpu.HBM)
ANY = pl.BlockSpec(memory_space=pl.ANY)


def params(mebibytes):
    return pltpu.CompilerParams(vmem_limit_bytes=mebibytes * 1024 * 1024)


def last_contract(left, right):
    return lax.dot_general(
        left, right, (((1,), (1,)), ((), ())), preferred_element_type=jnp.float32
    )


def rows_contract(left, right):
    return lax.dot_general(
        left, right, (((0,), (0,)), ((), ())), preferred_element_type=jnp.float32
    )


def plain_dot(left, right):
    return jnp.dot(left, right, preferred_element_type=jnp.float32)


def swap(array, axis, count, bit):
    pairs = [(device, device ^ bit) for device in range(count)]
    return lax.ppermute(array, axis, pairs)


def bits_of(count):
    return [1 << place for place in range(count.bit_length() - 1)]


def head_statistics(tile, cols, inputs, key_weight, value_weight, queries, out_grad, keys, values, stats):
    reads, latents, _ = queries.shape
    keys[...] = plain_dot(inputs[...], key_weight[:, cols]).astype(jnp.bfloat16)
    values[...] = plain_dot(inputs[...], value_weight[:, cols]).astype(jnp.bfloat16)

    @pl.loop(0, latents // tile, unroll=True)
    def _(step):
        at = pl.ds(pl.multiple_of(step * tile, tile), tile)
        for read_index in range(reads):
            scores = last_contract(keys[...], queries[read_index, at, cols])
            scores = scores * (FACTOR * LOG2_E)
            weighted = last_contract(values[...], out_grad[read_index, at, cols])
            top = jnp.max(scores, axis=0, keepdims=True)
            expos = jnp.exp2(scores - top)
            total = jnp.sum(expos, axis=0, keepdims=True)
            accum = jnp.sum(expos * weighted, axis=0, keepdims=True)
            stats[read_index : read_index + 1, at] = top + jnp.log2(total)
            stats[reads + read_index : reads + read_index + 1, at] = accum / total


def first_kernel(tile, *refs):
    sources, results, targets, sems = refs[:5], refs[5:8], refs[8:13], refs[13]
    loads = []
    for index, (source, target) in enumerate(zip(sources, targets)):
        if index:
            source = source.at[..., :HD]
        loads.append(pltpu.make_async_copy(source, target, sems.at[index]))
    for load in loads:
        load.start()
    for load in loads:
        load.wait()
    head_statistics(tile, slice(0, HD), *targets, *results)


def later_kernel(tile, head_index, after, *refs):
    del after
    head_statistics(tile, slice(head_index * HD, (head_index + 1) * HD), *refs)


def merged(mine, theirs):
    reads = mine.shape[0] // 2
    own, other = mine[:reads], theirs[:reads]
    top = jnp.maximum(own, other)
    own_share = jnp.exp2(own - top)
    other_share = jnp.exp2(other - top)
    total = own_share + other_share
    delta = (mine[reads:] * own_share + theirs[reads:] * other_share) / total
    return top + jnp.log2(total), delta


def merge_kernel(mine, theirs, result):
    reads = mine.shape[0] // 2
    result[:reads], result[reads:] = merged(mine, theirs)


def group_at(bits, relative, me):
    low = me % GROUPS
    group = 0
    for bit, flip in zip(bits, relative):
        group = group + ((low // bit) % 2 ^ flip) * bit
    return group


LAST_BIT = 4
WEIGHT_PARTS = (((0, 256, (1, 2)),), ((0, 256, (1, 2)),))
QUERY_PARTS = (((0, 2, (2, 1, 4)),), ((0, 2, (1, 2, 4)),))


def grads_kernel(
    head_index, row_axis, low, after, inputs, keys, values, queries, out_grad, mine, theirs, *refs
):
    del after
    grads, score_grads = refs[:2]
    weight_parts = refs[2:-4]
    key_acc, value_acc, weights_ref, stats = refs[-4:]
    reads, latents, _ = queries.shape
    tile = latents // (GROUPS // 2)
    cols = slice(head_index * HD, (head_index + 1) * HD)
    stats[:reads], stats[reads:] = merged(mine, theirs)
    key_acc[...] = jnp.zeros_like(key_acc)
    value_acc[...] = jnp.zeros_like(value_acc)

    @pl.loop(0, latents // tile, unroll=True)
    def _(step):
        at = pl.ds(pl.multiple_of(step * tile, tile), tile)
        for read_index in range(reads):
            query_block = queries[read_index, at, cols]
            grad_block = out_grad[read_index, at, cols]
            scores = last_contract(keys[...], query_block) * (FACTOR * LOG2_E)
            weighted = last_contract(values[...], grad_block)
            probs = jnp.exp2(scores - stats[read_index : read_index + 1, at])
            delta = stats[reads + read_index : reads + read_index + 1, at]
            score_grad = (probs * (weighted - delta) * FACTOR).astype(jnp.bfloat16)
            score_grads[read_index, :, at] = score_grad
            key_acc[...] += plain_dot(score_grad, query_block)
            value_acc[...] += plain_dot(probs.astype(jnp.bfloat16), grad_block)

    grads[:, :HD] = key_acc[...].astype(jnp.bfloat16)
    grads[:, HD:] = value_acc[...].astype(jnp.bfloat16)
    weights_ref[...] = rows_contract(inputs[...], grads[...])
    features = inputs.shape[1]
    piece = features // GROUPS
    me = lax.axis_index(row_axis) // low
    for part, (begin, end, bits) in enumerate(WEIGHT_PARTS[head_index]):
        for first in range(2):
            ref = weight_parts[2 * part + first]
            for second in range(2):
                base = group_at(bits, (first, second), me)
                for high in range(2):
                    start = pl.multiple_of((base + LAST_BIT * high) * piece, piece)
                    ref[second, high] = weights_ref[pl.ds(start, piece), begin:end]


def input_kernel(head_axis, key_weight, value_weight, *refs):
    head_grads, (_, input_keep, input_send, total) = refs[:-4], refs[-4:]
    for head_index, grads in enumerate(head_grads):
        cols = slice(head_index * HD, (head_index + 1) * HD)
        part = last_contract(grads[:, :HD], key_weight[:, cols])
        part += last_contract(grads[:, HD:], value_weight[:, cols])
        total[...] = total[...] + part if head_index else part
    place = lax.axis_index(head_axis)
    shares = 2 * input_keep.shape[0]
    width = total.shape[1] // shares
    for relative in range(shares):
        ref = input_send if relative % 2 else input_keep
        start = pl.multiple_of((place ^ relative) * width, width)
        ref[relative // 2] = total[:, pl.ds(start, width)]


def query_kernel(parts, row_axis, low, score_grads, keys, *refs):
    tile_ref = refs[-1]
    reads, _, latents = score_grads.shape
    piece = latents // GROUPS
    me = lax.axis_index(row_axis) // low
    side = lax.rem(me, 2)
    for part, (begin, end, bits) in enumerate(parts):
        for upper in range(GROUPS // 2):
            pair = (me // 2) ^ upper
            at = pl.ds(pl.multiple_of(pair * 2 * piece, 2 * piece), 2 * piece)
            for read_index in range(begin, end):
                slot = upper * reads + read_index
                tile_ref[slot] = rows_contract(score_grads[read_index, :, at], keys[...])
                for flip in range(2):
                    half = pl.ds(pl.multiple_of((side ^ flip) * piece, piece), piece)
                    relative = 2 * upper + flip
                    ref = refs[2 * part + (1 if relative & bits[0] else 0)]
                    index = 2 * ((relative & bits[1]) // bits[1]) + (relative & bits[2]) // bits[2]
                    ref[index, read_index - begin] = tile_ref[slot, half, :]


def assemble_kernel(weight_parts, query_parts, row_axis, low, *refs):
    query_out, key_out, value_out = refs[-3:]
    refs = list(refs[:-3])
    piece = key_out.shape[0] // GROUPS
    me = lax.axis_index(row_axis) // low
    for head_index, begin, end, bits in weight_parts:
        cols = slice(head_index * HD, (head_index + 1) * HD)
        for first in range(2):
            source = refs.pop(0)
            for second in range(2):
                base = group_at(bits, (first, second), me)
                for high in range(2):
                    start = pl.multiple_of((base + LAST_BIT * high) * piece, piece)
                    at = pl.ds(start, piece)
                    if begin == 0:
                        key_out[at, cols] = source[second, high, :, :HD]
                    if end == 2 * HD:
                        value_out[at, cols] = source[second, high, :, end - begin - HD :]
    for head_index, begin, end in query_parts:
        cols = slice(head_index * HD, (head_index + 1) * HD)
        total = refs.pop(0)[0]
        if low == 1:
            total = total + refs.pop(0)[0]
        query_out[begin:end, :, cols] = total


def shape_of(shape, dtype=jnp.float32):
    return jax.ShapeDtypeStruct(shape, dtype)


def scatter_steps(keep, send, count, bits):
    for index, bit in enumerate(bits):
        theirs = swap(send, "rows", count, bit)
        if index + 1 == len(bits):
            return keep, theirs
        middle = keep.shape[0] // 2
        send = keep[middle:] + theirs[middle:]
        keep = keep[:middle] + theirs[:middle]


def on_device(row_devices, head_devices, inputs, key_weight, value_weight, queries, out_grad):
    reads, latents, columns = queries.shape
    head_count = columns // HD
    row_count, features = inputs.shape
    low = row_devices // GROUPS
    tile = latents // (GROUPS // 2)
    piece = features // GROUPS
    operands = (inputs, key_weight, value_weight, queries, out_grad)
    block_work = pl.CostEstimate(
        flops=8 * reads * row_count * latents * HD,
        bytes_accessed=4 * 2**20,
        transcendentals=reads * row_count * latents,
    )

    projected = []
    for head_index in range(head_count):
        first = head_index == 0
        loaded = [
            pltpu.VMEM(item.shape[:-1] + ((HD,) if place else item.shape[-1:]), item.dtype)
            for place, item in enumerate(operands)
        ]
        projected.append(
            pl.pallas_call(
                functools.partial(first_kernel, tile)
                if first
                else functools.partial(later_kernel, tile, head_index),
                out_shape=(
                    shape_of((row_count, HD), jnp.bfloat16),
                    shape_of((row_count, HD), jnp.bfloat16),
                    shape_of((2 * reads, latents)),
                ),
                in_specs=[HBM] * 5 if first else [ANY] + [VMEM] * 5,
                out_specs=(VMEM,) * 3,
                scratch_shapes=loaded + [pltpu.SemaphoreType.DMA((5,))] if first else [],
                compiler_params=params(57 if first else 16),
                cost_estimate=block_work,
                name="project",
            )(*([] if first else [projected[0][2]]), *operands)
        )

    stats_parts = []
    for head_index in range(head_count):
        stats = projected[head_index][2]
        for bit in bits_of(row_devices)[:-1]:
            theirs = swap(stats, "rows", row_devices, bit)
            stats = pl.pallas_call(
                merge_kernel,
                out_shape=shape_of(stats.shape),
                in_specs=[VMEM] * 2,
                out_specs=VMEM,
                compiler_params=params(2),
                name="merge",
            )(stats, theirs)
        stats_parts.append((stats, swap(stats, "rows", row_devices, bits_of(row_devices)[-1])))

    order_low = (lax.axis_index("rows") % low) ^ jnp.arange(low, dtype=jnp.int32)
    low_bits = [bit for bit in bits_of(row_devices) if bit < low]

    def scatter_low(block, axis):
        if low == 1:
            return block
        parts = jnp.moveaxis(
            block.reshape(block.shape[:axis] + (low, -1) + block.shape[axis + 1 :]), axis, 0
        )
        parts = jnp.take(parts, order_low, axis=0)
        for bit in low_bits:
            parts = parts.reshape((-1, 2) + parts.shape[1:])
            parts = parts[:, 0] + swap(parts[:, 1], "rows", row_devices, bit)
        return parts[0]

    def sum_low(block):
        for bit in low_bits:
            block = block + row_swap(block, bit=bit)
        return block

    row_swap = functools.partial(swap, axis="rows", count=row_devices)

    def kernel_call(kernel, shapes, operands, scratch, limit, name):
        return pl.pallas_call(
            kernel,
            out_shape=[shape_of(*item) for item in shapes],
            in_specs=[ANY if name == "grads" and not place else VMEM for place in range(len(operands))],
            out_specs=[VMEM] * len(shapes),
            scratch_shapes=scratch,
            compiler_params=params(limit),
            cost_estimate=block_work,
            name=name,
        )(*operands)

    grads_out, query_out = [], []
    for head_index in range(head_count):
        keys, values, _ = projected[head_index]
        results = kernel_call(
            functools.partial(grads_kernel, head_index, "rows", low),
            [((row_count, 2 * HD), jnp.bfloat16), ((reads, row_count, latents), jnp.bfloat16)]
            + [
                ((2, 2, piece, end - begin),)
                for begin, end, _ in WEIGHT_PARTS[head_index]
                for _ in range(2)
            ],
            [
                grads_out[-1][0] if grads_out else stats_parts[0][0],
                *(inputs, keys, values, queries, out_grad),
                *stats_parts[head_index],
            ],
            [
                pltpu.VMEM((row_count, HD), jnp.float32),
                pltpu.VMEM((row_count, HD), jnp.float32),
                pltpu.VMEM((features, 2 * HD), jnp.float32),
                pltpu.VMEM((2 * reads, latents), jnp.float32),
            ],
            20,
            "grads",
        )
        grads_out.append(results)
        query_out.append(
            kernel_call(
                functools.partial(query_kernel, QUERY_PARTS[head_index], "rows", low),
                [
                    ((GROUPS // 2, end - begin, latents // GROUPS, HD),)
                    for begin, end, _ in QUERY_PARTS[head_index]
                    for _ in range(2)
                ],
                [results[1], keys],
                [pltpu.VMEM((GROUPS // 2 * reads, tile, HD), jnp.float32)],
                16,
                "query",
            )
        )

    assembled, weight_list, marks = [], [], []
    for head_index in range(head_count):
        for part, (begin, end, bits) in enumerate(WEIGHT_PARTS[head_index]):
            keep, send = grads_out[head_index][2 + 2 * part : 4 + 2 * part]
            first, second = (bit * low for bit in bits)
            mine, theirs = scatter_steps(keep, send, row_devices, (first, second))
            marks.append(mine)
            mine = mine + theirs
            mine = sum_low(mine + row_swap(mine, bit=LAST_BIT * low))
            near = jnp.concatenate([mine, row_swap(mine, bit=second)], axis=0)
            assembled += [near, row_swap(near, bit=first)]
            weight_list.append((head_index, begin, end, bits))
    query_list = []
    for head_index in range(head_count):
        for part, (begin, end, bits) in enumerate(QUERY_PARTS[head_index]):
            keep, send = query_out[head_index][2 * part : 2 * part + 2]
            mine, theirs = scatter_steps(keep, send, row_devices, [bit * low for bit in bits])
            if low == 1:
                assembled += [mine, theirs]
            else:
                assembled.append(scatter_low((mine + theirs)[0], 1)[None])
            query_list.append((head_index, begin, end))

    share = ((head_devices // 2, row_count, features // head_devices),)
    after = marks[0]
    input_keep, input_send = pl.pallas_call(
        functools.partial(input_kernel, "heads"),
        out_shape=[shape_of(*share)] * 2,
        in_specs=[VMEM] * (2 + head_count) + [ANY],
        out_specs=[VMEM] * 2,
        scratch_shapes=[pltpu.VMEM((row_count, features), jnp.float32)],
        compiler_params=params(16),
        cost_estimate=block_work,
        name="input",
    )(key_weight, value_weight, *(item[0] for item in grads_out), after)
    total = input_keep + swap(input_send, "heads", head_devices, 1)
    for bit in bits_of(head_devices)[1:]:
        pairs = total.reshape((-1, 2) + total.shape[1:])
        total = pairs[:, 0] + swap(pairs[:, 1], "heads", head_devices, bit)

    query_grad, key_weight_grad, value_weight_grad = pl.pallas_call(
        functools.partial(assemble_kernel, weight_list, query_list, "rows", low),
        out_shape=(shape_of((reads, latents // row_devices, columns)),)
        + (shape_of((features, columns)),) * 2,
        in_specs=[VMEM] * len(assembled),
        out_specs=(VMEM,) * 3,
        compiler_params=params(8),
        name="assemble",
    )(*assembled)
    return (query_grad, key_weight_grad, value_weight_grad, total[0])


def solution(mesh):
    in_specs = (
        P("rows", None),
        P(None, "heads"),
        P(None, "heads"),
        P(None, None, "heads"),
        P(None, None, "heads"),
    )
    out_specs = (P(None, "rows", "heads"), P(None, "heads"), P(None, "heads"), P("rows", "heads"))

    def body(*args):
        return on_device(mesh.shape["rows"], mesh.shape["heads"], *args)

    return jax.shard_map(body, mesh=mesh, in_specs=in_specs, out_specs=out_specs, check_vma=False)
```

```python
import functools

import jax
import jax.numpy as jnp
from jax import lax
from jax.experimental import pallas as pl
from jax.experimental.pallas import tpu as pltpu
from jax.sharding import PartitionSpec as P

HD = 128
GROUPS = 8
FACTOR = HD ** (-0.5)
LOG2_E = 1.4426950408889634
VMEM = pl.BlockSpec(memory_space=pltpu.VMEM)
HBM = pl.BlockSpec(memory_space=pltpu.HBM)
ANY = pl.BlockSpec(memory_space=pl.ANY)


def params(mebibytes):
    return pltpu.CompilerParams(vmem_limit_bytes=mebibytes * 1024 * 1024)


def last_contract(left, right):
    return lax.dot_general(
        left, right, (((1,), (1,)), ((), ())), preferred_element_type=jnp.float32
    )


def rows_contract(left, right):
    return lax.dot_general(
        left, right, (((0,), (0,)), ((), ())), preferred_element_type=jnp.float32
    )


def plain_dot(left, right):
    return jnp.dot(left, right, preferred_element_type=jnp.float32)


def swap(array, axis, count, bit):
    pairs = [(device, device ^ bit) for device in range(count)]
    return lax.ppermute(array, axis, pairs)


def bits_of(count):
    return [1 << place for place in range(count.bit_length() - 1)]


def head_statistics(
    tile, cols, wait, inputs, key_weight, value_weight, queries, out_grad, keys, values, stats
):
    reads, latents, _ = queries.shape
    wait(0, 1)
    keys[...] = plain_dot(inputs[...], key_weight[:, cols]).astype(jnp.bfloat16)
    wait(2)
    values[...] = plain_dot(inputs[...], value_weight[:, cols]).astype(jnp.bfloat16)
    wait(3, 4)

    @pl.loop(0, latents // tile, unroll=True)
    def _(step):
        at = pl.ds(pl.multiple_of(step * tile, tile), tile)
        for read_index in range(reads):
            scores = last_contract(keys[...], queries[read_index, at, cols])
            scores = scores * (FACTOR * LOG2_E)
            weighted = last_contract(values[...], out_grad[read_index, at, cols])
            top = jnp.max(scores, axis=0, keepdims=True)
            expos = jnp.exp2(scores - top)
            total = jnp.sum(expos, axis=0, keepdims=True)
            accum = jnp.sum(expos * weighted, axis=0, keepdims=True)
            stats[read_index : read_index + 1, at] = top + jnp.log2(total)
            stats[reads + read_index : reads + read_index + 1, at] = accum / total


def first_kernel(tile, *refs):
    sources, results, targets, sems = refs[:5], refs[5:8], refs[8:13], refs[13]
    loads = []
    for index, (source, target) in enumerate(zip(sources, targets)):
        if index:
            source = source.at[..., :HD]
        loads.append(pltpu.make_async_copy(source, target, sems.at[index]))
    for load in loads:
        load.start()

    def wait(*places):
        for place in places:
            loads[place].wait()

    head_statistics(tile, slice(0, HD), wait, *targets, *results)


def later_kernel(tile, head_index, *refs):
    cols = slice(head_index * HD, (head_index + 1) * HD)
    head_statistics(tile, cols, lambda *_: None, *refs)


def merged(mine, theirs):
    reads = mine.shape[0] // 2
    own, other = mine[:reads], theirs[:reads]
    top = jnp.maximum(own, other)
    own_share = jnp.exp2(own - top)
    other_share = jnp.exp2(other - top)
    total = own_share + other_share
    delta = (mine[reads:] * own_share + theirs[reads:] * other_share) / total
    return top + jnp.log2(total), delta


def merge_kernel(mine, theirs, result):
    reads = mine.shape[0] // 2
    result[:reads], result[reads:] = merged(mine, theirs)


def group_at(bits, relative, me):
    low = me % GROUPS
    group = 0
    for bit, flip in zip(bits, relative):
        group = group + ((low // bit) % 2 ^ flip) * bit
    return group


LAST_BIT = 4
WEIGHT_PARTS = (((0, 256, (1, 2)),), ((0, 256, (1, 2)),))
QUERY_PARTS = (((0, 2, (2, 1, 4)),), ((0, 2, (1, 2, 4)),))
DIRECT = ()


def grads_kernel(
    head_index, row_axis, low, after, inputs, keys, values, queries, out_grad, mine, theirs, *refs
):
    del after
    grads, score_grads = refs[:2]
    weight_parts = refs[2:-4]
    key_acc, value_acc, weights_ref, stats = refs[-4:]
    reads, latents, _ = queries.shape
    tile = latents // (GROUPS // 2)
    cols = slice(head_index * HD, (head_index + 1) * HD)
    stats[:reads], stats[reads:] = merged(mine, theirs)
    key_acc[...] = jnp.zeros_like(key_acc)
    value_acc[...] = jnp.zeros_like(value_acc)

    @pl.loop(0, latents // tile, unroll=True)
    def _(step):
        at = pl.ds(pl.multiple_of(step * tile, tile), tile)
        for read_index in range(reads):
            query_block = queries[read_index, at, cols]
            grad_block = out_grad[read_index, at, cols]
            scores = last_contract(keys[...], query_block) * (FACTOR * LOG2_E)
            weighted = last_contract(values[...], grad_block)
            probs = jnp.exp2(scores - stats[read_index : read_index + 1, at])
            delta = stats[reads + read_index : reads + read_index + 1, at]
            score_grad = (probs * (weighted - delta) * FACTOR).astype(jnp.bfloat16)
            score_grads[read_index, :, at] = score_grad
            key_acc[...] += plain_dot(score_grad, query_block)
            value_acc[...] += plain_dot(probs.astype(jnp.bfloat16), grad_block)

    grads[:, :HD] = key_acc[...].astype(jnp.bfloat16)
    grads[:, HD:] = value_acc[...].astype(jnp.bfloat16)
    weights_ref[...] = rows_contract(inputs[...], grads[...])
    features = inputs.shape[1]
    piece = features // GROUPS
    me = lax.axis_index(row_axis) // low
    for part, (begin, end, bits) in enumerate(WEIGHT_PARTS[head_index]):
        for first in range(2):
            ref = weight_parts[2 * part + first]
            for second in range(2):
                base = group_at(bits, (first, second), me)
                for high in range(2):
                    start = pl.multiple_of((base + LAST_BIT * high) * piece, piece)
                    ref[second, high] = weights_ref[pl.ds(start, piece), begin:end]


def input_kernel(head_axis, key_weight, value_weight, *refs):
    head_grads, (_, input_keep, input_send, total) = refs[:-4], refs[-4:]
    for head_index, grads in enumerate(head_grads):
        cols = slice(head_index * HD, (head_index + 1) * HD)
        part = last_contract(grads[:, :HD], key_weight[:, cols])
        part += last_contract(grads[:, HD:], value_weight[:, cols])
        total[...] = total[...] + part if head_index else part
    place = lax.axis_index(head_axis)
    shares = 2 * input_keep.shape[0]
    width = total.shape[1] // shares
    for relative in range(shares):
        ref = input_send if relative >= shares // 2 else input_keep
        start = pl.multiple_of((place ^ relative) * width, width)
        ref[relative % (shares // 2)] = total[:, pl.ds(start, width)]


def query_kernel(parts, row_axis, low, score_grads, keys, *refs):
    tile_ref = refs[-1]
    reads, _, latents = score_grads.shape
    piece = latents // GROUPS
    me = lax.axis_index(row_axis) // low
    side = lax.rem(me, 2)
    for part, (begin, end, bits) in enumerate(parts):
        for upper in range(GROUPS // 2):
            pair = (me // 2) ^ upper
            at = pl.ds(pl.multiple_of(pair * 2 * piece, 2 * piece), 2 * piece)
            for read_index in range(begin, end):
                slot = upper * reads + read_index
                tile_ref[slot] = rows_contract(score_grads[read_index, :, at], keys[...])
                for flip in range(2):
                    half = pl.ds(pl.multiple_of((side ^ flip) * piece, piece), piece)
                    relative = 2 * upper + flip
                    ref = refs[2 * part + (1 if relative & bits[0] else 0)]
                    index = 2 * ((relative & bits[1]) // bits[1]) + (relative & bits[2]) // bits[2]
                    ref[index, read_index - begin] = tile_ref[slot, half, :]


def assemble_kernel(weight_parts, query_parts, row_axis, low, *refs):
    query_out, key_out, value_out, input_out = refs[-4:]
    refs = list(refs[:-4])
    input_out[...] = refs.pop(0)[0] + refs.pop(0)[0]
    piece = key_out.shape[0] // GROUPS
    me = lax.axis_index(row_axis) // low
    for head_index, begin, end, bits in weight_parts:
        cols = slice(head_index * HD, (head_index + 1) * HD)
        for first in range(2):
            source = refs.pop(0)
            for second in range(2):
                base = group_at(bits, (first, second), me)
                for high in range(2):
                    start = pl.multiple_of((base + LAST_BIT * high) * piece, piece)
                    at = pl.ds(start, piece)
                    if begin == 0:
                        key_out[at, cols] = source[second, high, :, :HD]
                    if end == 2 * HD:
                        value_out[at, cols] = source[second, high, :, end - begin - HD :]
    for head_index, begin, end, terms in query_parts:
        cols = slice(head_index * HD, (head_index + 1) * HD)
        total = refs.pop(0)[0]
        for _ in range(terms - 1):
            total = total + refs.pop(0)[0]
        query_out[begin:end, :, cols] = total


def shape_of(shape, dtype=jnp.float32):
    return jax.ShapeDtypeStruct(shape, dtype)


def scatter_steps(keep, send, count, bits):
    for index, bit in enumerate(bits):
        theirs = swap(send, "rows", count, bit)
        if index + 1 == len(bits):
            return keep, theirs
        middle = keep.shape[0] // 2
        send = keep[middle:] + theirs[middle:]
        keep = keep[:middle] + theirs[:middle]


def on_device(row_devices, head_devices, inputs, key_weight, value_weight, queries, out_grad):
    reads, latents, columns = queries.shape
    head_count = columns // HD
    row_count, features = inputs.shape
    low = row_devices // GROUPS
    tile = latents // (GROUPS // 2)
    piece = features // GROUPS
    operands = (inputs, key_weight, value_weight, queries, out_grad)
    block_work = pl.CostEstimate(
        flops=8 * reads * row_count * latents * HD,
        bytes_accessed=4 * 2**20,
        transcendentals=reads * row_count * latents,
    )

    projected = []
    for head_index in range(head_count):
        first = head_index == 0
        loaded = [
            pltpu.VMEM(item.shape[:-1] + ((HD,) if place else item.shape[-1:]), item.dtype)
            for place, item in enumerate(operands)
        ]
        projected.append(
            pl.pallas_call(
                functools.partial(first_kernel, tile)
                if first
                else functools.partial(later_kernel, tile, head_index),
                out_shape=(
                    shape_of((row_count, HD), jnp.bfloat16),
                    shape_of((row_count, HD), jnp.bfloat16),
                    shape_of((2 * reads, latents)),
                ),
                in_specs=[HBM if first else VMEM] * 5,
                out_specs=(VMEM,) * 3,
                scratch_shapes=loaded + [pltpu.SemaphoreType.DMA((5,))] if first else [],
                compiler_params=params(57 if first else 16),
                cost_estimate=block_work,
                name="project",
            )(*operands)
        )

    stats_parts = []
    for head_index in range(head_count):
        stats = projected[head_index][2]
        for bit in bits_of(row_devices)[:-1]:
            theirs = swap(stats, "rows", row_devices, bit)
            stats = pl.pallas_call(
                merge_kernel,
                out_shape=shape_of(stats.shape),
                in_specs=[VMEM] * 2,
                out_specs=VMEM,
                compiler_params=params(2),
                name="merge",
            )(stats, theirs)
        stats_parts.append((stats, swap(stats, "rows", row_devices, bits_of(row_devices)[-1])))

    order_low = (lax.axis_index("rows") % low) ^ jnp.arange(low, dtype=jnp.int32)
    low_bits = [bit for bit in bits_of(row_devices) if bit < low]

    def scatter_low(block, axis):
        if low == 1:
            return block
        parts = jnp.moveaxis(
            block.reshape(block.shape[:axis] + (low, -1) + block.shape[axis + 1 :]), axis, 0
        )
        parts = jnp.take(parts, order_low, axis=0)
        for bit in low_bits:
            parts = parts.reshape((-1, 2) + parts.shape[1:])
            parts = parts[:, 0] + swap(parts[:, 1], "rows", row_devices, bit)
        return parts[0]

    def sum_low(block):
        for bit in low_bits:
            block = block + row_swap(block, bit=bit)
        return block

    row_swap = functools.partial(swap, axis="rows", count=row_devices)

    def kernel_call(kernel, shapes, operands, scratch, limit, name):
        return pl.pallas_call(
            kernel,
            out_shape=[shape_of(*item) for item in shapes],
            in_specs=[ANY if name == "grads" and not place else VMEM for place in range(len(operands))],
            out_specs=[VMEM] * len(shapes),
            scratch_shapes=scratch,
            compiler_params=params(limit),
            cost_estimate=block_work,
            name=name,
        )(*operands)

    grads_out, query_out = [], []
    for head_index in range(head_count):
        keys, values, _ = projected[head_index]
        results = kernel_call(
            functools.partial(grads_kernel, head_index, "rows", low),
            [((row_count, 2 * HD), jnp.bfloat16), ((reads, row_count, latents), jnp.bfloat16)]
            + [
                ((2, 2, piece, end - begin),)
                for begin, end, _ in WEIGHT_PARTS[head_index]
                for _ in range(2)
            ],
            [
                grads_out[-1][0] if grads_out else stats_parts[0][0],
                *(inputs, keys, values, queries, out_grad),
                *stats_parts[head_index],
            ],
            [
                pltpu.VMEM((row_count, HD), jnp.float32),
                pltpu.VMEM((row_count, HD), jnp.float32),
                pltpu.VMEM((features, 2 * HD), jnp.float32),
                pltpu.VMEM((2 * reads, latents), jnp.float32),
            ],
            20,
            "grads",
        )
        grads_out.append(results)
        query_out.append(
            kernel_call(
                functools.partial(query_kernel, QUERY_PARTS[head_index], "rows", low),
                [
                    ((GROUPS // 2, end - begin, latents // GROUPS, HD),)
                    for begin, end, _ in QUERY_PARTS[head_index]
                    for _ in range(2)
                ],
                [results[1], keys],
                [pltpu.VMEM((GROUPS // 2 * reads, tile, HD), jnp.float32)],
                16,
                "query",
            )
        )

    assembled, weight_list, marks = [], [], []
    for head_index in range(head_count):
        for part, (begin, end, bits) in enumerate(WEIGHT_PARTS[head_index]):
            keep, send = grads_out[head_index][2 + 2 * part : 4 + 2 * part]
            first, second = (bit * low for bit in bits)
            mine, theirs = scatter_steps(keep, send, row_devices, (first, second))
            marks.append(mine)
            mine = mine + theirs
            mine = sum_low(mine + row_swap(mine, bit=LAST_BIT * low))
            near = jnp.concatenate([mine, row_swap(mine, bit=second)], axis=0)
            assembled += [near, row_swap(near, bit=first)]
            weight_list.append((head_index, begin, end, bits))
    query_list = []
    for head_index in range(head_count):
        for part, (begin, end, bits) in enumerate(QUERY_PARTS[head_index]):
            keep, send = query_out[head_index][2 * part : 2 * part + 2]
            if (head_index, part) in DIRECT:
                theirs = row_swap(send, bit=bits[0] * low)
                terms = [keep[:1] + theirs[:1]]
                for index in range(1, keep.shape[0]):
                    bit = (index // 2) * bits[1] + (index % 2) * bits[2]
                    block = keep[index : index + 1] + theirs[index : index + 1]
                    terms.append(row_swap(block, bit=bit * low))
            else:
                terms = scatter_steps(keep, send, row_devices, [bit * low for bit in bits])
            if low > 1:
                terms = [scatter_low(sum(terms)[0], 1)[None]]
            assembled += terms
            query_list.append((head_index, begin, end, len(terms)))

    share = ((head_devices // 2, row_count, features // head_devices),)
    after = query_out[-1][0]
    input_keep, input_send = pl.pallas_call(
        functools.partial(input_kernel, "heads"),
        out_shape=[shape_of(*share)] * 2,
        in_specs=[VMEM] * (2 + head_count) + [ANY],
        out_specs=[VMEM] * 2,
        scratch_shapes=[pltpu.VMEM((row_count, features), jnp.float32)],
        compiler_params=params(16),
        cost_estimate=block_work,
        name="input",
    )(key_weight, value_weight, *(item[0] for item in grads_out), after)
    head_bits = bits_of(head_devices)[::-1]
    keep, theirs = input_keep, swap(input_send, "heads", head_devices, head_bits[0])
    for bit in head_bits[1:]:
        send = keep[bit:] + theirs[bit:]
        keep, theirs = keep[:bit] + theirs[:bit], swap(send, "heads", head_devices, bit)
    input_terms = (keep, theirs)

    query_grad, key_weight_grad, value_weight_grad, input_grad = pl.pallas_call(
        functools.partial(assemble_kernel, weight_list, query_list, "rows", low),
        out_shape=(shape_of((reads, latents // row_devices, columns)),)
        + (shape_of((features, columns)),) * 2
        + (shape_of((row_count, features // head_devices)),),
        in_specs=[VMEM] * (2 + len(assembled)),
        out_specs=(VMEM,) * 4,
        compiler_params=params(8),
        name="assemble",
    )(*input_terms, *assembled)
    return (query_grad, key_weight_grad, value_weight_grad, input_grad)


def solution(mesh):
    in_specs = (
        P("rows", None),
        P(None, "heads"),
        P(None, "heads"),
        P(None, None, "heads"),
        P(None, None, "heads"),
    )
    out_specs = (P(None, "rows", "heads"), P(None, "heads"), P(None, "heads"), P("rows", "heads"))

    def body(*args):
        return on_device(mesh.shape["rows"], mesh.shape["heads"], *args)

    return jax.shard_map(body, mesh=mesh, in_specs=in_specs, out_specs=out_specs, check_vma=False)
```

```python
import functools

import jax
import jax.numpy as jnp
from jax import lax
from jax.experimental import pallas as pl
from jax.experimental.pallas import tpu as pltpu
from jax.sharding import PartitionSpec as P

HD = 128
GROUPS = 8
FACTOR = HD ** (-0.5)
LOG2_E = 1.4426950408889634
VMEM = pl.BlockSpec(memory_space=pltpu.VMEM)
HBM = pl.BlockSpec(memory_space=pltpu.HBM)
ANY = pl.BlockSpec(memory_space=pl.ANY)


def params(mebibytes):
    return pltpu.CompilerParams(vmem_limit_bytes=mebibytes * 1024 * 1024)


def last_contract(left, right):
    return lax.dot_general(
        left, right, (((1,), (1,)), ((), ())), preferred_element_type=jnp.float32
    )


def rows_contract(left, right):
    return lax.dot_general(
        left, right, (((0,), (0,)), ((), ())), preferred_element_type=jnp.float32
    )


def plain_dot(left, right):
    return jnp.dot(left, right, preferred_element_type=jnp.float32)


def swap(array, axis, count, bit):
    pairs = [(device, device ^ bit) for device in range(count)]
    return lax.ppermute(array, axis, pairs)


def bits_of(count):
    return [1 << place for place in range(count.bit_length() - 1)]


def head_statistics(
    tile, cols, wait, inputs, key_weight, value_weight, queries, out_grad, keys, values, stats
):
    reads, latents, _ = queries.shape
    wait(0, 1)
    keys[...] = plain_dot(inputs[...], key_weight[:, cols]).astype(jnp.bfloat16)
    wait(2)
    values[...] = plain_dot(inputs[...], value_weight[:, cols]).astype(jnp.bfloat16)
    wait(3, 4)

    @pl.loop(0, latents // tile, unroll=True)
    def _(step):
        at = pl.ds(pl.multiple_of(step * tile, tile), tile)
        for read_index in range(reads):
            scores = last_contract(keys[...], queries[read_index, at, cols])
            scores = scores * (FACTOR * LOG2_E)
            weighted = last_contract(values[...], out_grad[read_index, at, cols])
            top = jnp.max(scores, axis=0, keepdims=True)
            expos = jnp.exp2(scores - top)
            total = jnp.sum(expos, axis=0, keepdims=True)
            accum = jnp.sum(expos * weighted, axis=0, keepdims=True)
            stats[read_index : read_index + 1, at] = top + jnp.log2(total)
            stats[reads + read_index : reads + read_index + 1, at] = accum / total


def first_kernel(tile, *refs):
    sources, results, targets, sems = refs[:5], refs[5:8], refs[8:13], refs[13]
    loads = []
    for index, (source, target) in enumerate(zip(sources, targets)):
        if index:
            source = source.at[..., :HD]
        loads.append(pltpu.make_async_copy(source, target, sems.at[index]))
    for load in loads:
        load.start()

    def wait(*places):
        for place in places:
            loads[place].wait()

    head_statistics(tile, slice(0, HD), wait, *targets, *results)


def later_kernel(tile, head_index, *refs):
    cols = slice(head_index * HD, (head_index + 1) * HD)
    head_statistics(tile, cols, lambda *_: None, *refs)


def merged(mine, theirs):
    reads = mine.shape[0] // 2
    own, other = mine[:reads], theirs[:reads]
    top = jnp.maximum(own, other)
    own_share = jnp.exp2(own - top)
    other_share = jnp.exp2(other - top)
    total = own_share + other_share
    delta = (mine[reads:] * own_share + theirs[reads:] * other_share) / total
    return top + jnp.log2(total), delta


def merge_kernel(mine, theirs, result):
    reads = mine.shape[0] // 2
    result[:reads], result[reads:] = merged(mine, theirs)


def group_at(bits, relative, me):
    low = me % GROUPS
    group = 0
    for bit, flip in zip(bits, relative):
        group = group + ((low // bit) % 2 ^ flip) * bit
    return group


LAST_BIT = 4
WEIGHT_PARTS = (((0, 256, (1, 2)),), ((0, 256, (1, 2)),))
QUERY_PARTS = (((0, 2, (2, 1, 4)),), ((0, 2, (1, 2, 4)),))
AFTER = {'w0.3': 'q0.1', 'w1.4': 'q0.2'}


def grads_kernel(
    head_index, row_axis, low, after, inputs, keys, values, queries, out_grad, mine, theirs, *refs
):
    del after
    grads, score_grads = refs[:2]
    weight_parts = refs[2:-4]
    key_acc, value_acc, weights_ref, stats = refs[-4:]
    reads, latents, _ = queries.shape
    tile = latents // (GROUPS // 2)
    cols = slice(head_index * HD, (head_index + 1) * HD)
    stats[:reads], stats[reads:] = merged(mine, theirs)
    key_acc[...] = jnp.zeros_like(key_acc)
    value_acc[...] = jnp.zeros_like(value_acc)

    @pl.loop(0, latents // tile, unroll=True)
    def _(step):
        at = pl.ds(pl.multiple_of(step * tile, tile), tile)
        for read_index in range(reads):
            query_block = queries[read_index, at, cols]
            grad_block = out_grad[read_index, at, cols]
            scores = last_contract(keys[...], query_block) * (FACTOR * LOG2_E)
            weighted = last_contract(values[...], grad_block)
            probs = jnp.exp2(scores - stats[read_index : read_index + 1, at])
            delta = stats[reads + read_index : reads + read_index + 1, at]
            score_grad = (probs * (weighted - delta) * FACTOR).astype(jnp.bfloat16)
            score_grads[read_index, :, at] = score_grad
            key_acc[...] += plain_dot(score_grad, query_block)
            value_acc[...] += plain_dot(probs.astype(jnp.bfloat16), grad_block)

    grads[:, :HD] = key_acc[...].astype(jnp.bfloat16)
    grads[:, HD:] = value_acc[...].astype(jnp.bfloat16)
    weights_ref[...] = rows_contract(inputs[...], grads[...])
    features = inputs.shape[1]
    piece = features // GROUPS
    me = lax.axis_index(row_axis) // low
    for part, (begin, end, bits) in enumerate(WEIGHT_PARTS[head_index]):
        for first in range(2):
            ref = weight_parts[2 * part + first]
            for second in range(2):
                base = group_at(bits, (first, second), me)
                for high in range(2):
                    start = pl.multiple_of((base + LAST_BIT * high) * piece, piece)
                    ref[second, high] = weights_ref[pl.ds(start, piece), begin:end]


def input_kernel(head_axis, key_weight, value_weight, *refs):
    head_grads, (_, input_keep, input_send, total) = refs[:-4], refs[-4:]
    for head_index, grads in enumerate(head_grads):
        cols = slice(head_index * HD, (head_index + 1) * HD)
        part = last_contract(grads[:, :HD], key_weight[:, cols])
        part += last_contract(grads[:, HD:], value_weight[:, cols])
        total[...] = total[...] + part if head_index else part
    place = lax.axis_index(head_axis)
    shares = 2 * input_keep.shape[0]
    width = total.shape[1] // shares
    for relative in range(shares):
        ref = input_send if relative >= shares // 2 else input_keep
        start = pl.multiple_of((place ^ relative) * width, width)
        ref[relative % (shares // 2)] = total[:, pl.ds(start, width)]


def query_kernel(parts, row_axis, low, score_grads, keys, *refs):
    tile_ref = refs[-1]
    reads, _, latents = score_grads.shape
    piece = latents // GROUPS
    me = lax.axis_index(row_axis) // low
    side = lax.rem(me, 2)
    for part, (begin, end, bits) in enumerate(parts):
        for upper in range(GROUPS // 2):
            pair = (me // 2) ^ upper
            at = pl.ds(pl.multiple_of(pair * 2 * piece, 2 * piece), 2 * piece)
            for read_index in range(begin, end):
                slot = upper * reads + read_index
                tile_ref[slot] = rows_contract(score_grads[read_index, :, at], keys[...])
                for flip in range(2):
                    half = pl.ds(pl.multiple_of((side ^ flip) * piece, piece), piece)
                    relative = 2 * upper + flip
                    ref = refs[2 * part + (1 if relative & bits[0] else 0)]
                    index = 2 * ((relative & bits[1]) // bits[1]) + (relative & bits[2]) // bits[2]
                    ref[index, read_index - begin] = tile_ref[slot, half, :]


def assemble_kernel(weight_parts, query_parts, row_axis, low, *refs):
    query_out, key_out, value_out, input_out = refs[-4:]
    refs = list(refs[:-4])
    input_out[...] = refs.pop(0)[0] + refs.pop(0)[0]
    piece = key_out.shape[0] // GROUPS
    me = lax.axis_index(row_axis) // low
    for head_index, begin, end, bits in weight_parts:
        cols = slice(head_index * HD, (head_index + 1) * HD)
        for first in range(2):
            source = refs.pop(0)
            for second in range(2):
                base = group_at(bits, (first, second), me)
                for high in range(2):
                    start = pl.multiple_of((base + LAST_BIT * high) * piece, piece)
                    at = pl.ds(start, piece)
                    if begin == 0:
                        key_out[at, cols] = source[second, high, :, :HD]
                    if end == 2 * HD:
                        value_out[at, cols] = source[second, high, :, end - begin - HD :]
    for head_index, begin, end, terms in query_parts:
        cols = slice(head_index * HD, (head_index + 1) * HD)
        total = refs.pop(0)[0]
        for _ in range(terms - 1):
            total = total + refs.pop(0)[0]
        query_out[begin:end, :, cols] = total


def shape_of(shape, dtype=jnp.float32):
    return jax.ShapeDtypeStruct(shape, dtype)


def add_kernel(mine, theirs, after, total):
    del after
    total[...] = mine[...] + theirs[...]


def stack_kernel(mine, theirs, after, both):
    del after
    both[: mine.shape[0]] = mine[...]
    both[mine.shape[0] :] = theirs[...]


def on_device(row_devices, head_devices, inputs, key_weight, value_weight, queries, out_grad):
    reads, latents, columns = queries.shape
    head_count = columns // HD
    row_count, features = inputs.shape
    low = row_devices // GROUPS
    tile = latents // (GROUPS // 2)
    piece = features // GROUPS
    operands = (inputs, key_weight, value_weight, queries, out_grad)
    block_work = pl.CostEstimate(
        flops=8 * reads * row_count * latents * HD,
        bytes_accessed=4 * 2**20,
        transcendentals=reads * row_count * latents,
    )

    projected = []
    for head_index in range(head_count):
        first = head_index == 0
        loaded = [
            pltpu.VMEM(item.shape[:-1] + ((HD,) if place else item.shape[-1:]), item.dtype)
            for place, item in enumerate(operands)
        ]
        projected.append(
            pl.pallas_call(
                functools.partial(first_kernel, tile)
                if first
                else functools.partial(later_kernel, tile, head_index),
                out_shape=(
                    shape_of((row_count, HD), jnp.bfloat16),
                    shape_of((row_count, HD), jnp.bfloat16),
                    shape_of((2 * reads, latents)),
                ),
                in_specs=[HBM if first else VMEM] * 5,
                out_specs=(VMEM,) * 3,
                scratch_shapes=loaded + [pltpu.SemaphoreType.DMA((5,))] if first else [],
                compiler_params=params(57 if first else 16),
                cost_estimate=block_work,
                name="project",
            )(*operands)
        )

    stats_parts = []
    for head_index in range(head_count):
        stats = projected[head_index][2]
        for bit in bits_of(row_devices)[:-1]:
            theirs = swap(stats, "rows", row_devices, bit)
            stats = pl.pallas_call(
                merge_kernel,
                out_shape=shape_of(stats.shape),
                in_specs=[VMEM] * 2,
                out_specs=VMEM,
                compiler_params=params(2),
                name="merge",
            )(stats, theirs)
        stats_parts.append((stats, swap(stats, "rows", row_devices, bits_of(row_devices)[-1])))

    order_low = (lax.axis_index("rows") % low) ^ jnp.arange(low, dtype=jnp.int32)
    low_bits = [bit for bit in bits_of(row_devices) if bit < low]

    def scatter_low(block, axis):
        if low == 1:
            return block
        parts = jnp.moveaxis(
            block.reshape(block.shape[:axis] + (low, -1) + block.shape[axis + 1 :]), axis, 0
        )
        parts = jnp.take(parts, order_low, axis=0)
        for bit in low_bits:
            parts = parts.reshape((-1, 2) + parts.shape[1:])
            parts = parts[:, 0] + swap(parts[:, 1], "rows", row_devices, bit)
        return parts[0]

    def sum_low(block):
        for bit in low_bits:
            block = block + row_swap(block, bit=bit)
        return block

    row_swap = functools.partial(swap, axis="rows", count=row_devices)

    def kernel_call(kernel, shapes, operands, scratch, limit, name):
        return pl.pallas_call(
            kernel,
            out_shape=[shape_of(*item) for item in shapes],
            in_specs=[ANY if name == "grads" and not place else VMEM for place in range(len(operands))],
            out_specs=[VMEM] * len(shapes),
            scratch_shapes=scratch,
            compiler_params=params(limit),
            cost_estimate=block_work,
            name=name,
        )(*operands)

    grads_out, query_out = [], []
    for head_index in range(head_count):
        keys, values, _ = projected[head_index]
        results = kernel_call(
            functools.partial(grads_kernel, head_index, "rows", low),
            [((row_count, 2 * HD), jnp.bfloat16), ((reads, row_count, latents), jnp.bfloat16)]
            + [
                ((2, 2, piece, end - begin),)
                for begin, end, _ in WEIGHT_PARTS[head_index]
                for _ in range(2)
            ],
            [
                grads_out[-1][0] if grads_out else stats_parts[0][0],
                *(inputs, keys, values, queries, out_grad),
                *stats_parts[head_index],
            ],
            [
                pltpu.VMEM((row_count, HD), jnp.float32),
                pltpu.VMEM((row_count, HD), jnp.float32),
                pltpu.VMEM((features, 2 * HD), jnp.float32),
                pltpu.VMEM((2 * reads, latents), jnp.float32),
            ],
            20,
            "grads",
        )
        grads_out.append(results)
        query_out.append(
            kernel_call(
                functools.partial(query_kernel, QUERY_PARTS[head_index], "rows", low),
                [
                    ((GROUPS // 2, end - begin, latents // GROUPS, HD),)
                    for begin, end, _ in QUERY_PARTS[head_index]
                    for _ in range(2)
                ],
                [results[1], keys],
                [pltpu.VMEM((GROUPS // 2 * reads, tile, HD), jnp.float32)],
                16,
                "query",
            )
        )

    def added(kernel, shape, mine, theirs, after):
        return pl.pallas_call(
            kernel,
            out_shape=shape_of(shape),
            in_specs=[VMEM, VMEM, ANY],
            out_specs=VMEM,
            compiler_params=params(4),
            cost_estimate=pl.CostEstimate(flops=1024, bytes_accessed=1024, transcendentals=0),
            name="added",
        )(mine, theirs, after)

    marks = {}
    query_terms, query_list = [], []
    for head_index in range(head_count):
        for part, (begin, end, bits) in enumerate(QUERY_PARTS[head_index]):
            keep, send = query_out[head_index][2 * part : 2 * part + 2]
            for place, bit in enumerate(bits):
                theirs = row_swap(send, bit=bit * low)
                if place + 1 < len(bits):
                    middle = keep.shape[0] // 2
                    send = keep[middle:] + theirs[middle:]
                    keep = keep[:middle] + theirs[:middle]
                    marks[f"q{head_index}.{place + 1}"] = send
            terms = [keep, theirs]
            if low > 1:
                terms = [scatter_low((keep + theirs)[0], 1)[None]]
            query_terms += terms
            query_list.append((head_index, begin, end, len(terms)))

    weight_terms, weight_list = [], []
    for head_index in range(head_count):
        for part, (begin, end, bits) in enumerate(WEIGHT_PARTS[head_index]):
            keep, send = grads_out[head_index][2 + 2 * part : 4 + 2 * part]
            first, second = (bit * low for bit in bits)
            theirs = row_swap(send, bit=first)
            send = keep[1:] + theirs[1:]
            mine = keep[:1] + theirs[:1]
            marks[f"w{head_index}.1"] = send
            theirs = row_swap(send, bit=second)
            for place, bit in ((2, LAST_BIT * low), (3, second)):
                after = AFTER.get(f"w{head_index}.{place}")
                if after:
                    mine = added(add_kernel, mine.shape, mine, theirs, marks[after])
                else:
                    mine = mine + theirs
                if place == 3:
                    mine = sum_low(mine)
                theirs = row_swap(mine, bit=bit)
            after = AFTER.get(f"w{head_index}.4")
            shape = (2, *mine.shape[1:])
            if after:
                near = added(stack_kernel, shape, mine, theirs, marks[after])
            else:
                near = jnp.concatenate([mine, theirs], axis=0)
            weight_terms += [near, row_swap(near, bit=first)]
            weight_list.append((head_index, begin, end, bits))
    assembled = weight_terms + query_terms

    share = ((head_devices // 2, row_count, features // head_devices),)
    after = marks[AFTER["i.0"]] if "i.0" in AFTER else query_out[-1][0]
    input_keep, input_send = pl.pallas_call(
        functools.partial(input_kernel, "heads"),
        out_shape=[shape_of(*share)] * 2,
        in_specs=[VMEM] * (2 + head_count) + [ANY],
        out_specs=[VMEM] * 2,
        scratch_shapes=[pltpu.VMEM((row_count, features), jnp.float32)],
        compiler_params=params(16),
        cost_estimate=block_work,
        name="input",
    )(key_weight, value_weight, *(item[0] for item in grads_out), after)
    head_bits = bits_of(head_devices)[::-1]
    keep, theirs = input_keep, swap(input_send, "heads", head_devices, head_bits[0])
    for bit in head_bits[1:]:
        after = AFTER.get("i.1")
        if after:
            total = added(add_kernel, keep.shape, keep, theirs, marks[after])
            send, keep = total[bit:], total[:bit]
        else:
            send = keep[bit:] + theirs[bit:]
            keep = keep[:bit] + theirs[:bit]
        theirs = swap(send, "heads", head_devices, bit)
    input_terms = (keep, theirs)

    query_grad, key_weight_grad, value_weight_grad, input_grad = pl.pallas_call(
        functools.partial(assemble_kernel, weight_list, query_list, "rows", low),
        out_shape=(shape_of((reads, latents // row_devices, columns)),)
        + (shape_of((features, columns)),) * 2
        + (shape_of((row_count, features // head_devices)),),
        in_specs=[VMEM] * (2 + len(assembled)),
        out_specs=(VMEM,) * 4,
        compiler_params=params(8),
        name="assemble",
    )(*input_terms, *assembled)
    return (query_grad, key_weight_grad, value_weight_grad, input_grad)


def solution(mesh):
    in_specs = (
        P("rows", None),
        P(None, "heads"),
        P(None, "heads"),
        P(None, None, "heads"),
        P(None, None, "heads"),
    )
    out_specs = (P(None, "rows", "heads"), P(None, "heads"), P(None, "heads"), P("rows", "heads"))

    def body(*args):
        return on_device(mesh.shape["rows"], mesh.shape["heads"], *args)

    return jax.shard_map(body, mesh=mesh, in_specs=in_specs, out_specs=out_specs, check_vma=False)
```

```python
import functools

import jax
import jax.numpy as jnp
from jax import lax
from jax.experimental import pallas as pl
from jax.experimental.pallas import tpu as pltpu
from jax.sharding import PartitionSpec as P

HD = 128
GROUPS = 8
FACTOR = HD ** (-0.5)
LOG2_E = 1.4426950408889634
VMEM = pl.BlockSpec(memory_space=pltpu.VMEM)
HBM = pl.BlockSpec(memory_space=pltpu.HBM)
ANY = pl.BlockSpec(memory_space=pl.ANY)


def params(mebibytes):
    return pltpu.CompilerParams(vmem_limit_bytes=mebibytes * 1024 * 1024)


def last_contract(left, right):
    return lax.dot_general(
        left, right, (((1,), (1,)), ((), ())), preferred_element_type=jnp.float32
    )


def rows_contract(left, right):
    return lax.dot_general(
        left, right, (((0,), (0,)), ((), ())), preferred_element_type=jnp.float32
    )


def plain_dot(left, right):
    return jnp.dot(left, right, preferred_element_type=jnp.float32)


def swap(array, axis, count, bit):
    pairs = [(device, device ^ bit) for device in range(count)]
    return lax.ppermute(array, axis, pairs)


def counted(group):
    return group ^ ((group // 4) % 2 * 2)


def row_swap_of(array, count, bit):
    low = count // GROUPS
    if bit < low:
        return swap(array, "rows", count, bit)
    pairs = []
    for device in range(count):
        partner = counted(counted(device // low) ^ (bit // low))
        pairs.append((device, partner * low + device % low))
    return lax.ppermute(array, "rows", pairs)


def bits_of(count):
    return [1 << place for place in range(count.bit_length() - 1)]


def head_statistics(
    tile, cols, wait, inputs, key_weight, value_weight, queries, out_grad, keys, values, stats
):
    reads, latents, _ = queries.shape
    wait(0, 1)
    keys[...] = plain_dot(inputs[...], key_weight[:, cols]).astype(jnp.bfloat16)
    wait(2)
    values[...] = plain_dot(inputs[...], value_weight[:, cols]).astype(jnp.bfloat16)
    wait(3, 4)

    @pl.loop(0, latents // tile, unroll=True)
    def _(step):
        at = pl.ds(pl.multiple_of(step * tile, tile), tile)
        for read_index in range(reads):
            scores = last_contract(keys[...], queries[read_index, at, cols])
            scores = scores * (FACTOR * LOG2_E)
            weighted = last_contract(values[...], out_grad[read_index, at, cols])
            top = jnp.max(scores, axis=0, keepdims=True)
            expos = jnp.exp2(scores - top)
            total = jnp.sum(expos, axis=0, keepdims=True)
            accum = jnp.sum(expos * weighted, axis=0, keepdims=True)
            stats[read_index : read_index + 1, at] = top + jnp.log2(total)
            stats[reads + read_index : reads + read_index + 1, at] = accum / total


def first_kernel(tile, *refs):
    sources, results, targets, sems = refs[:5], refs[5:8], refs[8:13], refs[13]
    loads = []
    for index, (source, target) in enumerate(zip(sources, targets)):
        if index:
            source = source.at[..., :HD]
        loads.append(pltpu.make_async_copy(source, target, sems.at[index]))
    for load in loads:
        load.start()

    def wait(*places):
        for place in places:
            loads[place].wait()

    head_statistics(tile, slice(0, HD), wait, *targets, *results)


def later_kernel(tile, head_index, *refs):
    cols = slice(head_index * HD, (head_index + 1) * HD)
    head_statistics(tile, cols, lambda *_: None, *refs)


def merged(mine, theirs):
    reads = mine.shape[0] // 2
    own, other = mine[:reads], theirs[:reads]
    top = jnp.maximum(own, other)
    own_share = jnp.exp2(own - top)
    other_share = jnp.exp2(other - top)
    total = own_share + other_share
    delta = (mine[reads:] * own_share + theirs[reads:] * other_share) / total
    return top + jnp.log2(total), delta


def merge_kernel(mine, theirs, result):
    reads = mine.shape[0] // 2
    result[:reads], result[reads:] = merged(mine, theirs)


def group_at(bits, relative, high, me):
    flips = sum(bit * flip for bit, flip in zip(bits, relative))
    return counted((counted(me) % LAST_BIT ^ flips) + LAST_BIT * high)


LAST_BIT = 4
WEIGHT_PARTS = (((0, 256, (1, 2)),), ((0, 256, (1, 2)),))
QUERY_PARTS = (((0, 2, (2, 1, 4)),), ((0, 2, (1, 2, 4)),))


def grads_kernel(
    head_index, row_axis, low, after, inputs, keys, values, queries, out_grad, mine, theirs, *refs
):
    del after
    grads, score_grads = refs[:2]
    weight_parts = refs[2:-4]
    key_acc, value_acc, weights_ref, stats = refs[-4:]
    reads, latents, _ = queries.shape
    tile = latents // (GROUPS // 2)
    cols = slice(head_index * HD, (head_index + 1) * HD)
    stats[:reads], stats[reads:] = merged(mine, theirs)
    key_acc[...] = jnp.zeros_like(key_acc)
    value_acc[...] = jnp.zeros_like(value_acc)

    @pl.loop(0, latents // tile, unroll=True)
    def _(step):
        at = pl.ds(pl.multiple_of(step * tile, tile), tile)
        for read_index in range(reads):
            query_block = queries[read_index, at, cols]
            grad_block = out_grad[read_index, at, cols]
            scores = last_contract(keys[...], query_block) * (FACTOR * LOG2_E)
            weighted = last_contract(values[...], grad_block)
            probs = jnp.exp2(scores - stats[read_index : read_index + 1, at])
            delta = stats[reads + read_index : reads + read_index + 1, at]
            score_grad = (probs * (weighted - delta) * FACTOR).astype(jnp.bfloat16)
            score_grads[read_index, :, at] = score_grad
            key_acc[...] += plain_dot(score_grad, query_block)
            value_acc[...] += plain_dot(probs.astype(jnp.bfloat16), grad_block)

    grads[:, :HD] = key_acc[...].astype(jnp.bfloat16)
    grads[:, HD:] = value_acc[...].astype(jnp.bfloat16)
    weights_ref[...] = rows_contract(inputs[...], grads[...])
    features = inputs.shape[1]
    piece = features // GROUPS
    me = lax.axis_index(row_axis) // low
    for part, (begin, end, bits) in enumerate(WEIGHT_PARTS[head_index]):
        for first in range(2):
            ref = weight_parts[2 * part + first]
            for second in range(2):
                for high in range(2):
                    group = group_at(bits, (first, second), high, me)
                    start = pl.multiple_of(group * piece, piece)
                    ref[second, high] = weights_ref[pl.ds(start, piece), begin:end]


def input_kernel(head_axis, key_weight, value_weight, *refs):
    head_grads, (_, input_keep, input_send, total) = refs[:-4], refs[-4:]
    for head_index, grads in enumerate(head_grads):
        cols = slice(head_index * HD, (head_index + 1) * HD)
        part = last_contract(grads[:, :HD], key_weight[:, cols])
        part += last_contract(grads[:, HD:], value_weight[:, cols])
        total[...] = total[...] + part if head_index else part
    place = lax.axis_index(head_axis)
    shares = 2 * input_keep.shape[0]
    width = total.shape[1] // shares
    for relative in range(shares):
        ref = input_send if relative >= shares // 2 else input_keep
        start = pl.multiple_of((place ^ relative) * width, width)
        ref[relative % (shares // 2)] = total[:, pl.ds(start, width)]


def query_kernel(parts, row_axis, low, score_grads, keys, *refs):
    tile_ref = refs[-1]
    reads, _, latents = score_grads.shape
    piece = latents // GROUPS
    me = lax.axis_index(row_axis) // low
    side = lax.rem(me, 2)
    for part, (begin, end, bits) in enumerate(parts):
        for upper in range(GROUPS // 2):
            pair = counted(counted(me) ^ (2 * upper)) // 2
            at = pl.ds(pl.multiple_of(pair * 2 * piece, 2 * piece), 2 * piece)
            for read_index in range(begin, end):
                slot = upper * reads + read_index
                tile_ref[slot] = rows_contract(score_grads[read_index, :, at], keys[...])
                for flip in range(2):
                    half = pl.ds(pl.multiple_of((side ^ flip) * piece, piece), piece)
                    relative = 2 * upper + flip
                    ref = refs[2 * part + (1 if relative & bits[0] else 0)]
                    index = 2 * ((relative & bits[1]) // bits[1]) + (relative & bits[2]) // bits[2]
                    ref[index, read_index - begin] = tile_ref[slot, half, :]


def weights_kernel(weight_parts, row_axis, low, *refs):
    key_out, value_out, input_out, done = refs[-4:]
    refs = list(refs[:-4])
    input_out[...] = refs.pop(0)[0] + refs.pop(0)[0]
    done[...] = jnp.zeros_like(done)
    piece = key_out.shape[0] // GROUPS
    me = lax.axis_index(row_axis) // low
    for head_index, begin, end, bits in weight_parts:
        cols = slice(head_index * HD, (head_index + 1) * HD)
        for first in range(2):
            source = refs.pop(0)
            for second in range(2):
                for high in range(2):
                    group = group_at(bits, (first, second), high, me)
                    start = pl.multiple_of(group * piece, piece)
                    at = pl.ds(start, piece)
                    if begin == 0:
                        key_out[at, cols] = source[second, high, :, :HD]
                    if end == 2 * HD:
                        value_out[at, cols] = source[second, high, :, end - begin - HD :]


def queries_kernel(query_parts, after, *refs):
    del after
    query_out = refs[-1]
    refs = list(refs[:-1])
    for head_index, begin, end, terms in query_parts:
        cols = slice(head_index * HD, (head_index + 1) * HD)
        total = refs.pop(0)[0]
        for _ in range(terms - 1):
            total = total + refs.pop(0)[0]
        query_out[begin:end, :, cols] = total


def shape_of(shape, dtype=jnp.float32):
    return jax.ShapeDtypeStruct(shape, dtype)


def scatter_steps(keep, send, count, bits):
    for index, bit in enumerate(bits):
        theirs = row_swap_of(send, count, bit)
        if index + 1 == len(bits):
            return keep, theirs
        middle = keep.shape[0] // 2
        send = keep[middle:] + theirs[middle:]
        keep = keep[:middle] + theirs[:middle]


def on_device(row_devices, head_devices, inputs, key_weight, value_weight, queries, out_grad):
    reads, latents, columns = queries.shape
    head_count = columns // HD
    row_count, features = inputs.shape
    low = row_devices // GROUPS
    tile = latents // (GROUPS // 2)
    piece = features // GROUPS
    operands = (inputs, key_weight, value_weight, queries, out_grad)
    block_work = pl.CostEstimate(
        flops=8 * reads * row_count * latents * HD,
        bytes_accessed=4 * 2**20,
        transcendentals=reads * row_count * latents,
    )

    projected = []
    for head_index in range(head_count):
        first = head_index == 0
        loaded = [
            pltpu.VMEM(item.shape[:-1] + ((HD,) if place else item.shape[-1:]), item.dtype)
            for place, item in enumerate(operands)
        ]
        projected.append(
            pl.pallas_call(
                functools.partial(first_kernel, tile)
                if first
                else functools.partial(later_kernel, tile, head_index),
                out_shape=(
                    shape_of((row_count, HD), jnp.bfloat16),
                    shape_of((row_count, HD), jnp.bfloat16),
                    shape_of((2 * reads, latents)),
                ),
                in_specs=[HBM if first else VMEM] * 5,
                out_specs=(VMEM,) * 3,
                scratch_shapes=loaded + [pltpu.SemaphoreType.DMA((5,))] if first else [],
                compiler_params=params(57 if first else 16),
                cost_estimate=block_work,
                name="project",
            )(*operands)
        )

    stats_parts = []
    for head_index in range(head_count):
        stats = projected[head_index][2]
        for bit in bits_of(row_devices)[:-1]:
            theirs = row_swap_of(stats, row_devices, bit)
            stats = pl.pallas_call(
                merge_kernel,
                out_shape=shape_of(stats.shape),
                in_specs=[VMEM] * 2,
                out_specs=VMEM,
                compiler_params=params(2),
                name="merge",
            )(stats, theirs)
        stats_parts.append((stats, row_swap_of(stats, row_devices, bits_of(row_devices)[-1])))

    order_low = (lax.axis_index("rows") % low) ^ jnp.arange(low, dtype=jnp.int32)
    low_bits = [bit for bit in bits_of(row_devices) if bit < low]

    def scatter_low(block, axis):
        if low == 1:
            return block
        parts = jnp.moveaxis(
            block.reshape(block.shape[:axis] + (low, -1) + block.shape[axis + 1 :]), axis, 0
        )
        parts = jnp.take(parts, order_low, axis=0)
        for bit in low_bits:
            parts = parts.reshape((-1, 2) + parts.shape[1:])
            parts = parts[:, 0] + swap(parts[:, 1], "rows", row_devices, bit)
        return parts[0]

    def sum_low(block):
        for bit in low_bits:
            block = block + row_swap(block, bit=bit)
        return block

    row_swap = functools.partial(row_swap_of, count=row_devices)

    def kernel_call(kernel, shapes, operands, scratch, limit, name):
        return pl.pallas_call(
            kernel,
            out_shape=[shape_of(*item) for item in shapes],
            in_specs=[ANY if name == "grads" and not place else VMEM for place in range(len(operands))],
            out_specs=[VMEM] * len(shapes),
            scratch_shapes=scratch,
            compiler_params=params(limit),
            cost_estimate=block_work,
            name=name,
        )(*operands)

    grads_out, query_out = [], []
    for head_index in range(head_count):
        keys, values, _ = projected[head_index]
        results = kernel_call(
            functools.partial(grads_kernel, head_index, "rows", low),
            [((row_count, 2 * HD), jnp.bfloat16), ((reads, row_count, latents), jnp.bfloat16)]
            + [
                ((2, 2, piece, end - begin),)
                for begin, end, _ in WEIGHT_PARTS[head_index]
                for _ in range(2)
            ],
            [
                grads_out[-1][0] if grads_out else stats_parts[0][0],
                *(inputs, keys, values, queries, out_grad),
                *stats_parts[head_index],
            ],
            [
                pltpu.VMEM((row_count, HD), jnp.float32),
                pltpu.VMEM((row_count, HD), jnp.float32),
                pltpu.VMEM((features, 2 * HD), jnp.float32),
                pltpu.VMEM((2 * reads, latents), jnp.float32),
            ],
            20,
            "grads",
        )
        grads_out.append(results)
        query_out.append(
            kernel_call(
                functools.partial(query_kernel, QUERY_PARTS[head_index], "rows", low),
                [
                    ((GROUPS // 2, end - begin, latents // GROUPS, HD),)
                    for begin, end, _ in QUERY_PARTS[head_index]
                    for _ in range(2)
                ],
                [results[1], keys],
                [pltpu.VMEM((GROUPS // 2 * reads, tile, HD), jnp.float32)],
                16,
                "query",
            )
        )

    weight_terms, weight_list = [], []
    for head_index in range(head_count):
        for part, (begin, end, bits) in enumerate(WEIGHT_PARTS[head_index]):
            keep, send = grads_out[head_index][2 + 2 * part : 4 + 2 * part]
            first, second = (bit * low for bit in bits)
            mine, theirs = scatter_steps(keep, send, row_devices, (first, second))
            mine = mine + theirs
            mine = sum_low(mine + row_swap(mine, bit=LAST_BIT * low))
            near = jnp.concatenate([mine, row_swap(mine, bit=second)], axis=0)
            weight_terms += [near, row_swap(near, bit=first)]
            weight_list.append((head_index, begin, end, bits))
    query_terms, query_list = [], []
    for head_index in range(head_count):
        for part, (begin, end, bits) in enumerate(QUERY_PARTS[head_index]):
            keep, send = query_out[head_index][2 * part : 2 * part + 2]
            terms = scatter_steps(keep, send, row_devices, [bit * low for bit in bits])
            if low > 1:
                terms = [scatter_low(sum(terms)[0], 1)[None]]
            query_terms += terms
            query_list.append((head_index, begin, end, len(terms)))

    share = ((head_devices // 2, row_count, features // head_devices),)
    after = query_out[-1][0]
    input_keep, input_send = pl.pallas_call(
        functools.partial(input_kernel, "heads"),
        out_shape=[shape_of(*share)] * 2,
        in_specs=[VMEM] * (2 + head_count) + [ANY],
        out_specs=[VMEM] * 2,
        scratch_shapes=[pltpu.VMEM((row_count, features), jnp.float32)],
        compiler_params=params(16),
        cost_estimate=block_work,
        name="input",
    )(key_weight, value_weight, *(item[0] for item in grads_out), after)
    head_bits = bits_of(head_devices)[::-1]
    keep, theirs = input_keep, swap(input_send, "heads", head_devices, head_bits[0])
    for bit in head_bits[1:]:
        send = keep[bit:] + theirs[bit:]
        keep, theirs = keep[:bit] + theirs[:bit], swap(send, "heads", head_devices, bit)
    input_terms = (keep, theirs)

    key_weight_grad, value_weight_grad, input_grad, done = pl.pallas_call(
        functools.partial(weights_kernel, weight_list, "rows", low),
        out_shape=(shape_of((features, columns)),) * 2
        + (shape_of((row_count, features // head_devices)), shape_of((8, 128))),
        in_specs=[VMEM] * (2 + len(weight_terms)),
        out_specs=(VMEM,) * 4,
        compiler_params=params(8),
        name="weights",
    )(*input_terms, *weight_terms)
    query_grad = pl.pallas_call(
        functools.partial(queries_kernel, query_list),
        out_shape=shape_of((reads, latents // row_devices, columns)),
        in_specs=[ANY] + [VMEM] * len(query_terms),
        out_specs=VMEM,
        compiler_params=params(4),
        name="queries",
    )(done, *query_terms)
    return (query_grad, key_weight_grad, value_weight_grad, input_grad)


def solution(mesh):
    in_specs = (
        P("rows", None),
        P(None, "heads"),
        P(None, "heads"),
        P(None, None, "heads"),
        P(None, None, "heads"),
    )
    out_specs = (P(None, "rows", "heads"), P(None, "heads"), P(None, "heads"), P("rows", "heads"))

    def body(*args):
        return on_device(mesh.shape["rows"], mesh.shape["heads"], *args)

    return jax.shard_map(body, mesh=mesh, in_specs=in_specs, out_specs=out_specs, check_vma=False)
```

```python
import functools

import jax
import jax.numpy as jnp
from jax import lax
from jax.experimental import pallas as pl
from jax.experimental.pallas import tpu as pltpu
from jax.sharding import PartitionSpec as P

HD = 128
GROUPS = 8
FACTOR = HD ** (-0.5)
LOG2_E = 1.4426950408889634
VMEM = pl.BlockSpec(memory_space=pltpu.VMEM)
HBM = pl.BlockSpec(memory_space=pltpu.HBM)
ANY = pl.BlockSpec(memory_space=pl.ANY)


def params(mebibytes):
    return pltpu.CompilerParams(vmem_limit_bytes=mebibytes * 1024 * 1024)


def last_contract(left, right):
    return lax.dot_general(
        left, right, (((1,), (1,)), ((), ())), preferred_element_type=jnp.float32
    )


def rows_contract(left, right):
    return lax.dot_general(
        left, right, (((0,), (0,)), ((), ())), preferred_element_type=jnp.float32
    )


def plain_dot(left, right):
    return jnp.dot(left, right, preferred_element_type=jnp.float32)


def swap(array, axis, count, bit):
    pairs = [(device, device ^ bit) for device in range(count)]
    return lax.ppermute(array, axis, pairs)


def counted(group):
    return group ^ ((group // 4) % 2 * 2)


def row_swap_of(array, count, bit):
    low = count // GROUPS
    if bit < low:
        return swap(array, "rows", count, bit)
    pairs = []
    for device in range(count):
        partner = counted(counted(device // low) ^ (bit // low))
        pairs.append((device, partner * low + device % low))
    return lax.ppermute(array, "rows", pairs)


def bits_of(count):
    return [1 << place for place in range(count.bit_length() - 1)]


def head_statistics(
    tile, cols, wait, inputs, key_weight, value_weight, queries, out_grad, keys, values, stats
):
    reads, latents, _ = queries.shape
    wait(0, 1)
    keys[...] = plain_dot(inputs[...], key_weight[:, cols]).astype(jnp.bfloat16)
    wait(2)
    values[...] = plain_dot(inputs[...], value_weight[:, cols]).astype(jnp.bfloat16)
    wait(3, 4)

    @pl.loop(0, latents // tile, unroll=True)
    def _(step):
        at = pl.ds(pl.multiple_of(step * tile, tile), tile)
        for read_index in range(reads):
            scores = last_contract(keys[...], queries[read_index, at, cols])
            scores = scores * (FACTOR * LOG2_E)
            weighted = last_contract(values[...], out_grad[read_index, at, cols])
            top = jnp.max(scores, axis=0, keepdims=True)
            expos = jnp.exp2(scores - top)
            total = jnp.sum(expos, axis=0, keepdims=True)
            accum = jnp.sum(expos * weighted, axis=0, keepdims=True)
            stats[read_index : read_index + 1, at] = top + jnp.log2(total)
            stats[reads + read_index : reads + read_index + 1, at] = accum / total


def first_kernel(tile, *refs):
    sources, results, targets, sems = refs[:5], refs[5:8], refs[8:13], refs[13]
    loads = []
    for index, (source, target) in enumerate(zip(sources, targets)):
        if index:
            source = source.at[..., :HD]
        loads.append(pltpu.make_async_copy(source, target, sems.at[index]))
    for load in loads:
        load.start()

    def wait(*places):
        for place in places:
            loads[place].wait()

    head_statistics(tile, slice(0, HD), wait, *targets, *results)


def later_kernel(tile, head_index, *refs):
    cols = slice(head_index * HD, (head_index + 1) * HD)
    head_statistics(tile, cols, lambda *_: None, *refs)


def merged(mine, theirs):
    reads = mine.shape[0] // 2
    own, other = mine[:reads], theirs[:reads]
    top = jnp.maximum(own, other)
    own_share = jnp.exp2(own - top)
    other_share = jnp.exp2(other - top)
    total = own_share + other_share
    delta = (mine[reads:] * own_share + theirs[reads:] * other_share) / total
    return top + jnp.log2(total), delta


def merge_kernel(mine, theirs, result):
    reads = mine.shape[0] // 2
    result[:reads], result[reads:] = merged(mine, theirs)


def group_at(bits, relative, high, me):
    flips = sum(bit * flip for bit, flip in zip(bits, relative))
    return counted((counted(me) % LAST_BIT ^ flips) + LAST_BIT * high)


LAST_BIT = 4
WEIGHT_PARTS = (((0, 256, (1, 2)),), ((0, 256, (1, 2)),))
QUERY_PARTS = (((0, 2, (2, 1, 4)),), ((0, 2, (1, 2, 4)),))
AFTER = {'i.0': 'w0.2'}


def grads_kernel(
    head_index, row_axis, low, after, inputs, keys, values, queries, out_grad, mine, theirs, *refs
):
    del after
    grads, score_grads = refs[:2]
    weight_parts = refs[2:-4]
    key_acc, value_acc, weights_ref, stats = refs[-4:]
    reads, latents, _ = queries.shape
    tile = latents // (GROUPS // 2)
    cols = slice(head_index * HD, (head_index + 1) * HD)
    stats[:reads], stats[reads:] = merged(mine, theirs)
    key_acc[...] = jnp.zeros_like(key_acc)
    value_acc[...] = jnp.zeros_like(value_acc)

    @pl.loop(0, latents // tile, unroll=True)
    def _(step):
        at = pl.ds(pl.multiple_of(step * tile, tile), tile)
        for read_index in range(reads):
            query_block = queries[read_index, at, cols]
            grad_block = out_grad[read_index, at, cols]
            scores = last_contract(keys[...], query_block) * (FACTOR * LOG2_E)
            weighted = last_contract(values[...], grad_block)
            probs = jnp.exp2(scores - stats[read_index : read_index + 1, at])
            delta = stats[reads + read_index : reads + read_index + 1, at]
            score_grad = (probs * (weighted - delta) * FACTOR).astype(jnp.bfloat16)
            score_grads[read_index, :, at] = score_grad
            key_acc[...] += plain_dot(score_grad, query_block)
            value_acc[...] += plain_dot(probs.astype(jnp.bfloat16), grad_block)

    grads[:, :HD] = key_acc[...].astype(jnp.bfloat16)
    grads[:, HD:] = value_acc[...].astype(jnp.bfloat16)
    weights_ref[...] = rows_contract(inputs[...], grads[...])
    features = inputs.shape[1]
    piece = features // GROUPS
    me = lax.axis_index(row_axis) // low
    for part, (begin, end, bits) in enumerate(WEIGHT_PARTS[head_index]):
        for first in range(2):
            ref = weight_parts[2 * part + first]
            for second in range(2):
                for high in range(2):
                    group = group_at(bits, (first, second), high, me)
                    start = pl.multiple_of(group * piece, piece)
                    ref[second, high] = weights_ref[pl.ds(start, piece), begin:end]


def input_kernel(head_axis, key_weight, value_weight, *refs):
    head_grads, (_, input_keep, input_send, total) = refs[:-4], refs[-4:]
    for head_index, grads in enumerate(head_grads):
        cols = slice(head_index * HD, (head_index + 1) * HD)
        part = last_contract(grads[:, :HD], key_weight[:, cols])
        part += last_contract(grads[:, HD:], value_weight[:, cols])
        total[...] = total[...] + part if head_index else part
    place = lax.axis_index(head_axis)
    shares = 2 * input_keep.shape[0]
    width = total.shape[1] // shares
    for relative in range(shares):
        ref = input_send if relative >= shares // 2 else input_keep
        start = pl.multiple_of((place ^ relative) * width, width)
        ref[relative % (shares // 2)] = total[:, pl.ds(start, width)]


def query_kernel(parts, row_axis, low, after, score_grads, keys, *refs):
    del after
    tile_ref = refs[-1]
    reads, _, latents = score_grads.shape
    piece = latents // GROUPS
    me = lax.axis_index(row_axis) // low
    side = lax.rem(me, 2)
    for part, (begin, end, bits) in enumerate(parts):
        for upper in range(GROUPS // 2):
            pair = counted(counted(me) ^ (2 * upper)) // 2
            at = pl.ds(pl.multiple_of(pair * 2 * piece, 2 * piece), 2 * piece)
            for read_index in range(begin, end):
                slot = upper * reads + read_index
                tile_ref[slot] = rows_contract(score_grads[read_index, :, at], keys[...])
                for flip in range(2):
                    half = pl.ds(pl.multiple_of((side ^ flip) * piece, piece), piece)
                    relative = 2 * upper + flip
                    ref = refs[2 * part + (1 if relative & bits[0] else 0)]
                    index = 2 * ((relative & bits[1]) // bits[1]) + (relative & bits[2]) // bits[2]
                    ref[index, read_index - begin] = tile_ref[slot, half, :]


def weights_kernel(weight_parts, row_axis, low, *refs):
    key_out, value_out, input_out, done = refs[-4:]
    refs = list(refs[:-4])
    input_out[...] = refs.pop(0)[0] + refs.pop(0)[0]
    done[...] = jnp.zeros_like(done)
    piece = key_out.shape[0] // GROUPS
    me = lax.axis_index(row_axis) // low
    for head_index, begin, end, bits in weight_parts:
        cols = slice(head_index * HD, (head_index + 1) * HD)
        for first in range(2):
            source = refs.pop(0)
            for second in range(2):
                for high in range(2):
                    group = group_at(bits, (first, second), high, me)
                    start = pl.multiple_of(group * piece, piece)
                    at = pl.ds(start, piece)
                    if begin == 0:
                        key_out[at, cols] = source[second, high, :, :HD]
                    if end == 2 * HD:
                        value_out[at, cols] = source[second, high, :, end - begin - HD :]


def queries_kernel(query_parts, after, *refs):
    del after
    query_out = refs[-1]
    refs = list(refs[:-1])
    for head_index, begin, end, terms in query_parts:
        cols = slice(head_index * HD, (head_index + 1) * HD)
        total = refs.pop(0)[0]
        for _ in range(terms - 1):
            total = total + refs.pop(0)[0]
        query_out[begin:end, :, cols] = total


def shape_of(shape, dtype=jnp.float32):
    return jax.ShapeDtypeStruct(shape, dtype)


def add_kernel(mine, theirs, after, total):
    del after
    total[...] = mine[...] + theirs[...]


def on_device(row_devices, head_devices, inputs, key_weight, value_weight, queries, out_grad):
    reads, latents, columns = queries.shape
    head_count = columns // HD
    row_count, features = inputs.shape
    low = row_devices // GROUPS
    tile = latents // (GROUPS // 2)
    piece = features // GROUPS
    operands = (inputs, key_weight, value_weight, queries, out_grad)
    block_work = pl.CostEstimate(
        flops=8 * reads * row_count * latents * HD,
        bytes_accessed=4 * 2**20,
        transcendentals=reads * row_count * latents,
    )

    projected = []
    for head_index in range(head_count):
        first = head_index == 0
        loaded = [
            pltpu.VMEM(item.shape[:-1] + ((HD,) if place else item.shape[-1:]), item.dtype)
            for place, item in enumerate(operands)
        ]
        projected.append(
            pl.pallas_call(
                functools.partial(first_kernel, tile)
                if first
                else functools.partial(later_kernel, tile, head_index),
                out_shape=(
                    shape_of((row_count, HD), jnp.bfloat16),
                    shape_of((row_count, HD), jnp.bfloat16),
                    shape_of((2 * reads, latents)),
                ),
                in_specs=[HBM if first else VMEM] * 5,
                out_specs=(VMEM,) * 3,
                scratch_shapes=loaded + [pltpu.SemaphoreType.DMA((5,))] if first else [],
                compiler_params=params(57 if first else 16),
                cost_estimate=block_work,
                name="project",
            )(*operands)
        )

    stats_parts = []
    for head_index in range(head_count):
        stats = projected[head_index][2]
        for bit in bits_of(row_devices)[:-1]:
            theirs = row_swap_of(stats, row_devices, bit)
            stats = pl.pallas_call(
                merge_kernel,
                out_shape=shape_of(stats.shape),
                in_specs=[VMEM] * 2,
                out_specs=VMEM,
                compiler_params=params(2),
                name="merge",
            )(stats, theirs)
        stats_parts.append((stats, row_swap_of(stats, row_devices, bits_of(row_devices)[-1])))

    order_low = (lax.axis_index("rows") % low) ^ jnp.arange(low, dtype=jnp.int32)
    low_bits = [bit for bit in bits_of(row_devices) if bit < low]

    def scatter_low(block, axis):
        if low == 1:
            return block
        parts = jnp.moveaxis(
            block.reshape(block.shape[:axis] + (low, -1) + block.shape[axis + 1 :]), axis, 0
        )
        parts = jnp.take(parts, order_low, axis=0)
        for bit in low_bits:
            parts = parts.reshape((-1, 2) + parts.shape[1:])
            parts = parts[:, 0] + swap(parts[:, 1], "rows", row_devices, bit)
        return parts[0]

    def sum_low(block):
        for bit in low_bits:
            block = block + row_swap(block, bit=bit)
        return block

    row_swap = functools.partial(row_swap_of, count=row_devices)

    def kernel_call(kernel, shapes, operands, scratch, limit, name):
        return pl.pallas_call(
            kernel,
            out_shape=[shape_of(*item) for item in shapes],
            in_specs=[ANY] + [VMEM] * (len(operands) - 1),
            out_specs=[VMEM] * len(shapes),
            scratch_shapes=scratch,
            compiler_params=params(limit),
            cost_estimate=block_work,
            name=name,
        )(*operands)

    grads_out, weight_steps, marks = [], [], {}
    for head_index in range(head_count):
        keys, values, _ = projected[head_index]
        results = kernel_call(
            functools.partial(grads_kernel, head_index, "rows", low),
            [((row_count, 2 * HD), jnp.bfloat16), ((reads, row_count, latents), jnp.bfloat16)]
            + [
                ((2, 2, piece, end - begin),)
                for begin, end, _ in WEIGHT_PARTS[head_index]
                for _ in range(2)
            ],
            [
                grads_out[-1][0] if grads_out else stats_parts[0][0],
                *(inputs, keys, values, queries, out_grad),
                *stats_parts[head_index],
            ],
            [
                pltpu.VMEM((row_count, HD), jnp.float32),
                pltpu.VMEM((row_count, HD), jnp.float32),
                pltpu.VMEM((features, 2 * HD), jnp.float32),
                pltpu.VMEM((2 * reads, latents), jnp.float32),
            ],
            20,
            "grads",
        )
        grads_out.append(results)
        marks[f"A{head_index}"] = results[0]
        for part, (begin, end, bits) in enumerate(WEIGHT_PARTS[head_index]):
            keep, send = results[2 + 2 * part : 4 + 2 * part]
            theirs = row_swap(send, bit=bits[0] * low)
            send = keep[1:] + theirs[1:]
            mine = keep[:1] + theirs[:1]
            marks[f"w{head_index}.1"] = send
            weight_steps.append((mine, row_swap(send, bit=bits[1] * low)))

    query_terms, query_list = [], []
    for head_index in range(head_count):
        results = kernel_call(
            functools.partial(query_kernel, QUERY_PARTS[head_index], "rows", low),
            [
                ((GROUPS // 2, end - begin, latents // GROUPS, HD),)
                for begin, end, _ in QUERY_PARTS[head_index]
                for _ in range(2)
            ],
            [
                marks[AFTER.get(f"B{head_index}", f"A{head_index}")],
                grads_out[head_index][1],
                projected[head_index][0],
            ],
            [pltpu.VMEM((GROUPS // 2 * reads, tile, HD), jnp.float32)],
            16,
            "query",
        )
        marks[f"B{head_index}"] = results[0]
        for part, (begin, end, bits) in enumerate(QUERY_PARTS[head_index]):
            keep, send = results[2 * part : 2 * part + 2]
            for place, bit in enumerate(bits):
                theirs = row_swap(send, bit=bit * low)
                if place + 1 < len(bits):
                    middle = keep.shape[0] // 2
                    send = keep[middle:] + theirs[middle:]
                    keep = keep[:middle] + theirs[:middle]
                    marks[f"q{head_index}.{place + 1}"] = send
            terms = [keep, theirs]
            if low > 1:
                terms = [scatter_low((keep + theirs)[0], 1)[None]]
            query_terms += terms
            query_list.append((head_index, begin, end, len(terms)))

    def added(kernel, shape, mine, theirs, after):
        return pl.pallas_call(
            kernel,
            out_shape=shape_of(shape),
            in_specs=[VMEM, VMEM, ANY],
            out_specs=VMEM,
            compiler_params=params(4),
            cost_estimate=pl.CostEstimate(flops=1024, bytes_accessed=1024, transcendentals=0),
            name="added",
        )(mine, theirs, after)

    weight_terms, weight_list = [], []
    for head_index in range(head_count):
        for begin, end, bits in WEIGHT_PARTS[head_index]:
            mine, theirs = weight_steps.pop(0)
            first, second = (bit * low for bit in bits)
            for place, bit in ((2, LAST_BIT * low), (3, second)):
                after = AFTER.get(f"w{head_index}.{place}")
                if after:
                    mine = added(add_kernel, mine.shape, mine, theirs, marks[after])
                else:
                    mine = mine + theirs
                if place == 3:
                    mine = sum_low(mine)
                theirs = row_swap(mine, bit=bit)
                marks[f"w{head_index}.{place}"] = mine
            near = jnp.concatenate([mine, theirs], axis=0)
            weight_terms += [near, row_swap(near, bit=first)]
            weight_list.append((head_index, begin, end, bits))

    share = ((head_devices // 2, row_count, features // head_devices),)
    after = marks[AFTER.get("i.0", "B1")]
    input_keep, input_send = pl.pallas_call(
        functools.partial(input_kernel, "heads"),
        out_shape=[shape_of(*share)] * 2,
        in_specs=[VMEM] * (2 + head_count) + [ANY],
        out_specs=[VMEM] * 2,
        scratch_shapes=[pltpu.VMEM((row_count, features), jnp.float32)],
        compiler_params=params(16),
        cost_estimate=block_work,
        name="input",
    )(key_weight, value_weight, *(item[0] for item in grads_out), after)
    head_bits = bits_of(head_devices)[::-1]
    keep, theirs = input_keep, swap(input_send, "heads", head_devices, head_bits[0])
    for bit in head_bits[1:]:
        send = keep[bit:] + theirs[bit:]
        keep, theirs = keep[:bit] + theirs[:bit], swap(send, "heads", head_devices, bit)
    input_terms = (keep, theirs)

    key_weight_grad, value_weight_grad, input_grad, done = pl.pallas_call(
        functools.partial(weights_kernel, weight_list, "rows", low),
        out_shape=(shape_of((features, columns)),) * 2
        + (shape_of((row_count, features // head_devices)), shape_of((8, 128))),
        in_specs=[VMEM] * (2 + len(weight_terms)),
        out_specs=(VMEM,) * 4,
        compiler_params=params(8),
        name="weights",
    )(*input_terms, *weight_terms)
    query_grad = pl.pallas_call(
        functools.partial(queries_kernel, query_list),
        out_shape=shape_of((reads, latents // row_devices, columns)),
        in_specs=[ANY] + [VMEM] * len(query_terms),
        out_specs=VMEM,
        compiler_params=params(4),
        name="queries",
    )(done, *query_terms)
    return (query_grad, key_weight_grad, value_weight_grad, input_grad)


def solution(mesh):
    in_specs = (
        P("rows", None),
        P(None, "heads"),
        P(None, "heads"),
        P(None, None, "heads"),
        P(None, None, "heads"),
    )
    out_specs = (P(None, "rows", "heads"), P(None, "heads"), P(None, "heads"), P("rows", "heads"))

    def body(*args):
        return on_device(mesh.shape["rows"], mesh.shape["heads"], *args)

    return jax.shard_map(body, mesh=mesh, in_specs=in_specs, out_specs=out_specs, check_vma=False)
```

```python
import functools

import jax
import jax.numpy as jnp
from jax import lax
from jax.experimental import pallas as pl
from jax.experimental.pallas import tpu as pltpu
from jax.sharding import PartitionSpec as P

HD = 128
GROUPS = 8
FACTOR = HD ** (-0.5)
LOG2_E = 1.4426950408889634
VMEM = pl.BlockSpec(memory_space=pltpu.VMEM)
HBM = pl.BlockSpec(memory_space=pltpu.HBM)
ANY = pl.BlockSpec(memory_space=pl.ANY)


def params(mebibytes):
    return pltpu.CompilerParams(vmem_limit_bytes=mebibytes * 1024 * 1024)


def last_contract(left, right):
    return lax.dot_general(
        left, right, (((1,), (1,)), ((), ())), preferred_element_type=jnp.float32
    )


def rows_contract(left, right):
    return lax.dot_general(
        left, right, (((0,), (0,)), ((), ())), preferred_element_type=jnp.float32
    )


def plain_dot(left, right):
    return jnp.dot(left, right, preferred_element_type=jnp.float32)


def swap(array, axis, count, bit):
    pairs = [(device, device ^ bit) for device in range(count)]
    return lax.ppermute(array, axis, pairs)


def counted(group):
    return group ^ ((group // 4) % 2 * 2)


def row_swap_of(array, count, bit):
    low = count // GROUPS
    if bit < low:
        return swap(array, "rows", count, bit)
    pairs = []
    for device in range(count):
        partner = counted(counted(device // low) ^ (bit // low))
        pairs.append((device, partner * low + device % low))
    return lax.ppermute(array, "rows", pairs)


def bits_of(count):
    return [1 << place for place in range(count.bit_length() - 1)]


def head_statistics(
    tile, cols, wait, inputs, key_weight, value_weight, queries, out_grad, keys, values, stats
):
    reads, latents, _ = queries.shape
    wait(0, 1)
    keys[...] = plain_dot(inputs[...], key_weight[:, cols]).astype(jnp.bfloat16)
    wait(2)
    values[...] = plain_dot(inputs[...], value_weight[:, cols]).astype(jnp.bfloat16)
    wait(3, 4)

    @pl.loop(0, latents // tile, unroll=True)
    def _(step):
        at = pl.ds(pl.multiple_of(step * tile, tile), tile)
        for read_index in range(reads):
            scores = last_contract(keys[...], queries[read_index, at, cols])
            scores = scores * (FACTOR * LOG2_E)
            weighted = last_contract(values[...], out_grad[read_index, at, cols])
            top = jnp.max(scores, axis=0, keepdims=True)
            expos = jnp.exp2(scores - top)
            total = jnp.sum(expos, axis=0, keepdims=True)
            accum = jnp.sum(expos * weighted, axis=0, keepdims=True)
            stats[read_index : read_index + 1, at] = top + jnp.log2(total)
            stats[reads + read_index : reads + read_index + 1, at] = accum / total


def first_kernel(tile, *refs):
    sources, results, targets, sems = refs[:5], refs[5:8], refs[8:13], refs[13]
    loads = []
    for index, (source, target) in enumerate(zip(sources, targets)):
        if index:
            source = source.at[..., :HD]
        loads.append(pltpu.make_async_copy(source, target, sems.at[index]))
    for load in loads:
        load.start()

    def wait(*places):
        for place in places:
            loads[place].wait()

    head_statistics(tile, slice(0, HD), wait, *targets, *results)


def later_kernel(tile, head_index, *refs):
    cols = slice(head_index * HD, (head_index + 1) * HD)
    head_statistics(tile, cols, lambda *_: None, *refs)


def merged(mine, theirs):
    reads = mine.shape[0] // 2
    own, other = mine[:reads], theirs[:reads]
    top = jnp.maximum(own, other)
    own_share = jnp.exp2(own - top)
    other_share = jnp.exp2(other - top)
    total = own_share + other_share
    delta = (mine[reads:] * own_share + theirs[reads:] * other_share) / total
    return top + jnp.log2(total), delta


def merge_kernel(mine, theirs, result):
    reads = mine.shape[0] // 2
    result[:reads], result[reads:] = merged(mine, theirs)


def group_at(bits, relative, high, me):
    flips = sum(bit * flip for bit, flip in zip(bits, relative))
    return counted((counted(me) % LAST_BIT ^ flips) + LAST_BIT * high)


LAST_BIT = 4
WEIGHT_PARTS = (((0, 256, (1, 2)),), ((0, 256, (1, 2)),))
QUERY_PARTS = (((0, 2, (2, 1, 4)),), ((0, 2, (1, 2, 4)),))
AFTER = {'w1.2': 'q0.1', 'i.0': 'w0.3'}


def grads_kernel(
    head_index, row_axis, low, after, inputs, keys, values, queries, out_grad, mine, theirs, *refs
):
    del after
    grads, score_grads = refs[:2]
    weight_parts = refs[2:-4]
    key_acc, value_acc, weights_ref, stats = refs[-4:]
    reads, latents, _ = queries.shape
    tile = latents // (GROUPS // 2)
    cols = slice(head_index * HD, (head_index + 1) * HD)
    stats[:reads], stats[reads:] = merged(mine, theirs)
    key_acc[...] = jnp.zeros_like(key_acc)
    value_acc[...] = jnp.zeros_like(value_acc)

    @pl.loop(0, latents // tile, unroll=True)
    def _(step):
        at = pl.ds(pl.multiple_of(step * tile, tile), tile)
        for read_index in range(reads):
            query_block = queries[read_index, at, cols]
            grad_block = out_grad[read_index, at, cols]
            scores = last_contract(keys[...], query_block) * (FACTOR * LOG2_E)
            weighted = last_contract(values[...], grad_block)
            probs = jnp.exp2(scores - stats[read_index : read_index + 1, at])
            delta = stats[reads + read_index : reads + read_index + 1, at]
            score_grad = (probs * (weighted - delta) * FACTOR).astype(jnp.bfloat16)
            score_grads[read_index, :, at] = score_grad
            key_acc[...] += plain_dot(score_grad, query_block)
            value_acc[...] += plain_dot(probs.astype(jnp.bfloat16), grad_block)

    grads[:, :HD] = key_acc[...].astype(jnp.bfloat16)
    grads[:, HD:] = value_acc[...].astype(jnp.bfloat16)
    weights_ref[...] = rows_contract(inputs[...], grads[...])
    features = inputs.shape[1]
    piece = features // GROUPS
    me = lax.axis_index(row_axis) // low
    for part, (begin, end, bits) in enumerate(WEIGHT_PARTS[head_index]):
        for first in range(2):
            ref = weight_parts[2 * part + first]
            for second in range(2):
                for high in range(2):
                    group = group_at(bits, (first, second), high, me)
                    start = pl.multiple_of(group * piece, piece)
                    ref[second, high] = weights_ref[pl.ds(start, piece), begin:end]


def input_kernel(head_axis, key_weight, value_weight, *refs):
    head_grads, (_, input_keep, input_send, total) = refs[:-4], refs[-4:]
    for head_index, grads in enumerate(head_grads):
        cols = slice(head_index * HD, (head_index + 1) * HD)
        part = last_contract(grads[:, :HD], key_weight[:, cols])
        part += last_contract(grads[:, HD:], value_weight[:, cols])
        total[...] = total[...] + part if head_index else part
    place = lax.axis_index(head_axis)
    shares = 2 * input_keep.shape[0]
    width = total.shape[1] // shares
    for relative in range(shares):
        ref = input_send if relative >= shares // 2 else input_keep
        start = pl.multiple_of((place ^ relative) * width, width)
        ref[relative % (shares // 2)] = total[:, pl.ds(start, width)]


def query_kernel(parts, row_axis, low, after, score_grads, keys, *refs):
    del after
    tile_ref = refs[-1]
    reads, _, latents = score_grads.shape
    piece = latents // GROUPS
    me = lax.axis_index(row_axis) // low
    side = lax.rem(me, 2)
    for part, (begin, end, bits) in enumerate(parts):
        for upper in range(GROUPS // 2):
            pair = counted(counted(me) ^ (2 * upper)) // 2
            at = pl.ds(pl.multiple_of(pair * 2 * piece, 2 * piece), 2 * piece)
            for read_index in range(begin, end):
                slot = upper * reads + read_index
                tile_ref[slot] = rows_contract(score_grads[read_index, :, at], keys[...])
                for flip in range(2):
                    half = pl.ds(pl.multiple_of((side ^ flip) * piece, piece), piece)
                    relative = 2 * upper + flip
                    ref = refs[2 * part + (1 if relative & bits[0] else 0)]
                    index = 2 * ((relative & bits[1]) // bits[1]) + (relative & bits[2]) // bits[2]
                    ref[index, read_index - begin] = tile_ref[slot, half, :]


def weights_kernel(weight_parts, row_axis, low, *refs):
    key_out, value_out, input_out, done = refs[-4:]
    refs = list(refs[:-4])
    input_out[...] = refs.pop(0)[0] + refs.pop(0)[0]
    done[...] = jnp.zeros_like(done)
    piece = key_out.shape[0] // GROUPS
    me = lax.axis_index(row_axis) // low
    for head_index, begin, end, bits in weight_parts:
        cols = slice(head_index * HD, (head_index + 1) * HD)
        for first in range(2):
            source = refs.pop(0)
            for second in range(2):
                for high in range(2):
                    group = group_at(bits, (first, second), high, me)
                    start = pl.multiple_of(group * piece, piece)
                    at = pl.ds(start, piece)
                    if begin == 0:
                        key_out[at, cols] = source[second, high, :, :HD]
                    if end == 2 * HD:
                        value_out[at, cols] = source[second, high, :, end - begin - HD :]


def queries_kernel(query_parts, after, *refs):
    del after
    query_out = refs[-1]
    refs = list(refs[:-1])
    for head_index, begin, end, terms in query_parts:
        cols = slice(head_index * HD, (head_index + 1) * HD)
        total = refs.pop(0)[0]
        for _ in range(terms - 1):
            total = total + refs.pop(0)[0]
        query_out[begin:end, :, cols] = total


def shape_of(shape, dtype=jnp.float32):
    return jax.ShapeDtypeStruct(shape, dtype)


def add_kernel(mine, theirs, after, total):
    del after
    total[...] = mine[...] + theirs[...]


def on_device(row_devices, head_devices, inputs, key_weight, value_weight, queries, out_grad):
    reads, latents, columns = queries.shape
    head_count = columns // HD
    row_count, features = inputs.shape
    low = row_devices // GROUPS
    tile = latents // (GROUPS // 2)
    piece = features // GROUPS
    operands = (inputs, key_weight, value_weight, queries, out_grad)
    block_work = pl.CostEstimate(
        flops=8 * reads * row_count * latents * HD,
        bytes_accessed=4 * 2**20,
        transcendentals=reads * row_count * latents,
    )

    projected = []
    for head_index in range(head_count):
        first = head_index == 0
        loaded = [
            pltpu.VMEM(item.shape[:-1] + ((HD,) if place else item.shape[-1:]), item.dtype)
            for place, item in enumerate(operands)
        ]
        projected.append(
            pl.pallas_call(
                functools.partial(first_kernel, tile)
                if first
                else functools.partial(later_kernel, tile, head_index),
                out_shape=(
                    shape_of((row_count, HD), jnp.bfloat16),
                    shape_of((row_count, HD), jnp.bfloat16),
                    shape_of((2 * reads, latents)),
                ),
                in_specs=[HBM if first else VMEM] * 5,
                out_specs=(VMEM,) * 3,
                scratch_shapes=loaded + [pltpu.SemaphoreType.DMA((5,))] if first else [],
                compiler_params=params(57 if first else 16),
                cost_estimate=block_work,
                name="project",
            )(*operands)
        )

    stats_parts = []
    for head_index in range(head_count):
        stats = projected[head_index][2]
        for bit in bits_of(row_devices)[:-1]:
            theirs = row_swap_of(stats, row_devices, bit)
            stats = pl.pallas_call(
                merge_kernel,
                out_shape=shape_of(stats.shape),
                in_specs=[VMEM] * 2,
                out_specs=VMEM,
                compiler_params=params(2),
                name="merge",
            )(stats, theirs)
        stats_parts.append((stats, row_swap_of(stats, row_devices, bits_of(row_devices)[-1])))

    order_low = (lax.axis_index("rows") % low) ^ jnp.arange(low, dtype=jnp.int32)
    low_bits = [bit for bit in bits_of(row_devices) if bit < low]

    def scatter_low(block, axis):
        if low == 1:
            return block
        parts = jnp.moveaxis(
            block.reshape(block.shape[:axis] + (low, -1) + block.shape[axis + 1 :]), axis, 0
        )
        parts = jnp.take(parts, order_low, axis=0)
        for bit in low_bits:
            parts = parts.reshape((-1, 2) + parts.shape[1:])
            parts = parts[:, 0] + swap(parts[:, 1], "rows", row_devices, bit)
        return parts[0]

    def sum_low(block):
        for bit in low_bits:
            block = block + row_swap(block, bit=bit)
        return block

    row_swap = functools.partial(row_swap_of, count=row_devices)

    def kernel_call(kernel, shapes, operands, scratch, limit, name):
        return pl.pallas_call(
            kernel,
            out_shape=[shape_of(*item) for item in shapes],
            in_specs=[ANY] + [VMEM] * (len(operands) - 1),
            out_specs=[VMEM] * len(shapes),
            scratch_shapes=scratch,
            compiler_params=params(limit),
            cost_estimate=block_work,
            name=name,
        )(*operands)

    grads_out, weight_steps, marks = [], [], {}
    for head_index in range(head_count):
        keys, values, _ = projected[head_index]
        results = kernel_call(
            functools.partial(grads_kernel, head_index, "rows", low),
            [((row_count, 2 * HD), jnp.bfloat16), ((reads, row_count, latents), jnp.bfloat16)]
            + [
                ((2, 2, piece, end - begin),)
                for begin, end, _ in WEIGHT_PARTS[head_index]
                for _ in range(2)
            ],
            [
                grads_out[-1][0] if grads_out else stats_parts[0][0],
                *(inputs, keys, values, queries, out_grad),
                *stats_parts[head_index],
            ],
            [
                pltpu.VMEM((row_count, HD), jnp.float32),
                pltpu.VMEM((row_count, HD), jnp.float32),
                pltpu.VMEM((features, 2 * HD), jnp.float32),
                pltpu.VMEM((2 * reads, latents), jnp.float32),
            ],
            20,
            "grads",
        )
        grads_out.append(results)
        marks[f"A{head_index}"] = results[0]
        for part, (begin, end, bits) in enumerate(WEIGHT_PARTS[head_index]):
            keep, send = results[2 + 2 * part : 4 + 2 * part]
            theirs = row_swap(send, bit=bits[0] * low)
            send = keep[1:] + theirs[1:]
            mine = keep[:1] + theirs[:1]
            marks[f"w{head_index}.1"] = send
            weight_steps.append((mine, row_swap(send, bit=bits[1] * low)))

    query_terms, query_list = [], []
    for head_index in range(head_count):
        results = kernel_call(
            functools.partial(query_kernel, QUERY_PARTS[head_index], "rows", low),
            [
                ((GROUPS // 2, end - begin, latents // GROUPS, HD),)
                for begin, end, _ in QUERY_PARTS[head_index]
                for _ in range(2)
            ],
            [
                marks[AFTER.get(f"B{head_index}", f"A{head_index}")],
                grads_out[head_index][1],
                projected[head_index][0],
            ],
            [pltpu.VMEM((GROUPS // 2 * reads, tile, HD), jnp.float32)],
            16,
            "query",
        )
        marks[f"B{head_index}"] = results[0]
        for part, (begin, end, bits) in enumerate(QUERY_PARTS[head_index]):
            keep, send = results[2 * part : 2 * part + 2]
            for place, bit in enumerate(bits):
                theirs = row_swap(send, bit=bit * low)
                if place + 1 < len(bits):
                    middle = keep.shape[0] // 2
                    send = keep[middle:] + theirs[middle:]
                    keep = keep[:middle] + theirs[:middle]
                    marks[f"q{head_index}.{place + 1}"] = send
            terms = [keep, theirs]
            if low > 1:
                terms = [scatter_low((keep + theirs)[0], 1)[None]]
            query_terms += terms
            query_list.append((head_index, begin, end, len(terms)))

    def added(kernel, shape, mine, theirs, after):
        return pl.pallas_call(
            kernel,
            out_shape=shape_of(shape),
            in_specs=[VMEM, VMEM, ANY],
            out_specs=VMEM,
            compiler_params=params(4),
            cost_estimate=pl.CostEstimate(flops=1024, bytes_accessed=1024, transcendentals=0),
            name="added",
        )(mine, theirs, after)

    weight_terms, weight_list = [], []
    for head_index in range(head_count):
        for begin, end, bits in WEIGHT_PARTS[head_index]:
            mine, theirs = weight_steps.pop(0)
            first, second = (bit * low for bit in bits)
            for place, bit in ((2, LAST_BIT * low), (3, second)):
                after = AFTER.get(f"w{head_index}.{place}")
                if after:
                    mine = added(add_kernel, mine.shape, mine, theirs, marks[after])
                else:
                    mine = mine + theirs
                if place == 3:
                    mine = sum_low(mine)
                theirs = row_swap(mine, bit=bit)
                marks[f"w{head_index}.{place}"] = mine
            near = jnp.concatenate([mine, theirs], axis=0)
            weight_terms += [near, row_swap(near, bit=first)]
            weight_list.append((head_index, begin, end, bits))

    share = ((head_devices // 2, row_count, features // head_devices),)
    after = marks[AFTER.get("i.0", "B1")]
    input_keep, input_send = pl.pallas_call(
        functools.partial(input_kernel, "heads"),
        out_shape=[shape_of(*share)] * 2,
        in_specs=[VMEM] * (2 + head_count) + [ANY],
        out_specs=[VMEM] * 2,
        scratch_shapes=[pltpu.VMEM((row_count, features), jnp.float32)],
        compiler_params=params(16),
        cost_estimate=block_work,
        name="input",
    )(key_weight, value_weight, *(item[0] for item in grads_out), after)
    head_bits = bits_of(head_devices)[::-1]
    keep, theirs = input_keep, swap(input_send, "heads", head_devices, head_bits[0])
    for bit in head_bits[1:]:
        send = keep[bit:] + theirs[bit:]
        keep, theirs = keep[:bit] + theirs[:bit], swap(send, "heads", head_devices, bit)
    input_terms = (keep, theirs)

    key_weight_grad, value_weight_grad, input_grad, done = pl.pallas_call(
        functools.partial(weights_kernel, weight_list, "rows", low),
        out_shape=(shape_of((features, columns)),) * 2
        + (shape_of((row_count, features // head_devices)), shape_of((8, 128))),
        in_specs=[VMEM] * (2 + len(weight_terms)),
        out_specs=(VMEM,) * 4,
        compiler_params=params(8),
        name="weights",
    )(*input_terms, *weight_terms)
    query_grad = pl.pallas_call(
        functools.partial(queries_kernel, query_list),
        out_shape=shape_of((reads, latents // row_devices, columns)),
        in_specs=[ANY] + [VMEM] * len(query_terms),
        out_specs=VMEM,
        compiler_params=params(4),
        name="queries",
    )(done, *query_terms)
    return (query_grad, key_weight_grad, value_weight_grad, input_grad)


def solution(mesh):
    in_specs = (
        P("rows", None),
        P(None, "heads"),
        P(None, "heads"),
        P(None, None, "heads"),
        P(None, None, "heads"),
    )
    out_specs = (P(None, "rows", "heads"), P(None, "heads"), P(None, "heads"), P("rows", "heads"))

    def body(*args):
        return on_device(mesh.shape["rows"], mesh.shape["heads"], *args)

    return jax.shard_map(body, mesh=mesh, in_specs=in_specs, out_specs=out_specs, check_vma=False)
```

```python
import functools

import jax
import jax.numpy as jnp
from jax import lax
from jax.experimental import pallas as pl
from jax.experimental.pallas import tpu as pltpu
from jax.sharding import PartitionSpec as P

HD = 128
GROUPS = 8
FACTOR = HD ** (-0.5)
LOG2_E = 1.4426950408889634
VMEM = pl.BlockSpec(memory_space=pltpu.VMEM)
HBM = pl.BlockSpec(memory_space=pltpu.HBM)
ANY = pl.BlockSpec(memory_space=pl.ANY)


def params(mebibytes):
    return pltpu.CompilerParams(vmem_limit_bytes=mebibytes * 1024 * 1024)


def last_contract(left, right):
    return lax.dot_general(
        left, right, (((1,), (1,)), ((), ())), preferred_element_type=jnp.float32
    )


def rows_contract(left, right):
    return lax.dot_general(
        left, right, (((0,), (0,)), ((), ())), preferred_element_type=jnp.float32
    )


def plain_dot(left, right):
    return jnp.dot(left, right, preferred_element_type=jnp.float32)


def swap(array, axis, count, bit):
    pairs = [(device, device ^ bit) for device in range(count)]
    return lax.ppermute(array, axis, pairs)


def counted(group):
    return group ^ ((group // 4) % 2 * 2)


def row_swap_of(array, count, bit):
    low = count // GROUPS
    if bit < low:
        return swap(array, "rows", count, bit)
    pairs = []
    for device in range(count):
        partner = counted(counted(device // low) ^ (bit // low))
        pairs.append((device, partner * low + device % low))
    return lax.ppermute(array, "rows", pairs)


def bits_of(count):
    return [1 << place for place in range(count.bit_length() - 1)]


def head_statistics(
    tile, cols, wait, inputs, key_weight, value_weight, queries, out_grad, keys, values, stats
):
    reads, latents, _ = queries.shape
    wait(0, 1)
    keys[...] = plain_dot(inputs[...], key_weight[:, cols]).astype(jnp.bfloat16)
    wait(2)
    values[...] = plain_dot(inputs[...], value_weight[:, cols]).astype(jnp.bfloat16)
    wait(3, 4)

    @pl.loop(0, latents // tile, unroll=True)
    def _(step):
        at = pl.ds(pl.multiple_of(step * tile, tile), tile)
        for read_index in range(reads):
            scores = last_contract(keys[...], queries[read_index, at, cols])
            scores = scores * (FACTOR * LOG2_E)
            weighted = last_contract(values[...], out_grad[read_index, at, cols])
            top = jnp.max(scores, axis=0, keepdims=True)
            expos = jnp.exp2(scores - top)
            total = jnp.sum(expos, axis=0, keepdims=True)
            accum = jnp.sum(expos * weighted, axis=0, keepdims=True)
            stats[read_index : read_index + 1, at] = top + jnp.log2(total)
            stats[reads + read_index : reads + read_index + 1, at] = accum / total


def first_kernel(tile, *refs):
    sources, results, targets, sems = refs[:5], refs[5:8], refs[8:13], refs[13]
    loads = []
    for index, (source, target) in enumerate(zip(sources, targets)):
        if index:
            source = source.at[..., :HD]
        loads.append(pltpu.make_async_copy(source, target, sems.at[index]))
    for load in loads:
        load.start()

    def wait(*places):
        for place in places:
            loads[place].wait()

    head_statistics(tile, slice(0, HD), wait, *targets, *results)


def later_kernel(tile, head_index, *refs):
    cols = slice(head_index * HD, (head_index + 1) * HD)
    head_statistics(tile, cols, lambda *_: None, *refs)


def merged(mine, theirs):
    reads = mine.shape[0] // 2
    own, other = mine[:reads], theirs[:reads]
    top = jnp.maximum(own, other)
    own_share = jnp.exp2(own - top)
    other_share = jnp.exp2(other - top)
    total = own_share + other_share
    delta = (mine[reads:] * own_share + theirs[reads:] * other_share) / total
    return top + jnp.log2(total), delta


def merge_kernel(mine, theirs, result):
    reads = mine.shape[0] // 2
    result[:reads], result[reads:] = merged(mine, theirs)


def group_at(bits, relative, high, me):
    flips = sum(bit * flip for bit, flip in zip(bits, relative))
    return counted((counted(me) % LAST_BIT ^ flips) + LAST_BIT * high)


LAST_BIT = 4
WEIGHT_PARTS = (((0, 256, (1, 2)),), ((0, 256, (1, 2)),))
QUERY_PARTS = (((0, 2, (2, 1, 4)),), ((0, 2, (1, 2, 4)),))
AFTER = {'w1.2': 'q0.1', 'i.0': 'w0.3'}


def grads_kernel(
    head_index, row_axis, low, after, inputs, keys, values, queries, out_grad, mine, theirs, *refs
):
    del after
    grads, score_grads = refs[:2]
    weight_parts = refs[2:-4]
    key_acc, value_acc, weights_ref, stats = refs[-4:]
    reads, latents, _ = queries.shape
    tile = latents // (GROUPS // 2)
    cols = slice(head_index * HD, (head_index + 1) * HD)
    stats[:reads], stats[reads:] = merged(mine, theirs)
    key_acc[...] = jnp.zeros_like(key_acc)
    value_acc[...] = jnp.zeros_like(value_acc)

    @pl.loop(0, latents // tile, unroll=True)
    def _(step):
        at = pl.ds(pl.multiple_of(step * tile, tile), tile)
        for read_index in range(reads):
            query_block = queries[read_index, at, cols]
            grad_block = out_grad[read_index, at, cols]
            scores = last_contract(keys[...], query_block) * (FACTOR * LOG2_E)
            weighted = last_contract(values[...], grad_block)
            probs = jnp.exp2(scores - stats[read_index : read_index + 1, at])
            delta = stats[reads + read_index : reads + read_index + 1, at]
            score_grad = (probs * (weighted - delta) * FACTOR).astype(jnp.bfloat16)
            score_grads[read_index, :, at] = score_grad
            key_acc[...] += plain_dot(score_grad, query_block)
            value_acc[...] += plain_dot(probs.astype(jnp.bfloat16), grad_block)

    grads[:, :HD] = key_acc[...].astype(jnp.bfloat16)
    grads[:, HD:] = value_acc[...].astype(jnp.bfloat16)
    weights_ref[...] = rows_contract(inputs[...], grads[...])
    features = inputs.shape[1]
    piece = features // GROUPS
    me = lax.axis_index(row_axis) // low
    for part, (begin, end, bits) in enumerate(WEIGHT_PARTS[head_index]):
        for first in range(2):
            ref = weight_parts[2 * part + first]
            for second in range(2):
                for high in range(2):
                    group = group_at(bits, (first, second), high, me)
                    start = pl.multiple_of(group * piece, piece)
                    ref[second, high] = weights_ref[pl.ds(start, piece), begin:end]


def input_kernel(head_axis, key_weight, value_weight, *refs):
    head_grads, (_, input_keep, input_send, total) = refs[:-4], refs[-4:]
    for head_index, grads in enumerate(head_grads):
        cols = slice(head_index * HD, (head_index + 1) * HD)
        part = last_contract(grads[:, :HD], key_weight[:, cols])
        part += last_contract(grads[:, HD:], value_weight[:, cols])
        total[...] = total[...] + part if head_index else part
    place = lax.axis_index(head_axis)
    shares = 2 * input_keep.shape[0]
    width = total.shape[1] // shares
    for relative in range(shares):
        ref = input_send if relative >= shares // 2 else input_keep
        start = pl.multiple_of((place ^ relative) * width, width)
        ref[relative % (shares // 2)] = total[:, pl.ds(start, width)]


def query_kernel(parts, row_axis, low, after, score_grads, keys, *refs):
    del after
    tile_ref = refs[-1]
    reads, _, latents = score_grads.shape
    piece = latents // GROUPS
    me = lax.axis_index(row_axis) // low
    side = lax.rem(me, 2)
    for part, (begin, end, bits) in enumerate(parts):
        for upper in range(GROUPS // 2):
            pair = counted(counted(me) ^ (2 * upper)) // 2
            at = pl.ds(pl.multiple_of(pair * 2 * piece, 2 * piece), 2 * piece)
            for read_index in range(begin, end):
                slot = upper * reads + read_index
                tile_ref[slot] = rows_contract(score_grads[read_index, :, at], keys[...])
                for flip in range(2):
                    half = pl.ds(pl.multiple_of((side ^ flip) * piece, piece), piece)
                    relative = 2 * upper + flip
                    ref = refs[2 * part + (1 if relative & bits[0] else 0)]
                    index = 2 * ((relative & bits[1]) // bits[1]) + (relative & bits[2]) // bits[2]
                    ref[index, read_index - begin] = tile_ref[slot, half, :]


def weights_kernel(weight_parts, row_axis, low, *refs):
    key_out, value_out, input_out, done = refs[-4:]
    refs = list(refs[:-4])
    input_out[...] = refs.pop(0)[0] + refs.pop(0)[0]
    done[...] = jnp.zeros_like(done)
    piece = key_out.shape[0] // GROUPS
    me = lax.axis_index(row_axis) // low
    for head_index, begin, end, bits in weight_parts:
        cols = slice(head_index * HD, (head_index + 1) * HD)
        for first in range(2):
            source = refs.pop(0)
            for second in range(2):
                for high in range(2):
                    group = group_at(bits, (first, second), high, me)
                    start = pl.multiple_of(group * piece, piece)
                    at = pl.ds(start, piece)
                    if begin == 0:
                        key_out[at, cols] = source[second, high, :, :HD]
                    if end == 2 * HD:
                        value_out[at, cols] = source[second, high, :, end - begin - HD :]


def queries_kernel(query_parts, after, *refs):
    del after
    query_out = refs[-1]
    refs = list(refs[:-1])
    for head_index, begin, end, terms in query_parts:
        cols = slice(head_index * HD, (head_index + 1) * HD)
        total = refs.pop(0)[0]
        for _ in range(terms - 1):
            total = total + refs.pop(0)[0]
        query_out[begin:end, :, cols] = total


def shape_of(shape, dtype=jnp.float32):
    return jax.ShapeDtypeStruct(shape, dtype)


def add_kernel(mine, theirs, after, total):
    del after
    total[...] = mine[...] + theirs[...]


def on_device(row_devices, head_devices, inputs, key_weight, value_weight, queries, out_grad):
    reads, latents, columns = queries.shape
    head_count = columns // HD
    row_count, features = inputs.shape
    low = row_devices // GROUPS
    tile = latents // (GROUPS // 2)
    piece = features // GROUPS
    operands = (inputs, key_weight, value_weight, queries, out_grad)
    block_work = pl.CostEstimate(
        flops=8 * reads * row_count * latents * HD,
        bytes_accessed=4 * 2**20,
        transcendentals=reads * row_count * latents,
    )

    projected = []
    for head_index in range(head_count):
        first = head_index == 0
        loaded = [
            pltpu.VMEM(item.shape[:-1] + ((HD,) if place else item.shape[-1:]), item.dtype)
            for place, item in enumerate(operands)
        ]
        projected.append(
            pl.pallas_call(
                functools.partial(first_kernel, tile)
                if first
                else functools.partial(later_kernel, tile, head_index),
                out_shape=(
                    shape_of((row_count, HD), jnp.bfloat16),
                    shape_of((row_count, HD), jnp.bfloat16),
                    shape_of((2 * reads, latents)),
                ),
                in_specs=[HBM if first else VMEM] * 5,
                out_specs=(VMEM,) * 3,
                scratch_shapes=loaded + [pltpu.SemaphoreType.DMA((5,))] if first else [],
                compiler_params=params(57 if first else 16),
                cost_estimate=block_work,
                name="project",
            )(*operands)
        )

    stats_parts = []
    for head_index in range(head_count):
        stats = projected[head_index][2]
        for bit in bits_of(row_devices)[:-1]:
            theirs = swap(stats, "rows", row_devices, bit)
            stats = pl.pallas_call(
                merge_kernel,
                out_shape=shape_of(stats.shape),
                in_specs=[VMEM] * 2,
                out_specs=VMEM,
                compiler_params=params(2),
                name="merge",
            )(stats, theirs)
        stats_parts.append((stats, swap(stats, "rows", row_devices, bits_of(row_devices)[-1])))

    order_low = (lax.axis_index("rows") % low) ^ jnp.arange(low, dtype=jnp.int32)
    low_bits = [bit for bit in bits_of(row_devices) if bit < low]

    def scatter_low(block, axis):
        if low == 1:
            return block
        parts = jnp.moveaxis(
            block.reshape(block.shape[:axis] + (low, -1) + block.shape[axis + 1 :]), axis, 0
        )
        parts = jnp.take(parts, order_low, axis=0)
        for bit in low_bits:
            parts = parts.reshape((-1, 2) + parts.shape[1:])
            parts = parts[:, 0] + swap(parts[:, 1], "rows", row_devices, bit)
        return parts[0]

    def sum_low(block):
        for bit in low_bits:
            block = block + row_swap(block, bit=bit)
        return block

    row_swap = functools.partial(row_swap_of, count=row_devices)

    def kernel_call(kernel, shapes, operands, scratch, limit, name):
        return pl.pallas_call(
            kernel,
            out_shape=[shape_of(*item) for item in shapes],
            in_specs=[ANY] + [VMEM] * (len(operands) - 1),
            out_specs=[VMEM] * len(shapes),
            scratch_shapes=scratch,
            compiler_params=params(limit),
            cost_estimate=block_work,
            name=name,
        )(*operands)

    grads_out, weight_steps, marks = [], [], {}
    for head_index in range(head_count):
        keys, values, _ = projected[head_index]
        results = kernel_call(
            functools.partial(grads_kernel, head_index, "rows", low),
            [((row_count, 2 * HD), jnp.bfloat16), ((reads, row_count, latents), jnp.bfloat16)]
            + [
                ((2, 2, piece, end - begin),)
                for begin, end, _ in WEIGHT_PARTS[head_index]
                for _ in range(2)
            ],
            [
                grads_out[-1][0] if grads_out else stats_parts[0][0],
                *(inputs, keys, values, queries, out_grad),
                *stats_parts[head_index],
            ],
            [
                pltpu.VMEM((row_count, HD), jnp.float32),
                pltpu.VMEM((row_count, HD), jnp.float32),
                pltpu.VMEM((features, 2 * HD), jnp.float32),
                pltpu.VMEM((2 * reads, latents), jnp.float32),
            ],
            20,
            "grads",
        )
        grads_out.append(results)
        marks[f"A{head_index}"] = results[0]
        for part, (begin, end, bits) in enumerate(WEIGHT_PARTS[head_index]):
            keep, send = results[2 + 2 * part : 4 + 2 * part]
            theirs = row_swap(send, bit=bits[0] * low)
            send = keep[1:] + theirs[1:]
            mine = keep[:1] + theirs[:1]
            marks[f"w{head_index}.1"] = send
            weight_steps.append((mine, row_swap(send, bit=bits[1] * low)))

    query_terms, query_list = [], []
    for head_index in range(head_count):
        results = kernel_call(
            functools.partial(query_kernel, QUERY_PARTS[head_index], "rows", low),
            [
                ((GROUPS // 2, end - begin, latents // GROUPS, HD),)
                for begin, end, _ in QUERY_PARTS[head_index]
                for _ in range(2)
            ],
            [
                marks[AFTER.get(f"B{head_index}", f"A{head_index}")],
                grads_out[head_index][1],
                projected[head_index][0],
            ],
            [pltpu.VMEM((GROUPS // 2 * reads, tile, HD), jnp.float32)],
            16,
            "query",
        )
        marks[f"B{head_index}"] = results[0]
        for part, (begin, end, bits) in enumerate(QUERY_PARTS[head_index]):
            keep, send = results[2 * part : 2 * part + 2]
            for place, bit in enumerate(bits):
                theirs = row_swap(send, bit=bit * low)
                if place + 1 < len(bits):
                    middle = keep.shape[0] // 2
                    send = keep[middle:] + theirs[middle:]
                    keep = keep[:middle] + theirs[:middle]
                    marks[f"q{head_index}.{place + 1}"] = send
            terms = [keep, theirs]
            if low > 1:
                terms = [scatter_low((keep + theirs)[0], 1)[None]]
            query_terms += terms
            query_list.append((head_index, begin, end, len(terms)))

    def added(kernel, shape, mine, theirs, after):
        return pl.pallas_call(
            kernel,
            out_shape=shape_of(shape),
            in_specs=[VMEM, VMEM, ANY],
            out_specs=VMEM,
            compiler_params=params(4),
            cost_estimate=pl.CostEstimate(flops=1024, bytes_accessed=1024, transcendentals=0),
            name="added",
        )(mine, theirs, after)

    weight_terms, weight_list = [], []
    for head_index in range(head_count):
        for begin, end, bits in WEIGHT_PARTS[head_index]:
            mine, theirs = weight_steps.pop(0)
            first, second = (bit * low for bit in bits)
            for place, bit in ((2, LAST_BIT * low), (3, second)):
                after = AFTER.get(f"w{head_index}.{place}")
                if after:
                    mine = added(add_kernel, mine.shape, mine, theirs, marks[after])
                else:
                    mine = mine + theirs
                if place == 3:
                    mine = sum_low(mine)
                theirs = row_swap(mine, bit=bit)
                marks[f"w{head_index}.{place}"] = mine
            near = jnp.concatenate([mine, theirs], axis=0)
            weight_terms += [near, row_swap(near, bit=first)]
            weight_list.append((head_index, begin, end, bits))

    share = ((head_devices // 2, row_count, features // head_devices),)
    after = marks[AFTER.get("i.0", "B1")]
    input_keep, input_send = pl.pallas_call(
        functools.partial(input_kernel, "heads"),
        out_shape=[shape_of(*share)] * 2,
        in_specs=[VMEM] * (2 + head_count) + [ANY],
        out_specs=[VMEM] * 2,
        scratch_shapes=[pltpu.VMEM((row_count, features), jnp.float32)],
        compiler_params=params(16),
        cost_estimate=block_work,
        name="input",
    )(key_weight, value_weight, *(item[0] for item in grads_out), after)
    head_bits = bits_of(head_devices)[::-1]
    keep, theirs = input_keep, swap(input_send, "heads", head_devices, head_bits[0])
    for bit in head_bits[1:]:
        send = keep[bit:] + theirs[bit:]
        keep, theirs = keep[:bit] + theirs[:bit], swap(send, "heads", head_devices, bit)
    input_terms = (keep, theirs)

    key_weight_grad, value_weight_grad, input_grad, done = pl.pallas_call(
        functools.partial(weights_kernel, weight_list, "rows", low),
        out_shape=(shape_of((features, columns)),) * 2
        + (shape_of((row_count, features // head_devices)), shape_of((8, 128))),
        in_specs=[VMEM] * (2 + len(weight_terms)),
        out_specs=(VMEM,) * 4,
        compiler_params=params(8),
        name="weights",
    )(*input_terms, *weight_terms)
    query_grad = pl.pallas_call(
        functools.partial(queries_kernel, query_list),
        out_shape=shape_of((reads, latents // row_devices, columns)),
        in_specs=[ANY] + [VMEM] * len(query_terms),
        out_specs=VMEM,
        compiler_params=params(4),
        name="queries",
    )(done, *query_terms)
    return (query_grad, key_weight_grad, value_weight_grad, input_grad)


def solution(mesh):
    in_specs = (
        P("rows", None),
        P(None, "heads"),
        P(None, "heads"),
        P(None, None, "heads"),
        P(None, None, "heads"),
    )
    out_specs = (P(None, "rows", "heads"), P(None, "heads"), P(None, "heads"), P("rows", "heads"))

    def body(*args):
        return on_device(mesh.shape["rows"], mesh.shape["heads"], *args)

    return jax.shard_map(body, mesh=mesh, in_specs=in_specs, out_specs=out_specs, check_vma=False)
```

```python
import functools

import jax
import jax.numpy as jnp
from jax import lax
from jax.experimental import pallas as pl
from jax.experimental.pallas import tpu as pltpu
from jax.sharding import PartitionSpec as P

HD = 128
GROUPS = 8
FACTOR = HD ** (-0.5)
LOG2_E = 1.4426950408889634
VMEM = pl.BlockSpec(memory_space=pltpu.VMEM)
HBM = pl.BlockSpec(memory_space=pltpu.HBM)
ANY = pl.BlockSpec(memory_space=pl.ANY)


def params(mebibytes):
    return pltpu.CompilerParams(vmem_limit_bytes=mebibytes * 1024 * 1024)


def last_contract(left, right):
    return lax.dot_general(
        left, right, (((1,), (1,)), ((), ())), preferred_element_type=jnp.float32
    )


def rows_contract(left, right):
    return lax.dot_general(
        left, right, (((0,), (0,)), ((), ())), preferred_element_type=jnp.float32
    )


def plain_dot(left, right):
    return jnp.dot(left, right, preferred_element_type=jnp.float32)


def swap(array, axis, count, bit):
    pairs = [(device, device ^ bit) for device in range(count)]
    return lax.ppermute(array, axis, pairs)


def counted(group):
    return group ^ ((group // 4) % 2 * 2)


def row_swap_of(array, count, bit):
    low = count // GROUPS
    if bit < low:
        return swap(array, "rows", count, bit)
    pairs = []
    for device in range(count):
        partner = counted(counted(device // low) ^ (bit // low))
        pairs.append((device, partner * low + device % low))
    return lax.ppermute(array, "rows", pairs)


def bits_of(count):
    return [1 << place for place in range(count.bit_length() - 1)]


def head_statistics(
    tile, cols, wait, inputs, key_weight, value_weight, queries, out_grad, keys, values, stats
):
    reads, latents, _ = queries.shape
    wait(0, 1)
    keys[...] = plain_dot(inputs[...], key_weight[:, cols]).astype(jnp.bfloat16)
    wait(2)
    values[...] = plain_dot(inputs[...], value_weight[:, cols]).astype(jnp.bfloat16)
    wait(3, 4)

    @pl.loop(0, latents // tile, unroll=True)
    def _(step):
        at = pl.ds(pl.multiple_of(step * tile, tile), tile)
        for read_index in range(reads):
            scores = last_contract(keys[...], queries[read_index, at, cols])
            scores = scores * (FACTOR * LOG2_E)
            weighted = last_contract(values[...], out_grad[read_index, at, cols])
            top = jnp.max(scores, axis=0, keepdims=True)
            expos = jnp.exp2(scores - top)
            total = jnp.sum(expos, axis=0, keepdims=True)
            accum = jnp.sum(expos * weighted, axis=0, keepdims=True)
            stats[read_index : read_index + 1, at] = top + jnp.log2(total)
            stats[reads + read_index : reads + read_index + 1, at] = accum / total


def first_kernel(tile, *refs):
    sources, results, targets, sems = refs[:5], refs[5:8], refs[8:13], refs[13]
    loads = []
    for index, (source, target) in enumerate(zip(sources, targets)):
        if index:
            source = source.at[..., :HD]
        loads.append(pltpu.make_async_copy(source, target, sems.at[index]))
    for load in loads:
        load.start()

    def wait(*places):
        for place in places:
            loads[place].wait()

    head_statistics(tile, slice(0, HD), wait, *targets, *results)


def later_kernel(tile, head_index, *refs):
    cols = slice(head_index * HD, (head_index + 1) * HD)
    head_statistics(tile, cols, lambda *_: None, *refs)


def merged(mine, theirs):
    reads = mine.shape[0] // 2
    own, other = mine[:reads], theirs[:reads]
    top = jnp.maximum(own, other)
    own_share = jnp.exp2(own - top)
    other_share = jnp.exp2(other - top)
    total = own_share + other_share
    delta = (mine[reads:] * own_share + theirs[reads:] * other_share) / total
    return top + jnp.log2(total), delta


def merge_kernel(mine, theirs, result):
    reads = mine.shape[0] // 2
    result[:reads], result[reads:] = merged(mine, theirs)


def group_at(bits, relative, high, me):
    flips = sum(bit * flip for bit, flip in zip(bits, relative))
    return counted((counted(me) % LAST_BIT ^ flips) + LAST_BIT * high)


LAST_BIT = 4
WEIGHT_PARTS = (((0, 256, (1, 2)),), ((0, 256, (1, 2)),))
QUERY_PARTS = (((0, 2, (2, 1, 4)),), ((0, 2, (1, 2, 4)),))
AFTER = {'w1.2': 'q0.1', 'i.0': 'w0.3'}


def grads_kernel(
    head_index, row_axis, low, after, inputs, keys, values, queries, out_grad, mine, theirs, *refs
):
    del after
    grads, score_grads = refs[:2]
    weight_parts = refs[2:-4]
    key_acc, value_acc, weights_ref, stats = refs[-4:]
    reads, latents, _ = queries.shape
    tile = latents // (GROUPS // 2)
    cols = slice(head_index * HD, (head_index + 1) * HD)
    stats[:reads], stats[reads:] = merged(mine, theirs)
    key_acc[...] = jnp.zeros_like(key_acc)
    value_acc[...] = jnp.zeros_like(value_acc)

    @pl.loop(0, latents // tile, unroll=True)
    def _(step):
        at = pl.ds(pl.multiple_of(step * tile, tile), tile)
        for read_index in range(reads):
            query_block = queries[read_index, at, cols]
            grad_block = out_grad[read_index, at, cols]
            scores = last_contract(keys[...], query_block) * (FACTOR * LOG2_E)
            weighted = last_contract(values[...], grad_block)
            probs = jnp.exp2(scores - stats[read_index : read_index + 1, at])
            delta = stats[reads + read_index : reads + read_index + 1, at]
            score_grad = (probs * (weighted - delta) * FACTOR).astype(jnp.bfloat16)
            score_grads[read_index, :, at] = score_grad
            key_acc[...] += plain_dot(score_grad, query_block)
            value_acc[...] += plain_dot(probs.astype(jnp.bfloat16), grad_block)

    grads[:, :HD] = key_acc[...].astype(jnp.bfloat16)
    grads[:, HD:] = value_acc[...].astype(jnp.bfloat16)
    weights_ref[...] = rows_contract(inputs[...], grads[...])
    features = inputs.shape[1]
    piece = features // GROUPS
    me = lax.axis_index(row_axis) // low
    for part, (begin, end, bits) in enumerate(WEIGHT_PARTS[head_index]):
        for first in range(2):
            ref = weight_parts[2 * part + first]
            for second in range(2):
                for high in range(2):
                    group = group_at(bits, (first, second), high, me)
                    start = pl.multiple_of(group * piece, piece)
                    ref[second, high] = weights_ref[pl.ds(start, piece), begin:end]


def input_kernel(head_axis, key_weight, value_weight, *refs):
    head_grads, (_, input_keep, input_send, total) = refs[:-4], refs[-4:]
    for head_index, grads in enumerate(head_grads):
        cols = slice(head_index * HD, (head_index + 1) * HD)
        part = last_contract(grads[:, :HD], key_weight[:, cols])
        part += last_contract(grads[:, HD:], value_weight[:, cols])
        total[...] = total[...] + part if head_index else part
    place = lax.axis_index(head_axis)
    shares = 2 * input_keep.shape[0]
    width = total.shape[1] // shares
    for relative in range(shares):
        ref = input_send if relative >= shares // 2 else input_keep
        start = pl.multiple_of((place ^ relative) * width, width)
        ref[relative % (shares // 2)] = total[:, pl.ds(start, width)]


def query_kernel(parts, row_axis, low, after, score_grads, keys, *refs):
    del after
    tile_ref = refs[-1]
    reads, _, latents = score_grads.shape
    piece = latents // GROUPS
    me = lax.axis_index(row_axis) // low
    side = lax.rem(me, 2)
    for part, (begin, end, bits) in enumerate(parts):
        for upper in range(GROUPS // 2):
            pair = (me // 2) ^ upper
            at = pl.ds(pl.multiple_of(pair * 2 * piece, 2 * piece), 2 * piece)
            for read_index in range(begin, end):
                slot = upper * reads + read_index
                tile_ref[slot] = rows_contract(score_grads[read_index, :, at], keys[...])
                for flip in range(2):
                    half = pl.ds(pl.multiple_of((side ^ flip) * piece, piece), piece)
                    relative = 2 * upper + flip
                    ref = refs[2 * part + (1 if relative & bits[0] else 0)]
                    index = 2 * ((relative & bits[1]) // bits[1]) + (relative & bits[2]) // bits[2]
                    ref[index, read_index - begin] = tile_ref[slot, half, :]


def weights_kernel(weight_parts, row_axis, low, *refs):
    key_out, value_out, input_out, done = refs[-4:]
    refs = list(refs[:-4])
    input_out[...] = refs.pop(0)[0] + refs.pop(0)[0]
    done[...] = jnp.zeros_like(done)
    piece = key_out.shape[0] // GROUPS
    me = lax.axis_index(row_axis) // low
    for head_index, begin, end, bits in weight_parts:
        cols = slice(head_index * HD, (head_index + 1) * HD)
        for first in range(2):
            source = refs.pop(0)
            for second in range(2):
                for high in range(2):
                    group = group_at(bits, (first, second), high, me)
                    start = pl.multiple_of(group * piece, piece)
                    at = pl.ds(start, piece)
                    if begin == 0:
                        key_out[at, cols] = source[second, high, :, :HD]
                    if end == 2 * HD:
                        value_out[at, cols] = source[second, high, :, end - begin - HD :]


def queries_kernel(query_parts, after, *refs):
    del after
    query_out = refs[-1]
    refs = list(refs[:-1])
    for head_index, begin, end, terms in query_parts:
        cols = slice(head_index * HD, (head_index + 1) * HD)
        total = refs.pop(0)[0]
        for _ in range(terms - 1):
            total = total + refs.pop(0)[0]
        query_out[begin:end, :, cols] = total


def shape_of(shape, dtype=jnp.float32):
    return jax.ShapeDtypeStruct(shape, dtype)


def add_kernel(mine, theirs, after, total):
    del after
    total[...] = mine[...] + theirs[...]


def on_device(row_devices, head_devices, inputs, key_weight, value_weight, queries, out_grad):
    reads, latents, columns = queries.shape
    head_count = columns // HD
    row_count, features = inputs.shape
    low = row_devices // GROUPS
    tile = latents // (GROUPS // 2)
    piece = features // GROUPS
    operands = (inputs, key_weight, value_weight, queries, out_grad)
    block_work = pl.CostEstimate(
        flops=8 * reads * row_count * latents * HD,
        bytes_accessed=4 * 2**20,
        transcendentals=reads * row_count * latents,
    )

    projected = []
    for head_index in range(head_count):
        first = head_index == 0
        loaded = [
            pltpu.VMEM(item.shape[:-1] + ((HD,) if place else item.shape[-1:]), item.dtype)
            for place, item in enumerate(operands)
        ]
        projected.append(
            pl.pallas_call(
                functools.partial(first_kernel, tile)
                if first
                else functools.partial(later_kernel, tile, head_index),
                out_shape=(
                    shape_of((row_count, HD), jnp.bfloat16),
                    shape_of((row_count, HD), jnp.bfloat16),
                    shape_of((2 * reads, latents)),
                ),
                in_specs=[HBM if first else VMEM] * 5,
                out_specs=(VMEM,) * 3,
                scratch_shapes=loaded + [pltpu.SemaphoreType.DMA((5,))] if first else [],
                compiler_params=params(57 if first else 16),
                cost_estimate=block_work,
                name="project",
            )(*operands)
        )

    stats_parts = []
    for head_index in range(head_count):
        stats = projected[head_index][2]
        for bit in bits_of(row_devices)[:-1]:
            theirs = swap(stats, "rows", row_devices, bit)
            stats = pl.pallas_call(
                merge_kernel,
                out_shape=shape_of(stats.shape),
                in_specs=[VMEM] * 2,
                out_specs=VMEM,
                compiler_params=params(2),
                name="merge",
            )(stats, theirs)
        stats_parts.append((stats, swap(stats, "rows", row_devices, bits_of(row_devices)[-1])))

    order_low = (lax.axis_index("rows") % low) ^ jnp.arange(low, dtype=jnp.int32)
    low_bits = [bit for bit in bits_of(row_devices) if bit < low]

    def scatter_low(block, axis):
        if low == 1:
            return block
        parts = jnp.moveaxis(
            block.reshape(block.shape[:axis] + (low, -1) + block.shape[axis + 1 :]), axis, 0
        )
        parts = jnp.take(parts, order_low, axis=0)
        for bit in low_bits:
            parts = parts.reshape((-1, 2) + parts.shape[1:])
            parts = parts[:, 0] + swap(parts[:, 1], "rows", row_devices, bit)
        return parts[0]

    def sum_low(block):
        for bit in low_bits:
            block = block + row_swap(block, bit=bit)
        return block

    row_swap = functools.partial(row_swap_of, count=row_devices)

    def kernel_call(kernel, shapes, operands, scratch, limit, name):
        return pl.pallas_call(
            kernel,
            out_shape=[shape_of(*item) for item in shapes],
            in_specs=[ANY] + [VMEM] * (len(operands) - 1),
            out_specs=[VMEM] * len(shapes),
            scratch_shapes=scratch,
            compiler_params=params(limit),
            cost_estimate=block_work,
            name=name,
        )(*operands)

    grads_out, weight_steps, marks = [], [], {}
    for head_index in range(head_count):
        keys, values, _ = projected[head_index]
        results = kernel_call(
            functools.partial(grads_kernel, head_index, "rows", low),
            [((row_count, 2 * HD), jnp.bfloat16), ((reads, row_count, latents), jnp.bfloat16)]
            + [
                ((2, 2, piece, end - begin),)
                for begin, end, _ in WEIGHT_PARTS[head_index]
                for _ in range(2)
            ],
            [
                grads_out[-1][0] if grads_out else stats_parts[0][0],
                *(inputs, keys, values, queries, out_grad),
                *stats_parts[head_index],
            ],
            [
                pltpu.VMEM((row_count, HD), jnp.float32),
                pltpu.VMEM((row_count, HD), jnp.float32),
                pltpu.VMEM((features, 2 * HD), jnp.float32),
                pltpu.VMEM((2 * reads, latents), jnp.float32),
            ],
            20,
            "grads",
        )
        grads_out.append(results)
        marks[f"A{head_index}"] = results[0]
        for part, (begin, end, bits) in enumerate(WEIGHT_PARTS[head_index]):
            keep, send = results[2 + 2 * part : 4 + 2 * part]
            theirs = row_swap(send, bit=bits[0] * low)
            send = keep[1:] + theirs[1:]
            mine = keep[:1] + theirs[:1]
            marks[f"w{head_index}.1"] = send
            weight_steps.append((mine, row_swap(send, bit=bits[1] * low)))

    query_terms, query_list = [], []
    for head_index in range(head_count):
        results = kernel_call(
            functools.partial(query_kernel, QUERY_PARTS[head_index], "rows", low),
            [
                ((GROUPS // 2, end - begin, latents // GROUPS, HD),)
                for begin, end, _ in QUERY_PARTS[head_index]
                for _ in range(2)
            ],
            [
                marks[AFTER.get(f"B{head_index}", f"A{head_index}")],
                grads_out[head_index][1],
                projected[head_index][0],
            ],
            [pltpu.VMEM((GROUPS // 2 * reads, tile, HD), jnp.float32)],
            16,
            "query",
        )
        marks[f"B{head_index}"] = results[0]
        for part, (begin, end, bits) in enumerate(QUERY_PARTS[head_index]):
            keep, send = results[2 * part : 2 * part + 2]
            for place, bit in enumerate(bits):
                theirs = swap(send, "rows", row_devices, bit * low)
                if place + 1 < len(bits):
                    middle = keep.shape[0] // 2
                    send = keep[middle:] + theirs[middle:]
                    keep = keep[:middle] + theirs[:middle]
                    marks[f"q{head_index}.{place + 1}"] = send
            terms = [keep, theirs]
            if low > 1:
                terms = [scatter_low((keep + theirs)[0], 1)[None]]
            query_terms += terms
            query_list.append((head_index, begin, end, len(terms)))

    def added(kernel, shape, mine, theirs, after):
        return pl.pallas_call(
            kernel,
            out_shape=shape_of(shape),
            in_specs=[VMEM, VMEM, ANY],
            out_specs=VMEM,
            compiler_params=params(4),
            cost_estimate=pl.CostEstimate(flops=1024, bytes_accessed=1024, transcendentals=0),
            name="added",
        )(mine, theirs, after)

    weight_terms, weight_list = [], []
    for head_index in range(head_count):
        for begin, end, bits in WEIGHT_PARTS[head_index]:
            mine, theirs = weight_steps.pop(0)
            first, second = (bit * low for bit in bits)
            for place, bit in ((2, LAST_BIT * low), (3, second)):
                after = AFTER.get(f"w{head_index}.{place}")
                if after:
                    mine = added(add_kernel, mine.shape, mine, theirs, marks[after])
                else:
                    mine = mine + theirs
                if place == 3:
                    mine = sum_low(mine)
                theirs = row_swap(mine, bit=bit)
                marks[f"w{head_index}.{place}"] = mine
            near = jnp.concatenate([mine, theirs], axis=0)
            weight_terms += [near, row_swap(near, bit=first)]
            weight_list.append((head_index, begin, end, bits))

    share = ((head_devices // 2, row_count, features // head_devices),)
    after = marks[AFTER.get("i.0", "B1")]
    input_keep, input_send = pl.pallas_call(
        functools.partial(input_kernel, "heads"),
        out_shape=[shape_of(*share)] * 2,
        in_specs=[VMEM] * (2 + head_count) + [ANY],
        out_specs=[VMEM] * 2,
        scratch_shapes=[pltpu.VMEM((row_count, features), jnp.float32)],
        compiler_params=params(16),
        cost_estimate=block_work,
        name="input",
    )(key_weight, value_weight, *(item[0] for item in grads_out), after)
    head_bits = bits_of(head_devices)[::-1]
    keep, theirs = input_keep, swap(input_send, "heads", head_devices, head_bits[0])
    for bit in head_bits[1:]:
        send = keep[bit:] + theirs[bit:]
        keep, theirs = keep[:bit] + theirs[:bit], swap(send, "heads", head_devices, bit)
    input_terms = (keep, theirs)

    key_weight_grad, value_weight_grad, input_grad, done = pl.pallas_call(
        functools.partial(weights_kernel, weight_list, "rows", low),
        out_shape=(shape_of((features, columns)),) * 2
        + (shape_of((row_count, features // head_devices)), shape_of((8, 128))),
        in_specs=[VMEM] * (2 + len(weight_terms)),
        out_specs=(VMEM,) * 4,
        compiler_params=params(8),
        name="weights",
    )(*input_terms, *weight_terms)
    query_grad = pl.pallas_call(
        functools.partial(queries_kernel, query_list),
        out_shape=shape_of((reads, latents // row_devices, columns)),
        in_specs=[ANY] + [VMEM] * len(query_terms),
        out_specs=VMEM,
        compiler_params=params(4),
        name="queries",
    )(done, *query_terms)
    return (query_grad, key_weight_grad, value_weight_grad, input_grad)


def solution(mesh):
    in_specs = (
        P("rows", None),
        P(None, "heads"),
        P(None, "heads"),
        P(None, None, "heads"),
        P(None, None, "heads"),
    )
    out_specs = (P(None, "rows", "heads"), P(None, "heads"), P(None, "heads"), P("rows", "heads"))

    def body(*args):
        return on_device(mesh.shape["rows"], mesh.shape["heads"], *args)

    return jax.shard_map(body, mesh=mesh, in_specs=in_specs, out_specs=out_specs, check_vma=False)
```

```python
import functools

import jax
import jax.numpy as jnp
from jax import lax
from jax.experimental import pallas as pl
from jax.experimental.pallas import tpu as pltpu
from jax.sharding import PartitionSpec as P

HD = 128
GROUPS = 8
FACTOR = HD ** (-0.5)
LOG2_E = 1.4426950408889634
VMEM = pl.BlockSpec(memory_space=pltpu.VMEM)
HBM = pl.BlockSpec(memory_space=pltpu.HBM)
ANY = pl.BlockSpec(memory_space=pl.ANY)


def params(mebibytes):
    return pltpu.CompilerParams(vmem_limit_bytes=mebibytes * 1024 * 1024)


def last_contract(left, right):
    return lax.dot_general(
        left, right, (((1,), (1,)), ((), ())), preferred_element_type=jnp.float32
    )


def rows_contract(left, right):
    return lax.dot_general(
        left, right, (((0,), (0,)), ((), ())), preferred_element_type=jnp.float32
    )


def plain_dot(left, right):
    return jnp.dot(left, right, preferred_element_type=jnp.float32)


def swap(array, axis, count, bit):
    pairs = [(device, device ^ bit) for device in range(count)]
    return lax.ppermute(array, axis, pairs)


def counted(group):
    return group ^ ((group // 4) % 2 * 2)


def row_swap_of(array, count, bit):
    low = count // GROUPS
    if bit < low:
        return swap(array, "rows", count, bit)
    pairs = []
    for device in range(count):
        partner = counted(counted(device // low) ^ (bit // low))
        pairs.append((device, partner * low + device % low))
    return lax.ppermute(array, "rows", pairs)


def bits_of(count):
    return [1 << place for place in range(count.bit_length() - 1)]


def head_statistics(
    tile, cols, wait, inputs, key_weight, value_weight, queries, out_grad, keys, values, stats
):
    reads, latents, _ = queries.shape
    wait(0, 1)
    keys[...] = plain_dot(inputs[...], key_weight[:, cols]).astype(jnp.bfloat16)
    wait(2)
    values[...] = plain_dot(inputs[...], value_weight[:, cols]).astype(jnp.bfloat16)
    wait(3, 4)

    @pl.loop(0, latents // tile, unroll=True)
    def _(step):
        at = pl.ds(pl.multiple_of(step * tile, tile), tile)
        for read_index in range(reads):
            scores = last_contract(keys[...], queries[read_index, at, cols])
            scores = scores * (FACTOR * LOG2_E)
            weighted = last_contract(values[...], out_grad[read_index, at, cols])
            top = jnp.max(scores, axis=0, keepdims=True)
            expos = jnp.exp2(scores - top)
            total = jnp.sum(expos, axis=0, keepdims=True)
            accum = jnp.sum(expos * weighted, axis=0, keepdims=True)
            stats[read_index : read_index + 1, at] = top + jnp.log2(total)
            stats[reads + read_index : reads + read_index + 1, at] = accum / total


def first_kernel(tile, *refs):
    sources, results, targets, sems = refs[:5], refs[5:8], refs[8:13], refs[13]
    loads = []
    for index, (source, target) in enumerate(zip(sources, targets)):
        if index:
            source = source.at[..., :HD]
        loads.append(pltpu.make_async_copy(source, target, sems.at[index]))
    for load in loads:
        load.start()

    def wait(*places):
        for place in places:
            loads[place].wait()

    head_statistics(tile, slice(0, HD), wait, *targets, *results)


def later_kernel(tile, head_index, *refs):
    cols = slice(head_index * HD, (head_index + 1) * HD)
    head_statistics(tile, cols, lambda *_: None, *refs)


def merged(mine, theirs):
    reads = mine.shape[0] // 2
    own, other = mine[:reads], theirs[:reads]
    top = jnp.maximum(own, other)
    own_share = jnp.exp2(own - top)
    other_share = jnp.exp2(other - top)
    total = own_share + other_share
    delta = (mine[reads:] * own_share + theirs[reads:] * other_share) / total
    return top + jnp.log2(total), delta


def merge_kernel(mine, theirs, after, result):
    del after
    reads = mine.shape[0] // 2
    result[:reads], result[reads:] = merged(mine, theirs)


def group_at(bits, relative, high, me):
    flips = sum(bit * flip for bit, flip in zip(bits, relative))
    return counted((counted(me) % LAST_BIT ^ flips) + LAST_BIT * high)


LAST_BIT = 4
WEIGHT_PARTS = (((0, 256, (1, 2)),), ((0, 256, (1, 2)),))
QUERY_PARTS = (((0, 2, (2, 1, 4)),), ((0, 2, (1, 2, 4)),))
AFTER = {'w1.3': 'q1.1'}
CHAIN = ()


def grads_kernel(
    head_index, row_axis, low, after, inputs, keys, values, queries, out_grad, mine, theirs, *refs
):
    del after
    grads, score_grads = refs[:2]
    weight_parts = refs[2:-4]
    key_acc, value_acc, weights_ref, stats = refs[-4:]
    reads, latents, _ = queries.shape
    tile = latents // (GROUPS // 2)
    cols = slice(head_index * HD, (head_index + 1) * HD)
    stats[:reads], stats[reads:] = merged(mine, theirs)
    key_acc[...] = jnp.zeros_like(key_acc)
    value_acc[...] = jnp.zeros_like(value_acc)

    @pl.loop(0, latents // tile, unroll=True)
    def _(step):
        at = pl.ds(pl.multiple_of(step * tile, tile), tile)
        for read_index in range(reads):
            query_block = queries[read_index, at, cols]
            grad_block = out_grad[read_index, at, cols]
            scores = last_contract(keys[...], query_block) * (FACTOR * LOG2_E)
            weighted = last_contract(values[...], grad_block)
            probs = jnp.exp2(scores - stats[read_index : read_index + 1, at])
            delta = stats[reads + read_index : reads + read_index + 1, at]
            score_grad = (probs * (weighted - delta) * FACTOR).astype(jnp.bfloat16)
            score_grads[read_index, :, at] = score_grad
            key_acc[...] += plain_dot(score_grad, query_block)
            value_acc[...] += plain_dot(probs.astype(jnp.bfloat16), grad_block)

    grads[:, :HD] = key_acc[...].astype(jnp.bfloat16)
    grads[:, HD:] = value_acc[...].astype(jnp.bfloat16)
    weights_ref[...] = rows_contract(inputs[...], grads[...])
    features = inputs.shape[1]
    piece = features // GROUPS
    me = lax.axis_index(row_axis) // low
    for part, (begin, end, bits) in enumerate(WEIGHT_PARTS[head_index]):
        for first in range(2):
            ref = weight_parts[2 * part + first]
            for second in range(2):
                for high in range(2):
                    group = group_at(bits, (first, second), high, me)
                    start = pl.multiple_of(group * piece, piece)
                    ref[second, high] = weights_ref[pl.ds(start, piece), begin:end]


def input_kernel(head_axis, key_weight, value_weight, *refs):
    head_grads, (_, input_keep, input_send, total) = refs[:-4], refs[-4:]
    for head_index, grads in enumerate(head_grads):
        cols = slice(head_index * HD, (head_index + 1) * HD)
        part = last_contract(grads[:, :HD], key_weight[:, cols])
        part += last_contract(grads[:, HD:], value_weight[:, cols])
        total[...] = total[...] + part if head_index else part
    place = lax.axis_index(head_axis)
    shares = 2 * input_keep.shape[0]
    width = total.shape[1] // shares
    for relative in range(shares):
        ref = input_send if relative >= shares // 2 else input_keep
        start = pl.multiple_of((place ^ relative) * width, width)
        ref[relative % (shares // 2)] = total[:, pl.ds(start, width)]


def query_kernel(parts, row_axis, low, after, score_grads, keys, *refs):
    del after
    tile_ref = refs[-1]
    reads, _, latents = score_grads.shape
    piece = latents // GROUPS
    me = lax.axis_index(row_axis) // low
    side = lax.rem(me, 2)
    for part, (begin, end, bits) in enumerate(parts):
        for upper in range(GROUPS // 2):
            pair = counted(counted(me) ^ (2 * upper)) // 2
            at = pl.ds(pl.multiple_of(pair * 2 * piece, 2 * piece), 2 * piece)
            for read_index in range(begin, end):
                slot = upper * reads + read_index
                tile_ref[slot] = rows_contract(score_grads[read_index, :, at], keys[...])
                for flip in range(2):
                    half = pl.ds(pl.multiple_of((side ^ flip) * piece, piece), piece)
                    relative = 2 * upper + flip
                    ref = refs[2 * part + (1 if relative & bits[0] else 0)]
                    index = 2 * ((relative & bits[1]) // bits[1]) + (relative & bits[2]) // bits[2]
                    ref[index, read_index - begin] = tile_ref[slot, half, :]


def weights_kernel(weight_parts, row_axis, low, *refs):
    key_out, value_out, input_out, done = refs[-4:]
    refs = list(refs[:-4])
    input_out[...] = refs.pop(0)[0] + refs.pop(0)[0]
    done[...] = jnp.zeros_like(done)
    piece = key_out.shape[0] // GROUPS
    me = lax.axis_index(row_axis) // low
    for head_index, begin, end, bits in weight_parts:
        cols = slice(head_index * HD, (head_index + 1) * HD)
        for first in range(2):
            source = refs.pop(0)
            for second in range(2):
                for high in range(2):
                    group = group_at(bits, (first, second), high, me)
                    start = pl.multiple_of(group * piece, piece)
                    at = pl.ds(start, piece)
                    if begin == 0:
                        key_out[at, cols] = source[second, high, :, :HD]
                    if end == 2 * HD:
                        value_out[at, cols] = source[second, high, :, end - begin - HD :]


def queries_kernel(query_parts, after, *refs):
    del after
    query_out = refs[-1]
    refs = list(refs[:-1])
    for head_index, begin, end, terms in query_parts:
        cols = slice(head_index * HD, (head_index + 1) * HD)
        total = refs.pop(0)[0]
        for _ in range(terms - 1):
            total = total + refs.pop(0)[0]
        query_out[begin:end, :, cols] = total


def shape_of(shape, dtype=jnp.float32):
    return jax.ShapeDtypeStruct(shape, dtype)


def split_kernel(keep, theirs, after, stays, goes):
    del after
    stays[...] = keep[:1] + theirs[:1]
    goes[...] = keep[1:] + theirs[1:]


def add_kernel(mine, theirs, after, total):
    del after
    total[...] = mine[...] + theirs[...]


def on_device(row_devices, head_devices, inputs, key_weight, value_weight, queries, out_grad):
    reads, latents, columns = queries.shape
    head_count = columns // HD
    row_count, features = inputs.shape
    low = row_devices // GROUPS
    tile = latents // (GROUPS // 2)
    piece = features // GROUPS
    operands = (inputs, key_weight, value_weight, queries, out_grad)
    block_work = pl.CostEstimate(
        flops=8 * reads * row_count * latents * HD,
        bytes_accessed=4 * 2**20,
        transcendentals=reads * row_count * latents,
    )

    projected = []
    for head_index in range(head_count):
        first = head_index == 0
        loaded = [
            pltpu.VMEM(item.shape[:-1] + ((HD,) if place else item.shape[-1:]), item.dtype)
            for place, item in enumerate(operands)
        ]
        projected.append(
            pl.pallas_call(
                functools.partial(first_kernel, tile)
                if first
                else functools.partial(later_kernel, tile, head_index),
                out_shape=(
                    shape_of((row_count, HD), jnp.bfloat16),
                    shape_of((row_count, HD), jnp.bfloat16),
                    shape_of((2 * reads, latents)),
                ),
                in_specs=[HBM if first else VMEM] * 5,
                out_specs=(VMEM,) * 3,
                scratch_shapes=loaded + [pltpu.SemaphoreType.DMA((5,))] if first else [],
                compiler_params=params(57 if first else 16),
                cost_estimate=block_work,
                name="project",
            )(*operands)
        )

    stats = [item[2] for item in projected]
    stats_got = [None] * head_count
    after = stats[-1]
    for place, bit in enumerate(bits_of(row_devices)):
        for head_index in range(head_count):
            if place:
                own = stats[head_index]
                use = (place, head_index) in CHAIN
                after = pl.pallas_call(
                    merge_kernel,
                    out_shape=shape_of(stats[head_index].shape),
                    in_specs=[VMEM, VMEM, ANY],
                    out_specs=VMEM,
                    compiler_params=params(2),
                    name="merge",
                )(stats[head_index], stats_got[head_index], after if use else own)
                stats[head_index] = after
            stats_got[head_index] = swap(stats[head_index], "rows", row_devices, bit)
    stats_parts = list(zip(stats, stats_got))

    order_low = (lax.axis_index("rows") % low) ^ jnp.arange(low, dtype=jnp.int32)
    low_bits = [bit for bit in bits_of(row_devices) if bit < low]

    def scatter_low(block, axis):
        if low == 1:
            return block
        parts = jnp.moveaxis(
            block.reshape(block.shape[:axis] + (low, -1) + block.shape[axis + 1 :]), axis, 0
        )
        parts = jnp.take(parts, order_low, axis=0)
        for bit in low_bits:
            parts = parts.reshape((-1, 2) + parts.shape[1:])
            parts = parts[:, 0] + swap(parts[:, 1], "rows", row_devices, bit)
        return parts[0]

    def sum_low(block):
        for bit in low_bits:
            block = block + row_swap(block, bit=bit)
        return block

    row_swap = functools.partial(row_swap_of, count=row_devices)

    def kernel_call(kernel, shapes, operands, scratch, limit, name):
        return pl.pallas_call(
            kernel,
            out_shape=[shape_of(*item) for item in shapes],
            in_specs=[ANY] + [VMEM] * (len(operands) - 1),
            out_specs=[VMEM] * len(shapes),
            scratch_shapes=scratch,
            compiler_params=params(limit),
            cost_estimate=block_work,
            name=name,
        )(*operands)

    def input_products(after):
        share = shape_of((head_devices // 2, row_count, features // head_devices))
        return pl.pallas_call(
            functools.partial(input_kernel, "heads"),
            out_shape=(share, share),
            in_specs=[VMEM] * (2 + head_count) + [ANY],
            out_specs=(VMEM,) * 2,
            scratch_shapes=[pltpu.VMEM((row_count, features), jnp.float32)],
            compiler_params=params(16),
            cost_estimate=block_work,
            name="input",
        )(key_weight, value_weight, *(item[0] for item in grads_out), after)

    grads_out, weight_steps, marks = [], [], {}
    for head_index in range(head_count):
        keys, values, _ = projected[head_index]
        results = kernel_call(
            functools.partial(grads_kernel, head_index, "rows", low),
            [((row_count, 2 * HD), jnp.bfloat16), ((reads, row_count, latents), jnp.bfloat16)]
            + [
                ((2, 2, piece, end - begin),)
                for begin, end, _ in WEIGHT_PARTS[head_index]
                for _ in range(2)
            ],
            [
                grads_out[-1][0] if grads_out else stats_parts[1][0],
                *(inputs, keys, values, queries, out_grad),
                *stats_parts[head_index],
            ],
            [
                pltpu.VMEM((row_count, HD), jnp.float32),
                pltpu.VMEM((row_count, HD), jnp.float32),
                pltpu.VMEM((features, 2 * HD), jnp.float32),
                pltpu.VMEM((2 * reads, latents), jnp.float32),
            ],
            20,
            "grads",
        )
        grads_out.append(results)
        marks[f"A{head_index}"] = results[0]
        for part, (begin, end, bits) in enumerate(WEIGHT_PARTS[head_index]):
            keep, send = results[2 + 2 * part : 4 + 2 * part]
            theirs = row_swap(send, bit=bits[0] * low)
            if head_index + 1 == head_count:
                input_keep, input_send = input_products(marks["w0.1"])
                mine, send = pl.pallas_call(
                    split_kernel,
                    out_shape=(shape_of((1, *keep.shape[1:])),) * 2,
                    in_specs=[VMEM, VMEM, ANY],
                    out_specs=(VMEM,) * 2,
                    compiler_params=params(4),
                    name="split",
                )(keep, theirs, input_keep)
            else:
                send = keep[1:] + theirs[1:]
                mine = keep[:1] + theirs[:1]
            marks[f"w{head_index}.1"] = send
            weight_steps.append((mine, row_swap(send, bit=bits[1] * low)))

    query_terms, query_list = [], []
    for head_index in range(head_count):
        results = kernel_call(
            functools.partial(query_kernel, QUERY_PARTS[head_index], "rows", low),
            [
                ((GROUPS // 2, end - begin, latents // GROUPS, HD),)
                for begin, end, _ in QUERY_PARTS[head_index]
                for _ in range(2)
            ],
            [
                marks[AFTER.get(f"B{head_index}", f"A{head_index}")],
                grads_out[head_index][1],
                projected[head_index][0],
            ],
            [pltpu.VMEM((GROUPS // 2 * reads, tile, HD), jnp.float32)],
            16,
            "query",
        )
        marks[f"B{head_index}"] = results[0]
        for part, (begin, end, bits) in enumerate(QUERY_PARTS[head_index]):
            keep, send = results[2 * part : 2 * part + 2]
            for place, bit in enumerate(bits):
                theirs = row_swap(send, bit=bit * low)
                if place + 1 < len(bits):
                    middle = keep.shape[0] // 2
                    send = keep[middle:] + theirs[middle:]
                    keep = keep[:middle] + theirs[:middle]
                    marks[f"q{head_index}.{place + 1}"] = send
            terms = [keep, theirs]
            if low > 1:
                terms = [scatter_low((keep + theirs)[0], 1)[None]]
            query_terms += terms
            query_list.append((head_index, begin, end, len(terms)))

    def added(kernel, shape, mine, theirs, after):
        return pl.pallas_call(
            kernel,
            out_shape=shape_of(shape),
            in_specs=[VMEM, VMEM, ANY],
            out_specs=VMEM,
            compiler_params=params(4),
            cost_estimate=pl.CostEstimate(flops=1024, bytes_accessed=1024, transcendentals=0),
            name="added",
        )(mine, theirs, after)

    weight_terms, weight_list = [], []
    for head_index in range(head_count):
        for begin, end, bits in WEIGHT_PARTS[head_index]:
            mine, theirs = weight_steps.pop(0)
            first, second = (bit * low for bit in bits)
            for place, bit in ((2, LAST_BIT * low), (3, second)):
                after = AFTER.get(f"w{head_index}.{place}")
                if after:
                    mine = added(add_kernel, mine.shape, mine, theirs, marks[after])
                else:
                    mine = mine + theirs
                if place == 3:
                    mine = sum_low(mine)
                theirs = row_swap(mine, bit=bit)
                marks[f"w{head_index}.{place}"] = mine
            near = jnp.concatenate([mine, theirs], axis=0)
            weight_terms += [near, row_swap(near, bit=first)]
            weight_list.append((head_index, begin, end, bits))

    head_bits = bits_of(head_devices)[::-1]
    keep, theirs = input_keep, swap(input_send, "heads", head_devices, head_bits[0])
    for bit in head_bits[1:]:
        send = keep[bit:] + theirs[bit:]
        keep, theirs = keep[:bit] + theirs[:bit], swap(send, "heads", head_devices, bit)
    input_terms = (keep, theirs)

    key_weight_grad, value_weight_grad, input_grad, done = pl.pallas_call(
        functools.partial(weights_kernel, weight_list, "rows", low),
        out_shape=(shape_of((features, columns)),) * 2
        + (shape_of((row_count, features // head_devices)), shape_of((8, 128))),
        in_specs=[VMEM] * (2 + len(weight_terms)),
        out_specs=(VMEM,) * 4,
        compiler_params=params(8),
        name="weights",
    )(*input_terms, *weight_terms)
    query_grad = pl.pallas_call(
        functools.partial(queries_kernel, query_list),
        out_shape=shape_of((reads, latents // row_devices, columns)),
        in_specs=[ANY] + [VMEM] * len(query_terms),
        out_specs=VMEM,
        compiler_params=params(4),
        name="queries",
    )(done, *query_terms)
    return (query_grad, key_weight_grad, value_weight_grad, input_grad)


def solution(mesh):
    in_specs = (
        P("rows", None),
        P(None, "heads"),
        P(None, "heads"),
        P(None, None, "heads"),
        P(None, None, "heads"),
    )
    out_specs = (P(None, "rows", "heads"), P(None, "heads"), P(None, "heads"), P("rows", "heads"))

    def body(*args):
        return on_device(mesh.shape["rows"], mesh.shape["heads"], *args)

    return jax.shard_map(body, mesh=mesh, in_specs=in_specs, out_specs=out_specs, check_vma=False)
```

```python
import functools

import jax
import jax.numpy as jnp
from jax import lax
from jax.experimental import pallas as pl
from jax.experimental.pallas import tpu as pltpu
from jax.sharding import PartitionSpec as P

HD = 128
GROUPS = 8
FACTOR = HD ** (-0.5)
LOG2_E = 1.4426950408889634
VMEM = pl.BlockSpec(memory_space=pltpu.VMEM)
HBM = pl.BlockSpec(memory_space=pltpu.HBM)
ANY = pl.BlockSpec(memory_space=pl.ANY)


def params(mebibytes):
    return pltpu.CompilerParams(vmem_limit_bytes=mebibytes * 1024 * 1024)


def last_contract(left, right):
    return lax.dot_general(
        left, right, (((1,), (1,)), ((), ())), preferred_element_type=jnp.float32
    )


def rows_contract(left, right):
    return lax.dot_general(
        left, right, (((0,), (0,)), ((), ())), preferred_element_type=jnp.float32
    )


def plain_dot(left, right):
    return jnp.dot(left, right, preferred_element_type=jnp.float32)


def swap(array, axis, count, bit):
    pairs = [(device, device ^ bit) for device in range(count)]
    return lax.ppermute(array, axis, pairs)


def counted(group):
    return group ^ ((group // 4) % 2 * 2)


def row_swap_of(array, count, bit):
    low = count // GROUPS
    if bit < low:
        return swap(array, "rows", count, bit)
    pairs = []
    for device in range(count):
        partner = counted(counted(device // low) ^ (bit // low))
        pairs.append((device, partner * low + device % low))
    return lax.ppermute(array, "rows", pairs)


def bits_of(count):
    return [1 << place for place in range(count.bit_length() - 1)]


def head_statistics(
    tile, cols, wait, inputs, key_weight, value_weight, queries, out_grad, keys, values, stats
):
    reads, latents, _ = queries.shape
    wait("inputs")
    wait("key_weight")
    keys[...] = plain_dot(inputs[...], key_weight[:, cols]).astype(jnp.bfloat16)
    wait("value_weight")
    values[...] = plain_dot(inputs[...], value_weight[:, cols]).astype(jnp.bfloat16)
    for step in range(latents // tile):
        at = slice(step * tile, (step + 1) * tile)
        for read_index in range(reads):
            wait((read_index, step))
            scores = last_contract(keys[...], queries[read_index, at, cols])
            scores = scores * (FACTOR * LOG2_E)
            weighted = last_contract(values[...], out_grad[read_index, at, cols])
            top = jnp.max(scores, axis=0, keepdims=True)
            expos = jnp.exp2(scores - top)
            total = jnp.sum(expos, axis=0, keepdims=True)
            accum = jnp.sum(expos * weighted, axis=0, keepdims=True)
            stats[read_index : read_index + 1, at] = top + jnp.log2(total)
            stats[reads + read_index : reads + read_index + 1, at] = accum / total


def first_kernel(tile, *refs):
    sources, results, targets, sems = refs[:5], refs[5:8], refs[8:13], refs[13]
    reads, latents, _ = targets[3].shape
    loads = {}

    def load(name, source, target):
        sem = sems.at[sum(len(copies) for copies in loads.values())]
        loads.setdefault(name, []).append(pltpu.make_async_copy(source, target, sem))
        loads[name][-1].start()

    load("inputs", sources[0], targets[0])
    load("key_weight", sources[1].at[:, :HD], targets[1])
    load("value_weight", sources[2].at[:, :HD], targets[2])
    for step in range(latents // tile):
        at = pl.ds(step * tile, tile)
        for read_index in range(reads):
            for source, target in zip(sources[3:], targets[3:]):
                load(
                    (read_index, step),
                    source.at[read_index, at, :HD],
                    target.at[read_index, at, :],
                )

    def wait(name):
        for copy in loads[name]:
            copy.wait()

    head_statistics(tile, slice(0, HD), wait, *targets, *results)


def later_kernel(tile, head_index, *refs):
    cols = slice(head_index * HD, (head_index + 1) * HD)
    head_statistics(tile, cols, lambda *_: None, *refs)


def merged(mine, theirs):
    reads = mine.shape[0] // 2
    own, other = mine[:reads], theirs[:reads]
    top = jnp.maximum(own, other)
    own_share = jnp.exp2(own - top)
    other_share = jnp.exp2(other - top)
    total = own_share + other_share
    delta = (mine[reads:] * own_share + theirs[reads:] * other_share) / total
    return top + jnp.log2(total), delta


def merge_kernel(mine, theirs, result):
    reads = mine.shape[0] // 2
    result[:reads], result[reads:] = merged(mine, theirs)


def group_at(bits, relative, high, me):
    flips = sum(bit * flip for bit, flip in zip(bits, relative))
    return counted((counted(me) % LAST_BIT ^ flips) + LAST_BIT * high)


LAST_BIT = 4
WEIGHT_PARTS = (((0, 256, (1, 2)),), ((0, 256, (1, 2)),))
QUERY_PARTS = (((0, 2, (2, 1, 4)),), ((0, 2, (1, 2, 4)),))
AFTER = {'w1.2': 'q0.1', 'i.0': 'w0.3'}


def grads_kernel(
    head_index, row_axis, low, after, inputs, keys, values, queries, out_grad, mine, theirs, *refs
):
    del after
    grads, score_grads = refs[:2]
    weight_parts = refs[2:-4]
    key_acc, value_acc, weights_ref, stats = refs[-4:]
    reads, latents, _ = queries.shape
    tile = latents // (GROUPS // 2)
    cols = slice(head_index * HD, (head_index + 1) * HD)
    stats[:reads], stats[reads:] = merged(mine, theirs)
    key_acc[...] = jnp.zeros_like(key_acc)
    value_acc[...] = jnp.zeros_like(value_acc)

    @pl.loop(0, latents // tile, unroll=True)
    def _(step):
        at = pl.ds(pl.multiple_of(step * tile, tile), tile)
        for read_index in range(reads):
            query_block = queries[read_index, at, cols]
            grad_block = out_grad[read_index, at, cols]
            scores = last_contract(keys[...], query_block) * (FACTOR * LOG2_E)
            weighted = last_contract(values[...], grad_block)
            probs = jnp.exp2(scores - stats[read_index : read_index + 1, at])
            delta = stats[reads + read_index : reads + read_index + 1, at]
            score_grad = (probs * (weighted - delta) * FACTOR).astype(jnp.bfloat16)
            score_grads[read_index, :, at] = score_grad
            key_acc[...] += plain_dot(score_grad, query_block)
            value_acc[...] += plain_dot(probs.astype(jnp.bfloat16), grad_block)

    grads[:, :HD] = key_acc[...].astype(jnp.bfloat16)
    grads[:, HD:] = value_acc[...].astype(jnp.bfloat16)
    weights_ref[...] = rows_contract(inputs[...], grads[...])
    features = inputs.shape[1]
    piece = features // GROUPS
    me = lax.axis_index(row_axis) // low
    for part, (begin, end, bits) in enumerate(WEIGHT_PARTS[head_index]):
        for first in range(2):
            ref = weight_parts[2 * part + first]
            for second in range(2):
                for high in range(2):
                    group = group_at(bits, (first, second), high, me)
                    start = pl.multiple_of(group * piece, piece)
                    ref[second, high] = weights_ref[pl.ds(start, piece), begin:end]


def input_kernel(head_axis, key_weight, value_weight, *refs):
    head_grads, (_, input_keep, input_send, total) = refs[:-4], refs[-4:]
    for head_index, grads in enumerate(head_grads):
        cols = slice(head_index * HD, (head_index + 1) * HD)
        part = last_contract(grads[:, :HD], key_weight[:, cols])
        part += last_contract(grads[:, HD:], value_weight[:, cols])
        total[...] = total[...] + part if head_index else part
    place = lax.axis_index(head_axis)
    shares = 2 * input_keep.shape[0]
    width = total.shape[1] // shares
    for relative in range(shares):
        ref = input_send if relative >= shares // 2 else input_keep
        start = pl.multiple_of((place ^ relative) * width, width)
        ref[relative % (shares // 2)] = total[:, pl.ds(start, width)]


def query_kernel(parts, row_axis, low, after, score_grads, keys, *refs):
    del after
    tile_ref = refs[-1]
    reads, _, latents = score_grads.shape
    piece = latents // GROUPS
    me = lax.axis_index(row_axis) // low
    side = lax.rem(me, 2)
    for part, (begin, end, bits) in enumerate(parts):
        for upper in range(GROUPS // 2):
            pair = counted(counted(me) ^ (2 * upper)) // 2
            at = pl.ds(pl.multiple_of(pair * 2 * piece, 2 * piece), 2 * piece)
            for read_index in range(begin, end):
                slot = upper * reads + read_index
                tile_ref[slot] = rows_contract(score_grads[read_index, :, at], keys[...])
                for flip in range(2):
                    half = pl.ds(pl.multiple_of((side ^ flip) * piece, piece), piece)
                    relative = 2 * upper + flip
                    ref = refs[2 * part + (1 if relative & bits[0] else 0)]
                    index = 2 * ((relative & bits[1]) // bits[1]) + (relative & bits[2]) // bits[2]
                    ref[index, read_index - begin] = tile_ref[slot, half, :]


def weights_kernel(weight_parts, row_axis, low, *refs):
    key_out, value_out, input_out, done = refs[-4:]
    refs = list(refs[:-4])
    input_out[...] = refs.pop(0)[0] + refs.pop(0)[0]
    done[...] = jnp.zeros_like(done)
    piece = key_out.shape[0] // GROUPS
    me = lax.axis_index(row_axis) // low
    for head_index, begin, end, bits in weight_parts:
        cols = slice(head_index * HD, (head_index + 1) * HD)
        for first in range(2):
            source = refs.pop(0)
            for second in range(2):
                for high in range(2):
                    group = group_at(bits, (first, second), high, me)
                    start = pl.multiple_of(group * piece, piece)
                    at = pl.ds(start, piece)
                    if begin == 0:
                        key_out[at, cols] = source[second, high, :, :HD]
                    if end == 2 * HD:
                        value_out[at, cols] = source[second, high, :, end - begin - HD :]


def queries_kernel(query_parts, after, *refs):
    del after
    query_out = refs[-1]
    refs = list(refs[:-1])
    for head_index, begin, end, terms in query_parts:
        cols = slice(head_index * HD, (head_index + 1) * HD)
        total = refs.pop(0)[0]
        for _ in range(terms - 1):
            total = total + refs.pop(0)[0]
        query_out[begin:end, :, cols] = total


def shape_of(shape, dtype=jnp.float32):
    return jax.ShapeDtypeStruct(shape, dtype)


def add_kernel(mine, theirs, after, total):
    del after
    total[...] = mine[...] + theirs[...]


def on_device(row_devices, head_devices, inputs, key_weight, value_weight, queries, out_grad):
    reads, latents, columns = queries.shape
    head_count = columns // HD
    row_count, features = inputs.shape
    low = row_devices // GROUPS
    tile = latents // (GROUPS // 2)
    piece = features // GROUPS
    operands = (inputs, key_weight, value_weight, queries, out_grad)
    block_work = pl.CostEstimate(
        flops=8 * reads * row_count * latents * HD,
        bytes_accessed=4 * 2**20,
        transcendentals=reads * row_count * latents,
    )

    projected = []
    for head_index in range(head_count):
        first = head_index == 0
        loaded = [
            pltpu.VMEM(item.shape[:-1] + ((HD,) if place else item.shape[-1:]), item.dtype)
            for place, item in enumerate(operands)
        ]
        projected.append(
            pl.pallas_call(
                functools.partial(first_kernel, tile)
                if first
                else functools.partial(later_kernel, tile, head_index),
                out_shape=(
                    shape_of((row_count, HD), jnp.bfloat16),
                    shape_of((row_count, HD), jnp.bfloat16),
                    shape_of((2 * reads, latents)),
                ),
                in_specs=[HBM if first else VMEM] * 5,
                out_specs=(VMEM,) * 3,
                scratch_shapes=loaded + [pltpu.SemaphoreType.DMA((3 + 2 * reads * (latents // tile),))]
                if first
                else [],
                compiler_params=params(57 if first else 16),
                cost_estimate=block_work,
                name="project",
            )(*operands)
        )

    stats_parts = []
    for head_index in range(head_count):
        stats = projected[head_index][2]
        for bit in bits_of(row_devices)[:-1]:
            theirs = swap(stats, "rows", row_devices, bit)
            stats = pl.pallas_call(
                merge_kernel,
                out_shape=shape_of(stats.shape),
                in_specs=[VMEM] * 2,
                out_specs=VMEM,
                compiler_params=params(2),
                name="merge",
            )(stats, theirs)
        stats_parts.append((stats, swap(stats, "rows", row_devices, bits_of(row_devices)[-1])))

    order_low = (lax.axis_index("rows") % low) ^ jnp.arange(low, dtype=jnp.int32)
    low_bits = [bit for bit in bits_of(row_devices) if bit < low]

    def scatter_low(block, axis):
        if low == 1:
            return block
        parts = jnp.moveaxis(
            block.reshape(block.shape[:axis] + (low, -1) + block.shape[axis + 1 :]), axis, 0
        )
        parts = jnp.take(parts, order_low, axis=0)
        for bit in low_bits:
            parts = parts.reshape((-1, 2) + parts.shape[1:])
            parts = parts[:, 0] + swap(parts[:, 1], "rows", row_devices, bit)
        return parts[0]

    def sum_low(block):
        for bit in low_bits:
            block = block + row_swap(block, bit=bit)
        return block

    row_swap = functools.partial(row_swap_of, count=row_devices)

    def kernel_call(kernel, shapes, operands, scratch, limit, name):
        return pl.pallas_call(
            kernel,
            out_shape=[shape_of(*item) for item in shapes],
            in_specs=[ANY] + [VMEM] * (len(operands) - 1),
            out_specs=[VMEM] * len(shapes),
            scratch_shapes=scratch,
            compiler_params=params(limit),
            cost_estimate=block_work,
            name=name,
        )(*operands)

    grads_out, weight_steps, marks = [], [], {}
    for head_index in range(head_count):
        keys, values, _ = projected[head_index]
        results = kernel_call(
            functools.partial(grads_kernel, head_index, "rows", low),
            [((row_count, 2 * HD), jnp.bfloat16), ((reads, row_count, latents), jnp.bfloat16)]
            + [
                ((2, 2, piece, end - begin),)
                for begin, end, _ in WEIGHT_PARTS[head_index]
                for _ in range(2)
            ],
            [
                grads_out[-1][0] if grads_out else stats_parts[0][0],
                *(inputs, keys, values, queries, out_grad),
                *stats_parts[head_index],
            ],
            [
                pltpu.VMEM((row_count, HD), jnp.float32),
                pltpu.VMEM((row_count, HD), jnp.float32),
                pltpu.VMEM((features, 2 * HD), jnp.float32),
                pltpu.VMEM((2 * reads, latents), jnp.float32),
            ],
            20,
            "grads",
        )
        grads_out.append(results)
        marks[f"A{head_index}"] = results[0]
        for part, (begin, end, bits) in enumerate(WEIGHT_PARTS[head_index]):
            keep, send = results[2 + 2 * part : 4 + 2 * part]
            theirs = row_swap(send, bit=bits[0] * low)
            send = keep[1:] + theirs[1:]
            mine = keep[:1] + theirs[:1]
            marks[f"w{head_index}.1"] = send
            weight_steps.append((mine, row_swap(send, bit=bits[1] * low)))

    query_terms, query_list = [], []
    for head_index in range(head_count):
        results = kernel_call(
            functools.partial(query_kernel, QUERY_PARTS[head_index], "rows", low),
            [
                ((GROUPS // 2, end - begin, latents // GROUPS, HD),)
                for begin, end, _ in QUERY_PARTS[head_index]
                for _ in range(2)
            ],
            [
                marks[AFTER.get(f"B{head_index}", f"A{head_index}")],
                grads_out[head_index][1],
                projected[head_index][0],
            ],
            [pltpu.VMEM((GROUPS // 2 * reads, tile, HD), jnp.float32)],
            16,
            "query",
        )
        marks[f"B{head_index}"] = results[0]
        for part, (begin, end, bits) in enumerate(QUERY_PARTS[head_index]):
            keep, send = results[2 * part : 2 * part + 2]
            for place, bit in enumerate(bits):
                theirs = row_swap(send, bit=bit * low)
                if place + 1 < len(bits):
                    middle = keep.shape[0] // 2
                    send = keep[middle:] + theirs[middle:]
                    keep = keep[:middle] + theirs[:middle]
                    marks[f"q{head_index}.{place + 1}"] = send
            terms = [keep, theirs]
            if low > 1:
                terms = [scatter_low((keep + theirs)[0], 1)[None]]
            query_terms += terms
            query_list.append((head_index, begin, end, len(terms)))

    def added(kernel, shape, mine, theirs, after):
        return pl.pallas_call(
            kernel,
            out_shape=shape_of(shape),
            in_specs=[VMEM, VMEM, ANY],
            out_specs=VMEM,
            compiler_params=params(4),
            cost_estimate=pl.CostEstimate(flops=1024, bytes_accessed=1024, transcendentals=0),
            name="added",
        )(mine, theirs, after)

    weight_terms, weight_list = [], []
    for head_index in range(head_count):
        for begin, end, bits in WEIGHT_PARTS[head_index]:
            mine, theirs = weight_steps.pop(0)
            first, second = (bit * low for bit in bits)
            for place, bit in ((2, LAST_BIT * low), (3, second)):
                after = AFTER.get(f"w{head_index}.{place}")
                if after:
                    mine = added(add_kernel, mine.shape, mine, theirs, marks[after])
                else:
                    mine = mine + theirs
                if place == 3:
                    mine = sum_low(mine)
                theirs = row_swap(mine, bit=bit)
                marks[f"w{head_index}.{place}"] = mine
            near = jnp.concatenate([mine, theirs], axis=0)
            weight_terms += [near, row_swap(near, bit=first)]
            weight_list.append((head_index, begin, end, bits))

    share = ((head_devices // 2, row_count, features // head_devices),)
    after = marks[AFTER.get("i.0", "B1")]
    input_keep, input_send = pl.pallas_call(
        functools.partial(input_kernel, "heads"),
        out_shape=[shape_of(*share)] * 2,
        in_specs=[VMEM] * (2 + head_count) + [ANY],
        out_specs=[VMEM] * 2,
        scratch_shapes=[pltpu.VMEM((row_count, features), jnp.float32)],
        compiler_params=params(16),
        cost_estimate=block_work,
        name="input",
    )(key_weight, value_weight, *(item[0] for item in grads_out), after)
    head_bits = bits_of(head_devices)[::-1]
    keep, theirs = input_keep, swap(input_send, "heads", head_devices, head_bits[0])
    for bit in head_bits[1:]:
        send = keep[bit:] + theirs[bit:]
        keep, theirs = keep[:bit] + theirs[:bit], swap(send, "heads", head_devices, bit)
    input_terms = (keep, theirs)

    key_weight_grad, value_weight_grad, input_grad, done = pl.pallas_call(
        functools.partial(weights_kernel, weight_list, "rows", low),
        out_shape=(shape_of((features, columns)),) * 2
        + (shape_of((row_count, features // head_devices)), shape_of((8, 128))),
        in_specs=[VMEM] * (2 + len(weight_terms)),
        out_specs=(VMEM,) * 4,
        compiler_params=params(8),
        name="weights",
    )(*input_terms, *weight_terms)
    query_grad = pl.pallas_call(
        functools.partial(queries_kernel, query_list),
        out_shape=shape_of((reads, latents // row_devices, columns)),
        in_specs=[ANY] + [VMEM] * len(query_terms),
        out_specs=VMEM,
        compiler_params=params(4),
        name="queries",
    )(done, *query_terms)
    return (query_grad, key_weight_grad, value_weight_grad, input_grad)


def solution(mesh):
    in_specs = (
        P("rows", None),
        P(None, "heads"),
        P(None, "heads"),
        P(None, None, "heads"),
        P(None, None, "heads"),
    )
    out_specs = (P(None, "rows", "heads"), P(None, "heads"), P(None, "heads"), P("rows", "heads"))

    def body(*args):
        return on_device(mesh.shape["rows"], mesh.shape["heads"], *args)

    return jax.shard_map(body, mesh=mesh, in_specs=in_specs, out_specs=out_specs, check_vma=False)
```

```python
import functools

import jax
import jax.numpy as jnp
from jax import lax
from jax.experimental import pallas as pl
from jax.experimental.pallas import tpu as pltpu
from jax.sharding import PartitionSpec as P

HD = 128
GROUPS = 8
FACTOR = HD ** (-0.5)
LOG2_E = 1.4426950408889634
VMEM = pl.BlockSpec(memory_space=pltpu.VMEM)
HBM = pl.BlockSpec(memory_space=pltpu.HBM)
ANY = pl.BlockSpec(memory_space=pl.ANY)


def params(mebibytes):
    return pltpu.CompilerParams(vmem_limit_bytes=mebibytes * 1024 * 1024)


def last_contract(left, right):
    return lax.dot_general(
        left, right, (((1,), (1,)), ((), ())), preferred_element_type=jnp.float32
    )


def rows_contract(left, right):
    return lax.dot_general(
        left, right, (((0,), (0,)), ((), ())), preferred_element_type=jnp.float32
    )


def plain_dot(left, right):
    return jnp.dot(left, right, preferred_element_type=jnp.float32)


def swap(array, axis, count, bit):
    pairs = [(device, device ^ bit) for device in range(count)]
    return lax.ppermute(array, axis, pairs)


def counted(group):
    return group ^ ((group // 4) % 2 * 2)


def row_swap_of(array, count, bit):
    low = count // GROUPS
    if bit < low:
        return swap(array, "rows", count, bit)
    pairs = []
    for device in range(count):
        partner = counted(counted(device // low) ^ (bit // low))
        pairs.append((device, partner * low + device % low))
    return lax.ppermute(array, "rows", pairs)


def bits_of(count):
    return [1 << place for place in range(count.bit_length() - 1)]


def head_statistics(
    tile, cols, wait, inputs, key_weight, value_weight, queries, out_grad, keys, values, stats
):
    reads, latents, _ = queries.shape
    wait(0, 1)
    keys[...] = plain_dot(inputs[...], key_weight[:, cols]).astype(jnp.bfloat16)
    wait(2)
    values[...] = plain_dot(inputs[...], value_weight[:, cols]).astype(jnp.bfloat16)
    wait(3, 4)

    @pl.loop(0, latents // tile, unroll=True)
    def _(step):
        at = pl.ds(pl.multiple_of(step * tile, tile), tile)
        for read_index in range(reads):
            scores = last_contract(keys[...], queries[read_index, at, cols])
            scores = scores * (FACTOR * LOG2_E)
            weighted = last_contract(values[...], out_grad[read_index, at, cols])
            top = jnp.max(scores, axis=0, keepdims=True)
            expos = jnp.exp2(scores - top)
            total = jnp.sum(expos, axis=0, keepdims=True)
            accum = jnp.sum(expos * weighted, axis=0, keepdims=True)
            stats[read_index : read_index + 1, at] = top + jnp.log2(total)
            stats[reads + read_index : reads + read_index + 1, at] = accum / total


def first_kernel(tile, *refs):
    sources, results, targets, sems = refs[:5], refs[5:8], refs[8:13], refs[13]
    loads = []
    for index, (source, target) in enumerate(zip(sources, targets)):
        if index:
            source = source.at[..., :HD]
        loads.append(pltpu.make_async_copy(source, target, sems.at[index]))
    for load in loads:
        load.start()

    def wait(*places):
        for place in places:
            loads[place].wait()

    head_statistics(tile, slice(0, HD), wait, *targets, *results)


def later_kernel(tile, head_index, *refs):
    cols = slice(head_index * HD, (head_index + 1) * HD)
    head_statistics(tile, cols, lambda *_: None, *refs)


def merged(mine, theirs):
    reads = mine.shape[0] // 2
    own, other = mine[:reads], theirs[:reads]
    top = jnp.maximum(own, other)
    own_share = jnp.exp2(own - top)
    other_share = jnp.exp2(other - top)
    total = own_share + other_share
    delta = (mine[reads:] * own_share + theirs[reads:] * other_share) / total
    return top + jnp.log2(total), delta


def merge_kernel(mine, theirs, result):
    reads = mine.shape[0] // 2
    result[:reads], result[reads:] = merged(mine, theirs)


def group_at(bits, relative, high, me):
    flips = sum(bit * flip for bit, flip in zip(bits, relative))
    return counted((counted(me) % LAST_BIT ^ flips) + LAST_BIT * high)


LAST_BIT = 4
WEIGHT_PARTS = (((0, 256, (1, 2)),), ((0, 256, (1, 2)),))
QUERY_PARTS = (((0, 2, (2, 1, 4)),), ((0, 2, (1, 2, 4)),))
AFTER = {'w1.2': 'q0.1', 'i.0': 'w0.3'}


def grads_kernel(
    head_index, row_axis, low, after, inputs, keys, values, queries, out_grad, mine, theirs, *refs
):
    del after
    grads, score_grads = refs[:2]
    weight_parts = refs[2:-4]
    key_acc, value_acc, weights_ref, stats = refs[-4:]
    reads, latents, _ = queries.shape
    tile = latents // 2
    cols = slice(head_index * HD, (head_index + 1) * HD)
    stats[:reads], stats[reads:] = merged(mine, theirs)
    key_acc[...] = jnp.zeros_like(key_acc)
    value_acc[...] = jnp.zeros_like(value_acc)

    @pl.loop(0, latents // tile, unroll=True)
    def _(step):
        at = pl.ds(pl.multiple_of(step * tile, tile), tile)
        for read_index in range(reads):
            query_block = queries[read_index, at, cols]
            grad_block = out_grad[read_index, at, cols]
            scores = last_contract(keys[...], query_block) * (FACTOR * LOG2_E)
            weighted = last_contract(values[...], grad_block)
            probs = jnp.exp2(scores - stats[read_index : read_index + 1, at])
            delta = stats[reads + read_index : reads + read_index + 1, at]
            score_grad = (probs * (weighted - delta) * FACTOR).astype(jnp.bfloat16)
            score_grads[read_index, :, at] = score_grad
            key_acc[...] += plain_dot(score_grad, query_block)
            value_acc[...] += plain_dot(probs.astype(jnp.bfloat16), grad_block)

    grads[:, :HD] = key_acc[...].astype(jnp.bfloat16)
    grads[:, HD:] = value_acc[...].astype(jnp.bfloat16)
    weights_ref[...] = rows_contract(inputs[...], grads[...])
    features = inputs.shape[1]
    piece = features // GROUPS
    me = lax.axis_index(row_axis) // low
    for part, (begin, end, bits) in enumerate(WEIGHT_PARTS[head_index]):
        for first in range(2):
            ref = weight_parts[2 * part + first]
            for second in range(2):
                for high in range(2):
                    group = group_at(bits, (first, second), high, me)
                    start = pl.multiple_of(group * piece, piece)
                    ref[second, high] = weights_ref[pl.ds(start, piece), begin:end]


def input_kernel(head_axis, key_weight, value_weight, *refs):
    head_grads, (_, input_keep, input_send, total) = refs[:-4], refs[-4:]
    for head_index, grads in enumerate(head_grads):
        cols = slice(head_index * HD, (head_index + 1) * HD)
        part = last_contract(grads[:, :HD], key_weight[:, cols])
        part += last_contract(grads[:, HD:], value_weight[:, cols])
        total[...] = total[...] + part if head_index else part
    place = lax.axis_index(head_axis)
    shares = 2 * input_keep.shape[0]
    width = total.shape[1] // shares
    for relative in range(shares):
        ref = input_send if relative >= shares // 2 else input_keep
        start = pl.multiple_of((place ^ relative) * width, width)
        ref[relative % (shares // 2)] = total[:, pl.ds(start, width)]


def query_kernel(parts, row_axis, low, after, score_grads, keys, *refs):
    del after
    tile_ref = refs[-1]
    reads, _, latents = score_grads.shape
    piece = latents // GROUPS
    me = lax.axis_index(row_axis) // low
    side = lax.rem(me, 2)
    for part, (begin, end, bits) in enumerate(parts):
        for upper in range(GROUPS // 2):
            pair = counted(counted(me) ^ (2 * upper)) // 2
            at = pl.ds(pl.multiple_of(pair * 2 * piece, 2 * piece), 2 * piece)
            for read_index in range(begin, end):
                slot = upper * reads + read_index
                tile_ref[slot] = rows_contract(score_grads[read_index, :, at], keys[...])
                for flip in range(2):
                    half = pl.ds(pl.multiple_of((side ^ flip) * piece, piece), piece)
                    relative = 2 * upper + flip
                    ref = refs[2 * part + (1 if relative & bits[0] else 0)]
                    index = 2 * ((relative & bits[1]) // bits[1]) + (relative & bits[2]) // bits[2]
                    ref[index, read_index - begin] = tile_ref[slot, half, :]


def weights_kernel(weight_parts, row_axis, low, *refs):
    key_out, value_out, input_out, done = refs[-4:]
    refs = list(refs[:-4])
    input_out[...] = refs.pop(0)[0] + refs.pop(0)[0]
    done[...] = jnp.zeros_like(done)
    piece = key_out.shape[0] // GROUPS
    me = lax.axis_index(row_axis) // low
    for head_index, begin, end, bits in weight_parts:
        cols = slice(head_index * HD, (head_index + 1) * HD)
        for first in range(2):
            source = refs.pop(0)
            for second in range(2):
                for high in range(2):
                    group = group_at(bits, (first, second), high, me)
                    start = pl.multiple_of(group * piece, piece)
                    at = pl.ds(start, piece)
                    if begin == 0:
                        key_out[at, cols] = source[second, high, :, :HD]
                    if end == 2 * HD:
                        value_out[at, cols] = source[second, high, :, end - begin - HD :]


def queries_kernel(query_parts, after, *refs):
    del after
    query_out = refs[-1]
    refs = list(refs[:-1])
    for head_index, begin, end, terms in query_parts:
        cols = slice(head_index * HD, (head_index + 1) * HD)
        total = refs.pop(0)[0]
        for _ in range(terms - 1):
            total = total + refs.pop(0)[0]
        query_out[begin:end, :, cols] = total


def shape_of(shape, dtype=jnp.float32):
    return jax.ShapeDtypeStruct(shape, dtype)


def add_kernel(mine, theirs, after, total):
    del after
    total[...] = mine[...] + theirs[...]


def on_device(row_devices, head_devices, inputs, key_weight, value_weight, queries, out_grad):
    reads, latents, columns = queries.shape
    head_count = columns // HD
    row_count, features = inputs.shape
    low = row_devices // GROUPS
    tile = latents // (GROUPS // 2)
    piece = features // GROUPS
    operands = (inputs, key_weight, value_weight, queries, out_grad)
    block_work = pl.CostEstimate(
        flops=8 * reads * row_count * latents * HD,
        bytes_accessed=4 * 2**20,
        transcendentals=reads * row_count * latents,
    )

    projected = []
    for head_index in range(head_count):
        first = head_index == 0
        loaded = [
            pltpu.VMEM(item.shape[:-1] + ((HD,) if place else item.shape[-1:]), item.dtype)
            for place, item in enumerate(operands)
        ]
        projected.append(
            pl.pallas_call(
                functools.partial(first_kernel, latents // 2)
                if first
                else functools.partial(later_kernel, latents // 2, head_index),
                out_shape=(
                    shape_of((row_count, HD), jnp.bfloat16),
                    shape_of((row_count, HD), jnp.bfloat16),
                    shape_of((2 * reads, latents)),
                ),
                in_specs=[HBM if first else VMEM] * 5,
                out_specs=(VMEM,) * 3,
                scratch_shapes=loaded + [pltpu.SemaphoreType.DMA((5,))] if first else [],
                compiler_params=params(57 if first else 16),
                cost_estimate=block_work,
                name="project",
            )(*operands)
        )

    stats_parts = []
    for head_index in range(head_count):
        stats = projected[head_index][2]
        for bit in bits_of(row_devices)[:-1]:
            theirs = swap(stats, "rows", row_devices, bit)
            stats = pl.pallas_call(
                merge_kernel,
                out_shape=shape_of(stats.shape),
                in_specs=[VMEM] * 2,
                out_specs=VMEM,
                compiler_params=params(2),
                name="merge",
            )(stats, theirs)
        stats_parts.append((stats, swap(stats, "rows", row_devices, bits_of(row_devices)[-1])))

    order_low = (lax.axis_index("rows") % low) ^ jnp.arange(low, dtype=jnp.int32)
    low_bits = [bit for bit in bits_of(row_devices) if bit < low]

    def scatter_low(block, axis):
        if low == 1:
            return block
        parts = jnp.moveaxis(
            block.reshape(block.shape[:axis] + (low, -1) + block.shape[axis + 1 :]), axis, 0
        )
        parts = jnp.take(parts, order_low, axis=0)
        for bit in low_bits:
            parts = parts.reshape((-1, 2) + parts.shape[1:])
            parts = parts[:, 0] + swap(parts[:, 1], "rows", row_devices, bit)
        return parts[0]

    def sum_low(block):
        for bit in low_bits:
            block = block + row_swap(block, bit=bit)
        return block

    row_swap = functools.partial(row_swap_of, count=row_devices)

    def kernel_call(kernel, shapes, operands, scratch, limit, name):
        return pl.pallas_call(
            kernel,
            out_shape=[shape_of(*item) for item in shapes],
            in_specs=[ANY] + [VMEM] * (len(operands) - 1),
            out_specs=[VMEM] * len(shapes),
            scratch_shapes=scratch,
            compiler_params=params(limit),
            cost_estimate=block_work,
            name=name,
        )(*operands)

    grads_out, weight_steps, marks = [], [], {}
    for head_index in range(head_count):
        keys, values, _ = projected[head_index]
        results = kernel_call(
            functools.partial(grads_kernel, head_index, "rows", low),
            [((row_count, 2 * HD), jnp.bfloat16), ((reads, row_count, latents), jnp.bfloat16)]
            + [
                ((2, 2, piece, end - begin),)
                for begin, end, _ in WEIGHT_PARTS[head_index]
                for _ in range(2)
            ],
            [
                grads_out[-1][0] if grads_out else stats_parts[0][0],
                *(inputs, keys, values, queries, out_grad),
                *stats_parts[head_index],
            ],
            [
                pltpu.VMEM((row_count, HD), jnp.float32),
                pltpu.VMEM((row_count, HD), jnp.float32),
                pltpu.VMEM((features, 2 * HD), jnp.float32),
                pltpu.VMEM((2 * reads, latents), jnp.float32),
            ],
            20,
            "grads",
        )
        grads_out.append(results)
        marks[f"A{head_index}"] = results[0]
        for part, (begin, end, bits) in enumerate(WEIGHT_PARTS[head_index]):
            keep, send = results[2 + 2 * part : 4 + 2 * part]
            theirs = row_swap(send, bit=bits[0] * low)
            send = keep[1:] + theirs[1:]
            mine = keep[:1] + theirs[:1]
            marks[f"w{head_index}.1"] = send
            weight_steps.append((mine, row_swap(send, bit=bits[1] * low)))

    query_terms, query_list = [], []
    for head_index in range(head_count):
        results = kernel_call(
            functools.partial(query_kernel, QUERY_PARTS[head_index], "rows", low),
            [
                ((GROUPS // 2, end - begin, latents // GROUPS, HD),)
                for begin, end, _ in QUERY_PARTS[head_index]
                for _ in range(2)
            ],
            [
                marks[AFTER.get(f"B{head_index}", f"A{head_index}")],
                grads_out[head_index][1],
                projected[head_index][0],
            ],
            [pltpu.VMEM((GROUPS // 2 * reads, tile, HD), jnp.float32)],
            16,
            "query",
        )
        marks[f"B{head_index}"] = results[0]
        for part, (begin, end, bits) in enumerate(QUERY_PARTS[head_index]):
            keep, send = results[2 * part : 2 * part + 2]
            for place, bit in enumerate(bits):
                theirs = row_swap(send, bit=bit * low)
                if place + 1 < len(bits):
                    middle = keep.shape[0] // 2
                    send = keep[middle:] + theirs[middle:]
                    keep = keep[:middle] + theirs[:middle]
                    marks[f"q{head_index}.{place + 1}"] = send
            terms = [keep, theirs]
            if low > 1:
                terms = [scatter_low((keep + theirs)[0], 1)[None]]
            query_terms += terms
            query_list.append((head_index, begin, end, len(terms)))

    def added(kernel, shape, mine, theirs, after):
        return pl.pallas_call(
            kernel,
            out_shape=shape_of(shape),
            in_specs=[VMEM, VMEM, ANY],
            out_specs=VMEM,
            compiler_params=params(4),
            cost_estimate=pl.CostEstimate(flops=1024, bytes_accessed=1024, transcendentals=0),
            name="added",
        )(mine, theirs, after)

    weight_terms, weight_list = [], []
    for head_index in range(head_count):
        for begin, end, bits in WEIGHT_PARTS[head_index]:
            mine, theirs = weight_steps.pop(0)
            first, second = (bit * low for bit in bits)
            for place, bit in ((2, LAST_BIT * low), (3, second)):
                after = AFTER.get(f"w{head_index}.{place}")
                if after:
                    mine = added(add_kernel, mine.shape, mine, theirs, marks[after])
                else:
                    mine = mine + theirs
                if place == 3:
                    mine = sum_low(mine)
                theirs = row_swap(mine, bit=bit)
                marks[f"w{head_index}.{place}"] = mine
            near = jnp.concatenate([mine, theirs], axis=0)
            weight_terms += [near, row_swap(near, bit=first)]
            weight_list.append((head_index, begin, end, bits))

    share = ((head_devices // 2, row_count, features // head_devices),)
    after = marks[AFTER.get("i.0", "B1")]
    input_keep, input_send = pl.pallas_call(
        functools.partial(input_kernel, "heads"),
        out_shape=[shape_of(*share)] * 2,
        in_specs=[VMEM] * (2 + head_count) + [ANY],
        out_specs=[VMEM] * 2,
        scratch_shapes=[pltpu.VMEM((row_count, features), jnp.float32)],
        compiler_params=params(16),
        cost_estimate=block_work,
        name="input",
    )(key_weight, value_weight, *(item[0] for item in grads_out), after)
    head_bits = bits_of(head_devices)[::-1]
    keep, theirs = input_keep, swap(input_send, "heads", head_devices, head_bits[0])
    for bit in head_bits[1:]:
        send = keep[bit:] + theirs[bit:]
        keep, theirs = keep[:bit] + theirs[:bit], swap(send, "heads", head_devices, bit)
    input_terms = (keep, theirs)

    key_weight_grad, value_weight_grad, input_grad, done = pl.pallas_call(
        functools.partial(weights_kernel, weight_list, "rows", low),
        out_shape=(shape_of((features, columns)),) * 2
        + (shape_of((row_count, features // head_devices)), shape_of((8, 128))),
        in_specs=[VMEM] * (2 + len(weight_terms)),
        out_specs=(VMEM,) * 4,
        compiler_params=params(8),
        name="weights",
    )(*input_terms, *weight_terms)
    query_grad = pl.pallas_call(
        functools.partial(queries_kernel, query_list),
        out_shape=shape_of((reads, latents // row_devices, columns)),
        in_specs=[ANY] + [VMEM] * len(query_terms),
        out_specs=VMEM,
        compiler_params=params(4),
        name="queries",
    )(done, *query_terms)
    return (query_grad, key_weight_grad, value_weight_grad, input_grad)


def solution(mesh):
    in_specs = (
        P("rows", None),
        P(None, "heads"),
        P(None, "heads"),
        P(None, None, "heads"),
        P(None, None, "heads"),
    )
    out_specs = (P(None, "rows", "heads"), P(None, "heads"), P(None, "heads"), P("rows", "heads"))

    def body(*args):
        return on_device(mesh.shape["rows"], mesh.shape["heads"], *args)

    return jax.shard_map(body, mesh=mesh, in_specs=in_specs, out_specs=out_specs, check_vma=False)
```

```python
import functools

import jax
import jax.numpy as jnp
from jax import lax
from jax.experimental import pallas as pl
from jax.experimental.pallas import tpu as pltpu
from jax.sharding import PartitionSpec as P

HD = 128
GROUPS = 8
FACTOR = HD ** (-0.5)
LOG2_E = 1.4426950408889634
VMEM = pl.BlockSpec(memory_space=pltpu.VMEM)
HBM = pl.BlockSpec(memory_space=pltpu.HBM)
ANY = pl.BlockSpec(memory_space=pl.ANY)


def params(mebibytes):
    return pltpu.CompilerParams(vmem_limit_bytes=mebibytes * 1024 * 1024)


def last_contract(left, right):
    return lax.dot_general(
        left, right, (((1,), (1,)), ((), ())), preferred_element_type=jnp.float32
    )


def rows_contract(left, right):
    return lax.dot_general(
        left, right, (((0,), (0,)), ((), ())), preferred_element_type=jnp.float32
    )


def plain_dot(left, right):
    return jnp.dot(left, right, preferred_element_type=jnp.float32)


def swap(array, axis, count, bit):
    pairs = [(device, device ^ bit) for device in range(count)]
    return lax.ppermute(array, axis, pairs)


def counted(group):
    return group ^ ((group // 4) % 2 * 2)


def row_swap_of(array, count, bit):
    low = count // GROUPS
    if bit < low:
        return swap(array, "rows", count, bit)
    pairs = []
    for device in range(count):
        partner = counted(counted(device // low) ^ (bit // low))
        pairs.append((device, partner * low + device % low))
    return lax.ppermute(array, "rows", pairs)


def bits_of(count):
    return [1 << place for place in range(count.bit_length() - 1)]


def head_statistics(
    tile, cols, wait, inputs, key_weight, value_weight, queries, out_grad, keys, values, stats
):
    reads, latents, _ = queries.shape
    wait(0, 1)
    keys[...] = plain_dot(inputs[...], key_weight[:, cols]).astype(jnp.bfloat16)
    wait(2)
    values[...] = plain_dot(inputs[...], value_weight[:, cols]).astype(jnp.bfloat16)
    wait(3, 4)

    @pl.loop(0, latents // tile, unroll=True)
    def _(step):
        at = pl.ds(pl.multiple_of(step * tile, tile), tile)
        for read_index in range(reads):
            scores = last_contract(keys[...], queries[read_index, at, cols])
            scores = scores * (FACTOR * LOG2_E)
            weighted = last_contract(values[...], out_grad[read_index, at, cols])
            top = jnp.max(scores, axis=0, keepdims=True)
            expos = jnp.exp2(scores - top)
            total = jnp.sum(expos, axis=0, keepdims=True)
            accum = jnp.sum(expos * weighted, axis=0, keepdims=True)
            stats[read_index : read_index + 1, at] = top + jnp.log2(total)
            stats[reads + read_index : reads + read_index + 1, at] = accum / total


def first_kernel(tile, *refs):
    sources, results, targets, sems = refs[:5], refs[5:8], refs[8:13], refs[13]
    loads = []
    for index, (source, target) in enumerate(zip(sources, targets)):
        if index:
            source = source.at[..., :HD]
        loads.append(pltpu.make_async_copy(source, target, sems.at[index]))
    for load in loads:
        load.start()

    def wait(*places):
        for place in places:
            loads[place].wait()

    head_statistics(tile, slice(0, HD), wait, *targets, *results)


def later_kernel(tile, head_index, *refs):
    cols = slice(head_index * HD, (head_index + 1) * HD)
    head_statistics(tile, cols, lambda *_: None, *refs)


def merged(mine, theirs):
    reads = mine.shape[0] // 2
    own, other = mine[:reads], theirs[:reads]
    top = jnp.maximum(own, other)
    own_share = jnp.exp2(own - top)
    other_share = jnp.exp2(other - top)
    total = own_share + other_share
    delta = (mine[reads:] * own_share + theirs[reads:] * other_share) / total
    return top + jnp.log2(total), delta


def merge_kernel(mine, theirs, result):
    reads = mine.shape[0] // 2
    result[:reads], result[reads:] = merged(mine, theirs)


def group_at(bits, relative, high, me):
    flips = sum(bit * flip for bit, flip in zip(bits, relative))
    return (me % LAST_BIT ^ flips) + LAST_BIT * high


LAST_BIT = 4
WEIGHT_PARTS = (((0, 256, (1, 2)),), ((0, 256, (1, 2)),))
QUERY_PARTS = (((0, 2, (2, 1, 4)),), ((0, 2, (1, 2, 4)),))
AFTER = {'w1.2': 'q0.1', 'i.0': 'w0.3'}


def grads_kernel(
    head_index, row_axis, low, after, inputs, keys, values, queries, out_grad, mine, theirs, *refs
):
    del after
    grads, score_grads = refs[:2]
    weight_parts = refs[2:-4]
    key_acc, value_acc, weights_ref, stats = refs[-4:]
    reads, latents, _ = queries.shape
    tile = latents // 2
    cols = slice(head_index * HD, (head_index + 1) * HD)
    stats[:reads], stats[reads:] = merged(mine, theirs)
    key_acc[...] = jnp.zeros_like(key_acc)
    value_acc[...] = jnp.zeros_like(value_acc)

    @pl.loop(0, latents // tile, unroll=True)
    def _(step):
        at = pl.ds(pl.multiple_of(step * tile, tile), tile)
        for read_index in range(reads):
            query_block = queries[read_index, at, cols]
            grad_block = out_grad[read_index, at, cols]
            scores = last_contract(keys[...], query_block) * (FACTOR * LOG2_E)
            weighted = last_contract(values[...], grad_block)
            probs = jnp.exp2(scores - stats[read_index : read_index + 1, at])
            delta = stats[reads + read_index : reads + read_index + 1, at]
            score_grad = (probs * (weighted - delta) * FACTOR).astype(jnp.bfloat16)
            score_grads[read_index, :, at] = score_grad
            key_acc[...] += plain_dot(score_grad, query_block)
            value_acc[...] += plain_dot(probs.astype(jnp.bfloat16), grad_block)

    grads[:, :HD] = key_acc[...].astype(jnp.bfloat16)
    grads[:, HD:] = value_acc[...].astype(jnp.bfloat16)
    weights_ref[...] = rows_contract(inputs[...], grads[...])
    features = inputs.shape[1]
    piece = features // GROUPS
    me = lax.axis_index(row_axis) // low
    for part, (begin, end, bits) in enumerate(WEIGHT_PARTS[head_index]):
        for first in range(2):
            ref = weight_parts[2 * part + first]
            for second in range(2):
                for high in range(2):
                    group = group_at(bits, (first, second), high, me)
                    start = pl.multiple_of(group * piece, piece)
                    ref[second, high] = weights_ref[pl.ds(start, piece), begin:end]


def input_kernel(head_axis, key_weight, value_weight, *refs):
    head_grads, (_, input_keep, input_send, total) = refs[:-4], refs[-4:]
    for head_index, grads in enumerate(head_grads):
        cols = slice(head_index * HD, (head_index + 1) * HD)
        part = last_contract(grads[:, :HD], key_weight[:, cols])
        part += last_contract(grads[:, HD:], value_weight[:, cols])
        total[...] = total[...] + part if head_index else part
    place = lax.axis_index(head_axis)
    shares = 2 * input_keep.shape[0]
    width = total.shape[1] // shares
    for relative in range(shares):
        ref = input_send if relative >= shares // 2 else input_keep
        start = pl.multiple_of((place ^ relative) * width, width)
        ref[relative % (shares // 2)] = total[:, pl.ds(start, width)]


def query_kernel(parts, row_axis, low, after, score_grads, keys, *refs):
    del after
    tile_ref = refs[-1]
    reads, _, latents = score_grads.shape
    piece = latents // GROUPS
    me = lax.axis_index(row_axis) // low
    side = lax.rem(me, 2)
    for part, (begin, end, bits) in enumerate(parts):
        for upper in range(GROUPS // 2):
            pair = counted(counted(me) ^ (2 * upper)) // 2
            at = pl.ds(pl.multiple_of(pair * 2 * piece, 2 * piece), 2 * piece)
            for read_index in range(begin, end):
                slot = upper * reads + read_index
                tile_ref[slot] = rows_contract(score_grads[read_index, :, at], keys[...])
                for flip in range(2):
                    half = pl.ds(pl.multiple_of((side ^ flip) * piece, piece), piece)
                    relative = 2 * upper + flip
                    ref = refs[2 * part + (1 if relative & bits[0] else 0)]
                    index = 2 * ((relative & bits[1]) // bits[1]) + (relative & bits[2]) // bits[2]
                    ref[index, read_index - begin] = tile_ref[slot, half, :]


def weights_kernel(weight_parts, row_axis, low, *refs):
    key_out, value_out, input_out, done = refs[-4:]
    refs = list(refs[:-4])
    input_out[...] = refs.pop(0)[0] + refs.pop(0)[0]
    done[...] = jnp.zeros_like(done)
    piece = key_out.shape[0] // GROUPS
    me = lax.axis_index(row_axis) // low
    for head_index, begin, end, bits in weight_parts:
        cols = slice(head_index * HD, (head_index + 1) * HD)
        for first in range(2):
            source = refs.pop(0)
            for second in range(2):
                for high in range(2):
                    group = group_at(bits, (first, second), high, me)
                    start = pl.multiple_of(group * piece, piece)
                    at = pl.ds(start, piece)
                    if begin == 0:
                        key_out[at, cols] = source[second, high, :, :HD]
                    if end == 2 * HD:
                        value_out[at, cols] = source[second, high, :, end - begin - HD :]


def queries_kernel(query_parts, after, *refs):
    del after
    query_out = refs[-1]
    refs = list(refs[:-1])
    for head_index, begin, end, terms in query_parts:
        cols = slice(head_index * HD, (head_index + 1) * HD)
        total = refs.pop(0)[0]
        for _ in range(terms - 1):
            total = total + refs.pop(0)[0]
        query_out[begin:end, :, cols] = total


def shape_of(shape, dtype=jnp.float32):
    return jax.ShapeDtypeStruct(shape, dtype)


def add_kernel(mine, theirs, after, total):
    del after
    total[...] = mine[...] + theirs[...]


def on_device(row_devices, head_devices, inputs, key_weight, value_weight, queries, out_grad):
    reads, latents, columns = queries.shape
    head_count = columns // HD
    row_count, features = inputs.shape
    low = row_devices // GROUPS
    tile = latents // (GROUPS // 2)
    piece = features // GROUPS
    operands = (inputs, key_weight, value_weight, queries, out_grad)
    block_work = pl.CostEstimate(
        flops=8 * reads * row_count * latents * HD,
        bytes_accessed=4 * 2**20,
        transcendentals=reads * row_count * latents,
    )

    projected = []
    for head_index in range(head_count):
        first = head_index == 0
        loaded = [
            pltpu.VMEM(item.shape[:-1] + ((HD,) if place else item.shape[-1:]), item.dtype)
            for place, item in enumerate(operands)
        ]
        projected.append(
            pl.pallas_call(
                functools.partial(first_kernel, tile)
                if first
                else functools.partial(later_kernel, latents // 2, head_index),
                out_shape=(
                    shape_of((row_count, HD), jnp.bfloat16),
                    shape_of((row_count, HD), jnp.bfloat16),
                    shape_of((2 * reads, latents)),
                ),
                in_specs=[HBM if first else VMEM] * 5,
                out_specs=(VMEM,) * 3,
                scratch_shapes=loaded + [pltpu.SemaphoreType.DMA((5,))] if first else [],
                compiler_params=params(57 if first else 16),
                cost_estimate=block_work,
                name="project",
            )(*operands)
        )

    stats_parts = []
    for head_index in range(head_count):
        stats = projected[head_index][2]
        for bit in bits_of(row_devices)[:-1]:
            theirs = swap(stats, "rows", row_devices, bit)
            stats = pl.pallas_call(
                merge_kernel,
                out_shape=shape_of(stats.shape),
                in_specs=[VMEM] * 2,
                out_specs=VMEM,
                compiler_params=params(2),
                name="merge",
            )(stats, theirs)
        stats_parts.append((stats, swap(stats, "rows", row_devices, bits_of(row_devices)[-1])))

    order_low = (lax.axis_index("rows") % low) ^ jnp.arange(low, dtype=jnp.int32)
    low_bits = [bit for bit in bits_of(row_devices) if bit < low]

    def scatter_low(block, axis):
        if low == 1:
            return block
        parts = jnp.moveaxis(
            block.reshape(block.shape[:axis] + (low, -1) + block.shape[axis + 1 :]), axis, 0
        )
        parts = jnp.take(parts, order_low, axis=0)
        for bit in low_bits:
            parts = parts.reshape((-1, 2) + parts.shape[1:])
            parts = parts[:, 0] + swap(parts[:, 1], "rows", row_devices, bit)
        return parts[0]

    def sum_low(block):
        for bit in low_bits:
            block = block + row_swap(block, bit=bit)
        return block

    row_swap = functools.partial(row_swap_of, count=row_devices)

    def kernel_call(kernel, shapes, operands, scratch, limit, name):
        return pl.pallas_call(
            kernel,
            out_shape=[shape_of(*item) for item in shapes],
            in_specs=[ANY] + [VMEM] * (len(operands) - 1),
            out_specs=[VMEM] * len(shapes),
            scratch_shapes=scratch,
            compiler_params=params(limit),
            cost_estimate=block_work,
            name=name,
        )(*operands)

    grads_out, weight_steps, marks = [], [], {}
    for head_index in range(head_count):
        keys, values, _ = projected[head_index]
        results = kernel_call(
            functools.partial(grads_kernel, head_index, "rows", low),
            [((row_count, 2 * HD), jnp.bfloat16), ((reads, row_count, latents), jnp.bfloat16)]
            + [
                ((2, 2, piece, end - begin),)
                for begin, end, _ in WEIGHT_PARTS[head_index]
                for _ in range(2)
            ],
            [
                grads_out[-1][0] if grads_out else stats_parts[0][0],
                *(inputs, keys, values, queries, out_grad),
                *stats_parts[head_index],
            ],
            [
                pltpu.VMEM((row_count, HD), jnp.float32),
                pltpu.VMEM((row_count, HD), jnp.float32),
                pltpu.VMEM((features, 2 * HD), jnp.float32),
                pltpu.VMEM((2 * reads, latents), jnp.float32),
            ],
            20,
            "grads",
        )
        grads_out.append(results)
        marks[f"A{head_index}"] = results[0]
        for part, (begin, end, bits) in enumerate(WEIGHT_PARTS[head_index]):
            keep, send = results[2 + 2 * part : 4 + 2 * part]
            theirs = swap(send, "rows", row_devices, bits[0] * low)
            send = keep[1:] + theirs[1:]
            mine = keep[:1] + theirs[:1]
            marks[f"w{head_index}.1"] = send
            weight_steps.append((mine, swap(send, "rows", row_devices, bits[1] * low)))

    query_terms, query_list = [], []
    for head_index in range(head_count):
        results = kernel_call(
            functools.partial(query_kernel, QUERY_PARTS[head_index], "rows", low),
            [
                ((GROUPS // 2, end - begin, latents // GROUPS, HD),)
                for begin, end, _ in QUERY_PARTS[head_index]
                for _ in range(2)
            ],
            [
                marks[AFTER.get(f"B{head_index}", f"A{head_index}")],
                grads_out[head_index][1],
                projected[head_index][0],
            ],
            [pltpu.VMEM((GROUPS // 2 * reads, tile, HD), jnp.float32)],
            16,
            "query",
        )
        marks[f"B{head_index}"] = results[0]
        for part, (begin, end, bits) in enumerate(QUERY_PARTS[head_index]):
            keep, send = results[2 * part : 2 * part + 2]
            for place, bit in enumerate(bits):
                theirs = row_swap(send, bit=bit * low)
                if place + 1 < len(bits):
                    middle = keep.shape[0] // 2
                    send = keep[middle:] + theirs[middle:]
                    keep = keep[:middle] + theirs[:middle]
                    marks[f"q{head_index}.{place + 1}"] = send
            terms = [keep, theirs]
            if low > 1:
                terms = [scatter_low((keep + theirs)[0], 1)[None]]
            query_terms += terms
            query_list.append((head_index, begin, end, len(terms)))

    def added(kernel, shape, mine, theirs, after):
        return pl.pallas_call(
            kernel,
            out_shape=shape_of(shape),
            in_specs=[VMEM, VMEM, ANY],
            out_specs=VMEM,
            compiler_params=params(4),
            cost_estimate=pl.CostEstimate(flops=1024, bytes_accessed=1024, transcendentals=0),
            name="added",
        )(mine, theirs, after)

    weight_terms, weight_list = [], []
    for head_index in range(head_count):
        for begin, end, bits in WEIGHT_PARTS[head_index]:
            mine, theirs = weight_steps.pop(0)
            first, second = (bit * low for bit in bits)
            for place, bit in ((2, LAST_BIT * low), (3, second)):
                after = AFTER.get(f"w{head_index}.{place}")
                if after:
                    mine = added(add_kernel, mine.shape, mine, theirs, marks[after])
                else:
                    mine = mine + theirs
                if place == 3:
                    mine = sum_low(mine)
                theirs = swap(mine, "rows", row_devices, bit)
                marks[f"w{head_index}.{place}"] = mine
            near = jnp.concatenate([mine, theirs], axis=0)
            weight_terms += [near, swap(near, "rows", row_devices, first)]
            weight_list.append((head_index, begin, end, bits))

    share = ((head_devices // 2, row_count, features // head_devices),)
    after = marks[AFTER.get("i.0", "B1")]
    input_keep, input_send = pl.pallas_call(
        functools.partial(input_kernel, "heads"),
        out_shape=[shape_of(*share)] * 2,
        in_specs=[VMEM] * (2 + head_count) + [ANY],
        out_specs=[VMEM] * 2,
        scratch_shapes=[pltpu.VMEM((row_count, features), jnp.float32)],
        compiler_params=params(16),
        cost_estimate=block_work,
        name="input",
    )(key_weight, value_weight, *(item[0] for item in grads_out), after)
    head_bits = bits_of(head_devices)[::-1]
    keep, theirs = input_keep, swap(input_send, "heads", head_devices, head_bits[0])
    for bit in head_bits[1:]:
        send = keep[bit:] + theirs[bit:]
        keep, theirs = keep[:bit] + theirs[:bit], swap(send, "heads", head_devices, bit)
    input_terms = (keep, theirs)

    key_weight_grad, value_weight_grad, input_grad, done = pl.pallas_call(
        functools.partial(weights_kernel, weight_list, "rows", low),
        out_shape=(shape_of((features, columns)),) * 2
        + (shape_of((row_count, features // head_devices)), shape_of((8, 128))),
        in_specs=[VMEM] * (2 + len(weight_terms)),
        out_specs=(VMEM,) * 4,
        compiler_params=params(8),
        name="weights",
    )(*input_terms, *weight_terms)
    query_grad = pl.pallas_call(
        functools.partial(queries_kernel, query_list),
        out_shape=shape_of((reads, latents // row_devices, columns)),
        in_specs=[ANY] + [VMEM] * len(query_terms),
        out_specs=VMEM,
        compiler_params=params(4),
        name="queries",
    )(done, *query_terms)
    return (query_grad, key_weight_grad, value_weight_grad, input_grad)


def solution(mesh):
    in_specs = (
        P("rows", None),
        P(None, "heads"),
        P(None, "heads"),
        P(None, None, "heads"),
        P(None, None, "heads"),
    )
    out_specs = (P(None, "rows", "heads"), P(None, "heads"), P(None, "heads"), P("rows", "heads"))

    def body(*args):
        return on_device(mesh.shape["rows"], mesh.shape["heads"], *args)

    return jax.shard_map(body, mesh=mesh, in_specs=in_specs, out_specs=out_specs, check_vma=False)
```

```python
import functools

import jax
import jax.numpy as jnp
from jax import lax
from jax.experimental import pallas as pl
from jax.experimental.pallas import tpu as pltpu
from jax.sharding import PartitionSpec as P

HD = 128
GROUPS = 8
FACTOR = HD ** (-0.5)
LOG2_E = 1.4426950408889634
VMEM = pl.BlockSpec(memory_space=pltpu.VMEM)
HBM = pl.BlockSpec(memory_space=pltpu.HBM)
ANY = pl.BlockSpec(memory_space=pl.ANY)


def params(mebibytes):
    return pltpu.CompilerParams(vmem_limit_bytes=mebibytes * 1024 * 1024)


def last_contract(left, right):
    return lax.dot_general(
        left, right, (((1,), (1,)), ((), ())), preferred_element_type=jnp.float32
    )


def rows_contract(left, right):
    return lax.dot_general(
        left, right, (((0,), (0,)), ((), ())), preferred_element_type=jnp.float32
    )


def plain_dot(left, right):
    return jnp.dot(left, right, preferred_element_type=jnp.float32)


def swap(array, axis, count, bit):
    pairs = [(device, device ^ bit) for device in range(count)]
    return lax.ppermute(array, axis, pairs)


def counted(group):
    return group ^ ((group // 4) % 2 * 2)


def row_swap_of(array, count, bit):
    low = count // GROUPS
    if bit < low:
        return swap(array, "rows", count, bit)
    pairs = []
    for device in range(count):
        partner = counted(counted(device // low) ^ (bit // low))
        pairs.append((device, partner * low + device % low))
    return lax.ppermute(array, "rows", pairs)


def bits_of(count):
    return [1 << place for place in range(count.bit_length() - 1)]


def head_statistics(
    tile, cols, wait, inputs, key_weight, value_weight, queries, out_grad, keys, values, stats
):
    reads, latents, _ = queries.shape
    wait(0, 1)
    keys[...] = plain_dot(inputs[...], key_weight[:, cols]).astype(jnp.bfloat16)
    wait(2)
    values[...] = plain_dot(inputs[...], value_weight[:, cols]).astype(jnp.bfloat16)
    wait(3, 4)

    @pl.loop(0, latents // tile, unroll=True)
    def _(step):
        at = pl.ds(pl.multiple_of(step * tile, tile), tile)
        for read_index in range(reads):
            scores = last_contract(keys[...], queries[read_index, at, cols])
            scores = scores * (FACTOR * LOG2_E)
            weighted = last_contract(values[...], out_grad[read_index, at, cols])
            top = jnp.max(scores, axis=0, keepdims=True)
            expos = jnp.exp2(scores - top)
            total = jnp.sum(expos, axis=0, keepdims=True)
            accum = jnp.sum(expos * weighted, axis=0, keepdims=True)
            stats[read_index : read_index + 1, at] = top + jnp.log2(total)
            stats[reads + read_index : reads + read_index + 1, at] = accum / total


def first_kernel(tile, *refs):
    sources, results, targets, sems = refs[:5], refs[5:8], refs[8:13], refs[13]
    loads = []
    for index, (source, target) in enumerate(zip(sources, targets)):
        if index:
            source = source.at[..., :HD]
        loads.append(pltpu.make_async_copy(source, target, sems.at[index]))
    for load in loads:
        load.start()

    def wait(*places):
        for place in places:
            loads[place].wait()

    head_statistics(tile, slice(0, HD), wait, *targets, *results)


def later_kernel(tile, head_index, *refs):
    cols = slice(head_index * HD, (head_index + 1) * HD)
    head_statistics(tile, cols, lambda *_: None, *refs)


def merged(mine, theirs):
    reads = mine.shape[0] // 2
    own, other = mine[:reads], theirs[:reads]
    top = jnp.maximum(own, other)
    own_share = jnp.exp2(own - top)
    other_share = jnp.exp2(other - top)
    total = own_share + other_share
    delta = (mine[reads:] * own_share + theirs[reads:] * other_share) / total
    return top + jnp.log2(total), delta


def merge_kernel(mine, theirs, result):
    reads = mine.shape[0] // 2
    result[:reads], result[reads:] = merged(mine, theirs)


def group_at(bits, relative, high, me):
    flips = sum(bit * flip for bit, flip in zip(bits, relative))
    return counted((counted(me) % LAST_BIT ^ flips) + LAST_BIT * high)


LAST_BIT = 4
WEIGHT_PARTS = (((0, 256, (1, 2)),), ((0, 256, (1, 2)),))
QUERY_PARTS = (((0, 2, (2, 1, 4)),), ((0, 2, (1, 2, 4)),))
AFTER = {'w1.2': 'q0.1', 'i.0': 'w0.3'}


def grads_kernel(
    head_index, row_axis, low, after, inputs, keys, values, queries, out_grad, mine, theirs, *refs
):
    del after
    grads, score_grads = refs[:2]
    weight_parts = refs[2:-4]
    key_acc, value_acc, weights_ref, stats = refs[-4:]
    reads, latents, _ = queries.shape
    tile = latents // 2
    cols = slice(head_index * HD, (head_index + 1) * HD)
    stats[:reads], stats[reads:] = merged(mine, theirs)
    key_acc[...] = jnp.zeros_like(key_acc)
    value_acc[...] = jnp.zeros_like(value_acc)

    @pl.loop(0, latents // tile, unroll=True)
    def _(step):
        at = pl.ds(pl.multiple_of(step * tile, tile), tile)
        for read_index in range(reads):
            query_block = queries[read_index, at, cols]
            grad_block = out_grad[read_index, at, cols]
            scores = last_contract(keys[...], query_block) * (FACTOR * LOG2_E)
            weighted = last_contract(values[...], grad_block)
            probs = jnp.exp2(scores - stats[read_index : read_index + 1, at])
            delta = stats[reads + read_index : reads + read_index + 1, at]
            score_grad = (probs * (weighted - delta) * FACTOR).astype(jnp.bfloat16)
            score_grads[read_index, :, at] = score_grad
            key_acc[...] += plain_dot(score_grad, query_block)
            value_acc[...] += plain_dot(probs.astype(jnp.bfloat16), grad_block)

    grads[:, :HD] = key_acc[...].astype(jnp.bfloat16)
    grads[:, HD:] = value_acc[...].astype(jnp.bfloat16)
    weights_ref[...] = rows_contract(inputs[...], grads[...])
    features = inputs.shape[1]
    piece = features // GROUPS
    me = lax.axis_index(row_axis) // low
    for part, (begin, end, bits) in enumerate(WEIGHT_PARTS[head_index]):
        for first in range(2):
            ref = weight_parts[2 * part + first]
            for second in range(2):
                for high in range(2):
                    group = group_at(bits, (first, second), high, me)
                    start = pl.multiple_of(group * piece, piece)
                    ref[second, high] = weights_ref[pl.ds(start, piece), begin:end]


def input_kernel(head_axis, key_weight, value_weight, *refs):
    head_grads, (_, input_keep, input_send, total) = refs[:-4], refs[-4:]
    for head_index, grads in enumerate(head_grads):
        cols = slice(head_index * HD, (head_index + 1) * HD)
        part = last_contract(grads[:, :HD], key_weight[:, cols])
        part += last_contract(grads[:, HD:], value_weight[:, cols])
        total[...] = total[...] + part if head_index else part
    place = lax.axis_index(head_axis)
    shares = 2 * input_keep.shape[0]
    width = total.shape[1] // shares
    for relative in range(shares):
        ref = input_send if relative >= shares // 2 else input_keep
        start = pl.multiple_of((place ^ relative) * width, width)
        ref[relative % (shares // 2)] = total[:, pl.ds(start, width)]


def query_kernel(parts, row_axis, low, after, score_grads, keys, *refs):
    del after
    tile_ref = refs[-1]
    reads, _, latents = score_grads.shape
    piece = latents // GROUPS
    me = lax.axis_index(row_axis) // low
    side = lax.rem(me, 2)
    for part, (begin, end, bits) in enumerate(parts):
        for upper in range(GROUPS // 2):
            pair = counted(counted(me) ^ (2 * upper)) // 2
            at = pl.ds(pl.multiple_of(pair * 2 * piece, 2 * piece), 2 * piece)
            for read_index in range(begin, end):
                slot = upper * reads + read_index
                tile_ref[slot] = rows_contract(score_grads[read_index, :, at], keys[...])
                for flip in range(2):
                    half = pl.ds(pl.multiple_of((side ^ flip) * piece, piece), piece)
                    relative = 2 * upper + flip
                    ref = refs[2 * part + (1 if relative & bits[0] else 0)]
                    index = 2 * ((relative & bits[1]) // bits[1]) + (relative & bits[2]) // bits[2]
                    ref[index, read_index - begin] = tile_ref[slot, half, :]


def weights_kernel(weight_parts, row_axis, low, *refs):
    key_out, value_out, input_out, done = refs[-4:]
    refs = list(refs[:-4])
    input_out[...] = refs.pop(0)[0] + refs.pop(0)[0]
    done[...] = jnp.zeros_like(done)
    piece = key_out.shape[0] // GROUPS
    me = lax.axis_index(row_axis) // low
    for head_index, begin, end, bits in weight_parts:
        cols = slice(head_index * HD, (head_index + 1) * HD)
        for first in range(2):
            source = refs.pop(0)
            for second in range(2):
                for high in range(2):
                    group = group_at(bits, (first, second), high, me)
                    start = pl.multiple_of(group * piece, piece)
                    at = pl.ds(start, piece)
                    if begin == 0:
                        key_out[at, cols] = source[second, high, :, :HD]
                    if end == 2 * HD:
                        value_out[at, cols] = source[second, high, :, end - begin - HD :]


def queries_kernel(query_parts, after, *refs):
    del after
    query_out = refs[-1]
    refs = list(refs[:-1])
    for head_index, begin, end, terms in query_parts:
        cols = slice(head_index * HD, (head_index + 1) * HD)
        total = refs.pop(0)[0]
        for _ in range(terms - 1):
            total = total + refs.pop(0)[0]
        query_out[begin:end, :, cols] = total


def shape_of(shape, dtype=jnp.float32):
    return jax.ShapeDtypeStruct(shape, dtype)


def add_kernel(mine, theirs, after, total):
    del after
    total[...] = mine[...] + theirs[...]


def on_device(row_devices, head_devices, inputs, key_weight, value_weight, queries, out_grad):
    reads, latents, columns = queries.shape
    head_count = columns // HD
    row_count, features = inputs.shape
    low = row_devices // GROUPS
    tile = latents // (GROUPS // 2)
    piece = features // GROUPS
    operands = (inputs, key_weight, value_weight, queries, out_grad)
    block_work = pl.CostEstimate(
        flops=8 * reads * row_count * latents * HD,
        bytes_accessed=4 * 2**20,
        transcendentals=reads * row_count * latents,
    )

    projected = []
    for head_index in range(head_count):
        first = head_index == 0
        loaded = [
            pltpu.VMEM(item.shape[:-1] + ((HD,) if place else item.shape[-1:]), item.dtype)
            for place, item in enumerate(operands)
        ]
        projected.append(
            pl.pallas_call(
                functools.partial(first_kernel, tile)
                if first
                else functools.partial(later_kernel, latents // 2, head_index),
                out_shape=(
                    shape_of((row_count, HD), jnp.bfloat16),
                    shape_of((row_count, HD), jnp.bfloat16),
                    shape_of((2 * reads, latents)),
                ),
                in_specs=[HBM if first else VMEM] * 5,
                out_specs=(VMEM,) * 3,
                scratch_shapes=loaded + [pltpu.SemaphoreType.DMA((5,))] if first else [],
                compiler_params=params(57 if first else 16),
                cost_estimate=block_work,
                name="project",
            )(*operands)
        )

    stats_parts = []
    for head_index in range(head_count):
        stats = projected[head_index][2]
        for bit in bits_of(row_devices)[:-1]:
            theirs = swap(stats, "rows", row_devices, bit)
            stats = pl.pallas_call(
                merge_kernel,
                out_shape=shape_of(stats.shape),
                in_specs=[VMEM] * 2,
                out_specs=VMEM,
                compiler_params=params(2),
                name="merge",
            )(stats, theirs)
        stats_parts.append((stats, swap(stats, "rows", row_devices, bits_of(row_devices)[-1])))

    order_low = (lax.axis_index("rows") % low) ^ jnp.arange(low, dtype=jnp.int32)
    low_bits = [bit for bit in bits_of(row_devices) if bit < low]

    def scatter_low(block, axis):
        if low == 1:
            return block
        parts = jnp.moveaxis(
            block.reshape(block.shape[:axis] + (low, -1) + block.shape[axis + 1 :]), axis, 0
        )
        parts = jnp.take(parts, order_low, axis=0)
        for bit in low_bits:
            parts = parts.reshape((-1, 2) + parts.shape[1:])
            parts = parts[:, 0] + swap(parts[:, 1], "rows", row_devices, bit)
        return parts[0]

    def sum_low(block):
        for bit in low_bits:
            block = block + row_swap(block, bit=bit)
        return block

    row_swap = functools.partial(row_swap_of, count=row_devices)

    def kernel_call(kernel, shapes, operands, scratch, limit, name):
        return pl.pallas_call(
            kernel,
            out_shape=[shape_of(*item) for item in shapes],
            in_specs=[ANY] + [VMEM] * (len(operands) - 1),
            out_specs=[VMEM] * len(shapes),
            scratch_shapes=scratch,
            compiler_params=params(limit),
            cost_estimate=block_work,
            name=name,
        )(*operands)

    grads_out, weight_steps, marks = [], [], {}
    for head_index in range(head_count):
        keys, values, _ = projected[head_index]
        results = kernel_call(
            functools.partial(grads_kernel, head_index, "rows", low),
            [((row_count, 2 * HD), jnp.bfloat16), ((reads, row_count, latents), jnp.bfloat16)]
            + [
                ((2, 2, piece, end - begin),)
                for begin, end, _ in WEIGHT_PARTS[head_index]
                for _ in range(2)
            ],
            [
                grads_out[-1][0] if grads_out else stats_parts[0][0],
                *(inputs, keys, values, queries, out_grad),
                *stats_parts[head_index],
            ],
            [
                pltpu.VMEM((row_count, HD), jnp.float32),
                pltpu.VMEM((row_count, HD), jnp.float32),
                pltpu.VMEM((features, 2 * HD), jnp.float32),
                pltpu.VMEM((2 * reads, latents), jnp.float32),
            ],
            20,
            "grads",
        )
        grads_out.append(results)
        marks[f"A{head_index}"] = results[0]
        for part, (begin, end, bits) in enumerate(WEIGHT_PARTS[head_index]):
            keep, send = results[2 + 2 * part : 4 + 2 * part]
            theirs = row_swap(send, bit=bits[0] * low)
            send = keep[1:] + theirs[1:]
            mine = keep[:1] + theirs[:1]
            marks[f"w{head_index}.1"] = send
            weight_steps.append((mine, row_swap(send, bit=bits[1] * low)))

    query_terms, query_list = [], []
    for head_index in range(head_count):
        results = kernel_call(
            functools.partial(query_kernel, QUERY_PARTS[head_index], "rows", low),
            [
                ((GROUPS // 2, end - begin, latents // GROUPS, HD),)
                for begin, end, _ in QUERY_PARTS[head_index]
                for _ in range(2)
            ],
            [
                marks[AFTER.get(f"B{head_index}", f"A{head_index}")],
                grads_out[head_index][1],
                projected[head_index][0],
            ],
            [pltpu.VMEM((GROUPS // 2 * reads, tile, HD), jnp.float32)],
            16,
            "query",
        )
        marks[f"B{head_index}"] = results[0]
        for part, (begin, end, bits) in enumerate(QUERY_PARTS[head_index]):
            keep, send = results[2 * part : 2 * part + 2]
            for place, bit in enumerate(bits):
                theirs = row_swap(send, bit=bit * low)
                if place + 1 < len(bits):
                    middle = keep.shape[0] // 2
                    send = keep[middle:] + theirs[middle:]
                    keep = keep[:middle] + theirs[:middle]
                    marks[f"q{head_index}.{place + 1}"] = send
            terms = [keep, theirs]
            if low > 1:
                terms = [scatter_low((keep + theirs)[0], 1)[None]]
            query_terms += terms
            query_list.append((head_index, begin, end, len(terms)))

    def added(kernel, shape, mine, theirs, after):
        return pl.pallas_call(
            kernel,
            out_shape=shape_of(shape),
            in_specs=[VMEM, VMEM, ANY],
            out_specs=VMEM,
            compiler_params=params(4),
            cost_estimate=pl.CostEstimate(flops=1024, bytes_accessed=1024, transcendentals=0),
            name="added",
        )(mine, theirs, after)

    weight_terms, weight_list = [], []
    for head_index in range(head_count):
        for begin, end, bits in WEIGHT_PARTS[head_index]:
            mine, theirs = weight_steps.pop(0)
            first, second = (bit * low for bit in bits)
            for place, bit in ((2, LAST_BIT * low), (3, second)):
                after = AFTER.get(f"w{head_index}.{place}")
                if after:
                    mine = added(add_kernel, mine.shape, mine, theirs, marks[after])
                else:
                    mine = mine + theirs
                if place == 3:
                    mine = sum_low(mine)
                theirs = row_swap(mine, bit=bit)
                marks[f"w{head_index}.{place}"] = mine
            near = jnp.concatenate([mine, theirs], axis=0)
            weight_terms += [near, row_swap(near, bit=first)]
            weight_list.append((head_index, begin, end, bits))

    share = ((head_devices // 2, row_count, features // head_devices),)
    after = marks[AFTER.get("i.0", "B1")]
    input_keep, input_send = pl.pallas_call(
        functools.partial(input_kernel, "heads"),
        out_shape=[shape_of(*share)] * 2,
        in_specs=[VMEM] * (2 + head_count) + [ANY],
        out_specs=[VMEM] * 2,
        scratch_shapes=[pltpu.VMEM((row_count, features), jnp.float32)],
        compiler_params=params(16),
        cost_estimate=block_work,
        name="input",
    )(key_weight, value_weight, *(item[0] for item in grads_out), after)
    head_bits = bits_of(head_devices)[::-1]
    keep, theirs = input_keep, swap(input_send, "heads", head_devices, head_bits[0])
    for bit in head_bits[1:]:
        send = keep[bit:] + theirs[bit:]
        keep, theirs = keep[:bit] + theirs[:bit], swap(send, "heads", head_devices, bit)
    input_terms = (keep, theirs)

    key_weight_grad, value_weight_grad, input_grad, done = pl.pallas_call(
        functools.partial(weights_kernel, weight_list, "rows", low),
        out_shape=(shape_of((features, columns)),) * 2
        + (shape_of((row_count, features // head_devices)), shape_of((8, 128))),
        in_specs=[VMEM] * (2 + len(weight_terms)),
        out_specs=(VMEM,) * 4,
        compiler_params=params(8),
        name="weights",
    )(*input_terms, *weight_terms)
    query_grad = pl.pallas_call(
        functools.partial(queries_kernel, query_list),
        out_shape=shape_of((reads, latents // row_devices, columns)),
        in_specs=[ANY] + [VMEM] * len(query_terms),
        out_specs=VMEM,
        compiler_params=params(4),
        name="queries",
    )(done, *query_terms)
    return (query_grad, key_weight_grad, value_weight_grad, input_grad)


def solution(mesh):
    in_specs = (
        P("rows", None),
        P(None, "heads"),
        P(None, "heads"),
        P(None, None, "heads"),
        P(None, None, "heads"),
    )
    out_specs = (P(None, "rows", "heads"), P(None, "heads"), P(None, "heads"), P("rows", "heads"))

    def body(*args):
        return on_device(mesh.shape["rows"], mesh.shape["heads"], *args)

    return jax.shard_map(body, mesh=mesh, in_specs=in_specs, out_specs=out_specs, check_vma=False)
```

```python
import functools

import jax
import jax.numpy as jnp
from jax import lax
from jax.experimental import pallas as pl
from jax.experimental.pallas import tpu as pltpu
from jax.sharding import PartitionSpec as P

HD = 128
GROUPS = 8
FACTOR = HD ** (-0.5)
LOG2_E = 1.4426950408889634
VMEM = pl.BlockSpec(memory_space=pltpu.VMEM)
HBM = pl.BlockSpec(memory_space=pltpu.HBM)
ANY = pl.BlockSpec(memory_space=pl.ANY)


def params(mebibytes):
    return pltpu.CompilerParams(vmem_limit_bytes=mebibytes * 1024 * 1024)


def last_contract(left, right):
    return lax.dot_general(
        left, right, (((1,), (1,)), ((), ())), preferred_element_type=jnp.float32
    )


def rows_contract(left, right):
    return lax.dot_general(
        left, right, (((0,), (0,)), ((), ())), preferred_element_type=jnp.float32
    )


def plain_dot(left, right):
    return jnp.dot(left, right, preferred_element_type=jnp.float32)


def swap(array, axis, count, bit):
    pairs = [(device, device ^ bit) for device in range(count)]
    return lax.ppermute(array, axis, pairs)


def counted(group):
    return group ^ ((group // 4) % 2 * 2)


def row_swap_of(array, count, bit):
    low = count // GROUPS
    if bit < low:
        return swap(array, "rows", count, bit)
    pairs = []
    for device in range(count):
        partner = counted(counted(device // low) ^ (bit // low))
        pairs.append((device, partner * low + device % low))
    return lax.ppermute(array, "rows", pairs)


def bits_of(count):
    return [1 << place for place in range(count.bit_length() - 1)]


def head_statistics(
    tile, cols, wait, inputs, key_weight, value_weight, queries, out_grad, keys, values, stats
):
    reads, latents, _ = queries.shape
    wait(0, 1)
    keys[...] = plain_dot(inputs[...], key_weight[:, cols]).astype(jnp.bfloat16)
    wait(2)
    values[...] = plain_dot(inputs[...], value_weight[:, cols]).astype(jnp.bfloat16)
    wait(3, 4)

    @pl.loop(0, latents // tile, unroll=True)
    def _(step):
        at = pl.ds(pl.multiple_of(step * tile, tile), tile)
        for read_index in range(reads):
            scores = last_contract(keys[...], queries[read_index, at, cols])
            scores = scores * (FACTOR * LOG2_E)
            weighted = last_contract(values[...], out_grad[read_index, at, cols])
            top = jnp.max(scores, axis=0, keepdims=True)
            expos = jnp.exp2(scores - top)
            total = jnp.sum(expos, axis=0, keepdims=True)
            accum = jnp.sum(expos * weighted, axis=0, keepdims=True)
            stats[read_index : read_index + 1, at] = top + jnp.log2(total)
            stats[reads + read_index : reads + read_index + 1, at] = accum / total


def first_kernel(tile, *refs):
    sources, results, targets, sems = refs[:5], refs[5:8], refs[8:13], refs[13]
    loads = []
    for index, (source, target) in enumerate(zip(sources, targets)):
        if index:
            source = source.at[..., :HD]
        loads.append(pltpu.make_async_copy(source, target, sems.at[index]))
    for load in loads:
        load.start()

    def wait(*places):
        for place in places:
            loads[place].wait()

    head_statistics(tile, slice(0, HD), wait, *targets, *results)


def later_kernel(tile, head_index, *refs):
    cols = slice(head_index * HD, (head_index + 1) * HD)
    head_statistics(tile, cols, lambda *_: None, *refs)


def merged(mine, theirs):
    reads = mine.shape[0] // 2
    own, other = mine[:reads], theirs[:reads]
    top = jnp.maximum(own, other)
    own_share = jnp.exp2(own - top)
    other_share = jnp.exp2(other - top)
    total = own_share + other_share
    delta = (mine[reads:] * own_share + theirs[reads:] * other_share) / total
    return top + jnp.log2(total), delta


def merge_kernel(mine, theirs, result):
    reads = mine.shape[0] // 2
    result[:reads], result[reads:] = merged(mine, theirs)


def group_at(bits, relative, high, me):
    flips = sum(bit * flip for bit, flip in zip(bits, relative))
    return counted((counted(me) % LAST_BIT ^ flips) + LAST_BIT * high)


LAST_BIT = 4
WEIGHT_PARTS = (((0, 256, (1, 2)),), ((0, 256, (1, 2)),))
QUERY_PARTS = (((0, 2, (2, 1, 4)),), ((0, 2, (1, 2, 4)),))
AFTER = {'w1.2': 'q0.1', 'i.0': 'w0.3'}


def grads_kernel(
    head_index, row_axis, low, after, inputs, keys, values, queries, out_grad, mine, theirs, *refs
):
    del after
    grads, score_grads = refs[:2]
    weight_parts = refs[2:-4]
    key_acc, value_acc, weights_ref, stats = refs[-4:]
    reads, latents, _ = queries.shape
    tile = latents // 2
    cols = slice(head_index * HD, (head_index + 1) * HD)
    stats[:reads], stats[reads:] = merged(mine, theirs)
    key_acc[...] = jnp.zeros_like(key_acc)
    value_acc[...] = jnp.zeros_like(value_acc)

    @pl.loop(0, latents // tile, unroll=True)
    def _(step):
        at = pl.ds(pl.multiple_of(step * tile, tile), tile)
        for read_index in range(reads):
            query_block = queries[read_index, at, cols]
            grad_block = out_grad[read_index, at, cols]
            scores = last_contract(keys[...], query_block) * (FACTOR * LOG2_E)
            weighted = last_contract(values[...], grad_block)
            probs = jnp.exp2(scores - stats[read_index : read_index + 1, at])
            delta = stats[reads + read_index : reads + read_index + 1, at]
            score_grad = (probs * (weighted - delta) * FACTOR).astype(jnp.bfloat16)
            score_grads[read_index, :, at] = score_grad
            key_acc[...] += plain_dot(score_grad, query_block)
            value_acc[...] += plain_dot(probs.astype(jnp.bfloat16), grad_block)

    grads[:, :HD] = key_acc[...].astype(jnp.bfloat16)
    grads[:, HD:] = value_acc[...].astype(jnp.bfloat16)
    weights_ref[...] = rows_contract(inputs[...], grads[...])
    features = inputs.shape[1]
    piece = features // GROUPS
    me = lax.axis_index(row_axis) // low
    for part, (begin, end, bits) in enumerate(WEIGHT_PARTS[head_index]):
        for first in range(2):
            ref = weight_parts[2 * part + first]
            for second in range(2):
                for high in range(2):
                    group = group_at(bits, (first, second), high, me)
                    start = pl.multiple_of(group * piece, piece)
                    ref[second, high] = weights_ref[pl.ds(start, piece), begin:end]


def input_kernel(head_axis, key_weight, value_weight, *refs):
    head_grads, (_, input_keep, input_send, total) = refs[:-4], refs[-4:]
    for head_index, grads in enumerate(head_grads):
        cols = slice(head_index * HD, (head_index + 1) * HD)
        part = last_contract(grads[:, :HD], key_weight[:, cols])
        part += last_contract(grads[:, HD:], value_weight[:, cols])
        total[...] = total[...] + part if head_index else part
    place = lax.axis_index(head_axis)
    shares = 2 * input_keep.shape[0]
    width = total.shape[1] // shares
    for relative in range(shares):
        ref = input_send if relative >= shares // 2 else input_keep
        start = pl.multiple_of((place ^ relative) * width, width)
        ref[relative % (shares // 2)] = total[:, pl.ds(start, width)]


def query_kernel(parts, row_axis, low, after, score_grads, keys, *refs):
    del after
    tile_ref = refs[-1]
    reads, _, latents = score_grads.shape
    piece = latents // GROUPS
    me = lax.axis_index(row_axis) // low
    side = lax.rem(me, 2)
    for part, (begin, end, bits) in enumerate(parts):
        for upper in range(GROUPS // 2):
            pair = counted(counted(me) ^ (2 * upper)) // 2
            at = pl.ds(pl.multiple_of(pair * 2 * piece, 2 * piece), 2 * piece)
            for read_index in range(begin, end):
                slot = upper * reads + read_index
                tile_ref[slot] = rows_contract(score_grads[read_index, :, at], keys[...])
                for flip in range(2):
                    half = pl.ds(pl.multiple_of((side ^ flip) * piece, piece), piece)
                    relative = 2 * upper + flip
                    ref = refs[2 * part + (1 if relative & bits[0] else 0)]
                    index = 2 * ((relative & bits[1]) // bits[1]) + (relative & bits[2]) // bits[2]
                    ref[index, read_index - begin] = tile_ref[slot, half, :]


def weights_kernel(weight_parts, row_axis, low, *refs):
    key_out, value_out, input_out, done = refs[-4:]
    refs = list(refs[:-4])
    input_out[...] = refs.pop(0)[0] + refs.pop(0)[0]
    done[...] = jnp.zeros_like(done)
    piece = key_out.shape[0] // GROUPS
    me = lax.axis_index(row_axis) // low
    for head_index, begin, end, bits in weight_parts:
        cols = slice(head_index * HD, (head_index + 1) * HD)
        for first in range(2):
            source = refs.pop(0)
            for second in range(2):
                for high in range(2):
                    group = group_at(bits, (first, second), high, me)
                    start = pl.multiple_of(group * piece, piece)
                    at = pl.ds(start, piece)
                    if begin == 0:
                        key_out[at, cols] = source[second, high, :, :HD]
                    if end == 2 * HD:
                        value_out[at, cols] = source[second, high, :, end - begin - HD :]


def queries_kernel(query_parts, after, *refs):
    del after
    query_out = refs[-1]
    refs = list(refs[:-1])
    for head_index, begin, end, terms in query_parts:
        cols = slice(head_index * HD, (head_index + 1) * HD)
        total = refs.pop(0)[0]
        for _ in range(terms - 1):
            total = total + refs.pop(0)[0]
        query_out[begin:end, :, cols] = total


def shape_of(shape, dtype=jnp.float32):
    return jax.ShapeDtypeStruct(shape, dtype)


def add_kernel(mine, theirs, after, total):
    del after
    total[...] = mine[...] + theirs[...]


def on_device(row_devices, head_devices, inputs, key_weight, value_weight, queries, out_grad):
    reads, latents, columns = queries.shape
    head_count = columns // HD
    row_count, features = inputs.shape
    low = row_devices // GROUPS
    tile = latents // (GROUPS // 2)
    piece = features // GROUPS
    operands = (inputs, key_weight, value_weight, queries, out_grad)
    block_work = pl.CostEstimate(
        flops=8 * reads * row_count * latents * HD,
        bytes_accessed=4 * 2**20,
        transcendentals=reads * row_count * latents,
    )

    projected = []
    for head_index in range(head_count):
        first = head_index == 0
        loaded = [
            pltpu.VMEM(item.shape[:-1] + ((HD,) if place else item.shape[-1:]), item.dtype)
            for place, item in enumerate(operands)
        ]
        projected.append(
            pl.pallas_call(
                functools.partial(first_kernel, tile)
                if first
                else functools.partial(later_kernel, latents, head_index),
                out_shape=(
                    shape_of((row_count, HD), jnp.bfloat16),
                    shape_of((row_count, HD), jnp.bfloat16),
                    shape_of((2 * reads, latents)),
                ),
                in_specs=[HBM if first else VMEM] * 5,
                out_specs=(VMEM,) * 3,
                scratch_shapes=loaded + [pltpu.SemaphoreType.DMA((5,))] if first else [],
                compiler_params=params(57 if first else 16),
                cost_estimate=block_work,
                name="project",
            )(*operands)
        )

    stats_parts = []
    for head_index in range(head_count):
        stats = projected[head_index][2]
        for bit in bits_of(row_devices)[:-1]:
            theirs = swap(stats, "rows", row_devices, bit)
            stats = pl.pallas_call(
                merge_kernel,
                out_shape=shape_of(stats.shape),
                in_specs=[VMEM] * 2,
                out_specs=VMEM,
                compiler_params=params(2),
                name="merge",
            )(stats, theirs)
        stats_parts.append((stats, swap(stats, "rows", row_devices, bits_of(row_devices)[-1])))

    order_low = (lax.axis_index("rows") % low) ^ jnp.arange(low, dtype=jnp.int32)
    low_bits = [bit for bit in bits_of(row_devices) if bit < low]

    def scatter_low(block, axis):
        if low == 1:
            return block
        parts = jnp.moveaxis(
            block.reshape(block.shape[:axis] + (low, -1) + block.shape[axis + 1 :]), axis, 0
        )
        parts = jnp.take(parts, order_low, axis=0)
        for bit in low_bits:
            parts = parts.reshape((-1, 2) + parts.shape[1:])
            parts = parts[:, 0] + swap(parts[:, 1], "rows", row_devices, bit)
        return parts[0]

    def sum_low(block):
        for bit in low_bits:
            block = block + row_swap(block, bit=bit)
        return block

    row_swap = functools.partial(row_swap_of, count=row_devices)

    def kernel_call(kernel, shapes, operands, scratch, limit, name):
        return pl.pallas_call(
            kernel,
            out_shape=[shape_of(*item) for item in shapes],
            in_specs=[ANY] + [VMEM] * (len(operands) - 1),
            out_specs=[VMEM] * len(shapes),
            scratch_shapes=scratch,
            compiler_params=params(limit),
            cost_estimate=block_work,
            name=name,
        )(*operands)

    grads_out, weight_steps, marks = [], [], {}
    for head_index in range(head_count):
        keys, values, _ = projected[head_index]
        results = kernel_call(
            functools.partial(grads_kernel, head_index, "rows", low),
            [((row_count, 2 * HD), jnp.bfloat16), ((reads, row_count, latents), jnp.bfloat16)]
            + [
                ((2, 2, piece, end - begin),)
                for begin, end, _ in WEIGHT_PARTS[head_index]
                for _ in range(2)
            ],
            [
                grads_out[-1][0] if grads_out else stats_parts[0][0],
                *(inputs, keys, values, queries, out_grad),
                *stats_parts[head_index],
            ],
            [
                pltpu.VMEM((row_count, HD), jnp.float32),
                pltpu.VMEM((row_count, HD), jnp.float32),
                pltpu.VMEM((features, 2 * HD), jnp.float32),
                pltpu.VMEM((2 * reads, latents), jnp.float32),
            ],
            20,
            "grads",
        )
        grads_out.append(results)
        marks[f"A{head_index}"] = results[0]
        for part, (begin, end, bits) in enumerate(WEIGHT_PARTS[head_index]):
            keep, send = results[2 + 2 * part : 4 + 2 * part]
            theirs = row_swap(send, bit=bits[0] * low)
            send = keep[1:] + theirs[1:]
            mine = keep[:1] + theirs[:1]
            marks[f"w{head_index}.1"] = send
            weight_steps.append((mine, row_swap(send, bit=bits[1] * low)))

    query_terms, query_list = [], []
    for head_index in range(head_count):
        results = kernel_call(
            functools.partial(query_kernel, QUERY_PARTS[head_index], "rows", low),
            [
                ((GROUPS // 2, end - begin, latents // GROUPS, HD),)
                for begin, end, _ in QUERY_PARTS[head_index]
                for _ in range(2)
            ],
            [
                marks[AFTER.get(f"B{head_index}", f"A{head_index}")],
                grads_out[head_index][1],
                projected[head_index][0],
            ],
            [pltpu.VMEM((GROUPS // 2 * reads, tile, HD), jnp.float32)],
            16,
            "query",
        )
        marks[f"B{head_index}"] = results[0]
        for part, (begin, end, bits) in enumerate(QUERY_PARTS[head_index]):
            keep, send = results[2 * part : 2 * part + 2]
            for place, bit in enumerate(bits):
                theirs = row_swap(send, bit=bit * low)
                if place + 1 < len(bits):
                    middle = keep.shape[0] // 2
                    send = keep[middle:] + theirs[middle:]
                    keep = keep[:middle] + theirs[:middle]
                    marks[f"q{head_index}.{place + 1}"] = send
            terms = [keep, theirs]
            if low > 1:
                terms = [scatter_low((keep + theirs)[0], 1)[None]]
            query_terms += terms
            query_list.append((head_index, begin, end, len(terms)))

    def added(kernel, shape, mine, theirs, after):
        return pl.pallas_call(
            kernel,
            out_shape=shape_of(shape),
            in_specs=[VMEM, VMEM, ANY],
            out_specs=VMEM,
            compiler_params=params(4),
            cost_estimate=pl.CostEstimate(flops=1024, bytes_accessed=1024, transcendentals=0),
            name="added",
        )(mine, theirs, after)

    weight_terms, weight_list = [], []
    for head_index in range(head_count):
        for begin, end, bits in WEIGHT_PARTS[head_index]:
            mine, theirs = weight_steps.pop(0)
            first, second = (bit * low for bit in bits)
            for place, bit in ((2, LAST_BIT * low), (3, second)):
                after = AFTER.get(f"w{head_index}.{place}")
                if after:
                    mine = added(add_kernel, mine.shape, mine, theirs, marks[after])
                else:
                    mine = mine + theirs
                if place == 3:
                    mine = sum_low(mine)
                theirs = row_swap(mine, bit=bit)
                marks[f"w{head_index}.{place}"] = mine
            near = jnp.concatenate([mine, theirs], axis=0)
            weight_terms += [near, row_swap(near, bit=first)]
            weight_list.append((head_index, begin, end, bits))

    share = ((head_devices // 2, row_count, features // head_devices),)
    after = marks[AFTER.get("i.0", "B1")]
    input_keep, input_send = pl.pallas_call(
        functools.partial(input_kernel, "heads"),
        out_shape=[shape_of(*share)] * 2,
        in_specs=[VMEM] * (2 + head_count) + [ANY],
        out_specs=[VMEM] * 2,
        scratch_shapes=[pltpu.VMEM((row_count, features), jnp.float32)],
        compiler_params=params(16),
        cost_estimate=block_work,
        name="input",
    )(key_weight, value_weight, *(item[0] for item in grads_out), after)
    head_bits = bits_of(head_devices)[::-1]
    keep, theirs = input_keep, swap(input_send, "heads", head_devices, head_bits[0])
    for bit in head_bits[1:]:
        send = keep[bit:] + theirs[bit:]
        keep, theirs = keep[:bit] + theirs[:bit], swap(send, "heads", head_devices, bit)
    input_terms = (keep, theirs)

    key_weight_grad, value_weight_grad, input_grad, done = pl.pallas_call(
        functools.partial(weights_kernel, weight_list, "rows", low),
        out_shape=(shape_of((features, columns)),) * 2
        + (shape_of((row_count, features // head_devices)), shape_of((8, 128))),
        in_specs=[VMEM] * (2 + len(weight_terms)),
        out_specs=(VMEM,) * 4,
        compiler_params=params(8),
        name="weights",
    )(*input_terms, *weight_terms)
    query_grad = pl.pallas_call(
        functools.partial(queries_kernel, query_list),
        out_shape=shape_of((reads, latents // row_devices, columns)),
        in_specs=[ANY] + [VMEM] * len(query_terms),
        out_specs=VMEM,
        compiler_params=params(4),
        name="queries",
    )(done, *query_terms)
    return (query_grad, key_weight_grad, value_weight_grad, input_grad)


def solution(mesh):
    in_specs = (
        P("rows", None),
        P(None, "heads"),
        P(None, "heads"),
        P(None, None, "heads"),
        P(None, None, "heads"),
    )
    out_specs = (P(None, "rows", "heads"), P(None, "heads"), P(None, "heads"), P("rows", "heads"))

    def body(*args):
        return on_device(mesh.shape["rows"], mesh.shape["heads"], *args)

    return jax.shard_map(body, mesh=mesh, in_specs=in_specs, out_specs=out_specs, check_vma=False)
```

```python
import functools

import jax
import jax.numpy as jnp
from jax import lax
from jax.experimental import pallas as pl
from jax.experimental.pallas import tpu as pltpu
from jax.sharding import PartitionSpec as P

HD = 128
GROUPS = 8
FACTOR = HD ** (-0.5)
LOG2_E = 1.4426950408889634
VMEM = pl.BlockSpec(memory_space=pltpu.VMEM)
HBM = pl.BlockSpec(memory_space=pltpu.HBM)
ANY = pl.BlockSpec(memory_space=pl.ANY)


def params(mebibytes):
    return pltpu.CompilerParams(vmem_limit_bytes=mebibytes * 1024 * 1024)


def last_contract(left, right):
    return lax.dot_general(
        left, right, (((1,), (1,)), ((), ())), preferred_element_type=jnp.float32
    )


def rows_contract(left, right):
    return lax.dot_general(
        left, right, (((0,), (0,)), ((), ())), preferred_element_type=jnp.float32
    )


def plain_dot(left, right):
    return jnp.dot(left, right, preferred_element_type=jnp.float32)


def swap(array, axis, count, bit):
    pairs = [(device, device ^ bit) for device in range(count)]
    return lax.ppermute(array, axis, pairs)


def counted(group):
    return group ^ ((group // 4) % 2 * 2)


def row_swap_of(array, count, bit):
    low = count // GROUPS
    if bit < low:
        return swap(array, "rows", count, bit)
    pairs = []
    for device in range(count):
        partner = counted(counted(device // low) ^ (bit // low))
        pairs.append((device, partner * low + device % low))
    return lax.ppermute(array, "rows", pairs)


def bits_of(count):
    return [1 << place for place in range(count.bit_length() - 1)]


def head_statistics(
    tile, cols, wait, inputs, key_weight, value_weight, queries, out_grad, keys, values, stats
):
    reads, latents, _ = queries.shape
    wait(0, 1)
    keys[...] = plain_dot(inputs[...], key_weight[:, cols]).astype(jnp.bfloat16)
    wait(2)
    values[...] = plain_dot(inputs[...], value_weight[:, cols]).astype(jnp.bfloat16)
    wait(3, 4)

    @pl.loop(0, latents // tile, unroll=True)
    def _(step):
        at = pl.ds(pl.multiple_of(step * tile, tile), tile)
        for read_index in range(reads):
            scores = last_contract(keys[...], queries[read_index, at, cols])
            scores = scores * (FACTOR * LOG2_E)
            weighted = last_contract(values[...], out_grad[read_index, at, cols])
            top = jnp.max(scores, axis=0, keepdims=True)
            expos = jnp.exp2(scores - top)
            total = jnp.sum(expos, axis=0, keepdims=True)
            accum = jnp.sum(expos * weighted, axis=0, keepdims=True)
            stats[read_index : read_index + 1, at] = top + jnp.log2(total)
            stats[reads + read_index : reads + read_index + 1, at] = accum / total


def first_kernel(tile, *refs):
    sources, results, targets, sems = refs[:5], refs[5:8], refs[8:13], refs[13]
    loads = []
    for index, (source, target) in enumerate(zip(sources, targets)):
        if index:
            source = source.at[..., :HD]
        loads.append(pltpu.make_async_copy(source, target, sems.at[index]))
    for load in loads:
        load.start()

    def wait(*places):
        for place in places:
            loads[place].wait()

    head_statistics(tile, slice(0, HD), wait, *targets, *results)


def later_kernel(tile, head_index, *refs):
    cols = slice(head_index * HD, (head_index + 1) * HD)
    head_statistics(tile, cols, lambda *_: None, *refs)


def merged(mine, theirs):
    reads = mine.shape[0] // 2
    own, other = mine[:reads], theirs[:reads]
    top = jnp.maximum(own, other)
    own_share = jnp.exp2(own - top)
    other_share = jnp.exp2(other - top)
    total = own_share + other_share
    delta = (mine[reads:] * own_share + theirs[reads:] * other_share) / total
    return top + jnp.log2(total), delta


def merge_kernel(mine, theirs, result):
    reads = mine.shape[0] // 2
    result[:reads], result[reads:] = merged(mine, theirs)


def group_at(bits, relative, high, me):
    flips = sum(bit * flip for bit, flip in zip(bits, relative))
    return counted((counted(me) % LAST_BIT ^ flips) + LAST_BIT * high)


LAST_BIT = 4
WEIGHT_PARTS = (((0, 256, (1, 2)),), ((0, 256, (1, 2)),))
QUERY_PARTS = (((0, 2, (2, 1, 4)),), ((0, 2, (1, 2, 4)),))
AFTER = {'w1.2': 'q0.1', 'i.0': 'w0.3'}


def grads_kernel(
    head_index, row_axis, low, after, inputs, keys, values, queries, out_grad, mine, theirs, *refs
):
    del after
    grads, score_grads = refs[:2]
    weight_parts = refs[2:-4]
    key_acc, value_acc, weights_ref, stats = refs[-4:]
    reads, latents, _ = queries.shape
    tile = latents // 2
    cols = slice(head_index * HD, (head_index + 1) * HD)
    stats[:reads], stats[reads:] = merged(mine, theirs)
    key_acc[...] = jnp.zeros_like(key_acc)
    value_acc[...] = jnp.zeros_like(value_acc)

    @pl.loop(0, latents // tile, unroll=True)
    def _(step):
        at = pl.ds(pl.multiple_of(step * tile, tile), tile)
        for read_index in range(reads):
            query_block = queries[read_index, at, cols]
            grad_block = out_grad[read_index, at, cols]
            scores = last_contract(keys[...], query_block) * (FACTOR * LOG2_E)
            weighted = last_contract(values[...], grad_block)
            probs = jnp.exp2(scores - stats[read_index : read_index + 1, at])
            delta = stats[reads + read_index : reads + read_index + 1, at]
            score_grad = (probs * (weighted - delta) * FACTOR).astype(jnp.bfloat16)
            score_grads[read_index, :, at] = score_grad
            key_acc[...] += plain_dot(score_grad, query_block)
            value_acc[...] += plain_dot(probs.astype(jnp.bfloat16), grad_block)

    grads[:, :HD] = key_acc[...].astype(jnp.bfloat16)
    grads[:, HD:] = value_acc[...].astype(jnp.bfloat16)
    weights_ref[...] = rows_contract(inputs[...], grads[...])
    features = inputs.shape[1]
    piece = features // GROUPS
    me = lax.axis_index(row_axis) // low
    for part, (begin, end, bits) in enumerate(WEIGHT_PARTS[head_index]):
        for first in range(2):
            ref = weight_parts[2 * part + first]
            for second in range(2):
                for high in range(2):
                    group = group_at(bits, (first, second), high, me)
                    start = pl.multiple_of(group * piece, piece)
                    ref[second, high] = weights_ref[pl.ds(start, piece), begin:end]


def input_kernel(head_axis, key_weight, value_weight, *refs):
    head_grads, (_, input_keep, input_send, total) = refs[:-4], refs[-4:]
    for head_index, grads in enumerate(head_grads):
        cols = slice(head_index * HD, (head_index + 1) * HD)
        part = last_contract(grads[:, :HD], key_weight[:, cols])
        part += last_contract(grads[:, HD:], value_weight[:, cols])
        total[...] = total[...] + part if head_index else part
    place = lax.axis_index(head_axis)
    shares = 2 * input_keep.shape[0]
    width = total.shape[1] // shares
    for relative in range(shares):
        ref = input_send if relative >= shares // 2 else input_keep
        start = pl.multiple_of((place ^ relative) * width, width)
        ref[relative % (shares // 2)] = total[:, pl.ds(start, width)]


def query_kernel(parts, row_axis, low, after, score_grads, keys, *refs):
    del after
    tile_ref = refs[-1]
    reads, _, latents = score_grads.shape
    piece = latents // GROUPS
    me = lax.axis_index(row_axis) // low
    side = lax.rem(me, 2)
    for part, (begin, end, bits) in enumerate(parts):
        for read_index in range(begin, end):
            for pair in range(GROUPS // 2):
                at = slice(pair * 2 * piece, (pair + 1) * 2 * piece)
                tile_ref[pair * reads + read_index] = rows_contract(
                    score_grads[read_index, :, at], keys[...]
                )
        for upper in range(GROUPS // 2):
            pair = counted(counted(me) ^ (2 * upper)) // 2
            for read_index in range(begin, end):
                slot = pair * reads + read_index
                for flip in range(2):
                    half = pl.ds(pl.multiple_of((side ^ flip) * piece, piece), piece)
                    relative = 2 * upper + flip
                    ref = refs[2 * part + (1 if relative & bits[0] else 0)]
                    index = 2 * ((relative & bits[1]) // bits[1]) + (relative & bits[2]) // bits[2]
                    ref[index, read_index - begin] = tile_ref[slot, half, :]


def weights_kernel(weight_parts, row_axis, low, *refs):
    key_out, value_out, input_out, done = refs[-4:]
    refs = list(refs[:-4])
    input_out[...] = refs.pop(0)[0] + refs.pop(0)[0]
    done[...] = jnp.zeros_like(done)
    piece = key_out.shape[0] // GROUPS
    me = lax.axis_index(row_axis) // low
    for head_index, begin, end, bits in weight_parts:
        cols = slice(head_index * HD, (head_index + 1) * HD)
        for first in range(2):
            source = refs.pop(0)
            for second in range(2):
                for high in range(2):
                    group = group_at(bits, (first, second), high, me)
                    start = pl.multiple_of(group * piece, piece)
                    at = pl.ds(start, piece)
                    if begin == 0:
                        key_out[at, cols] = source[second, high, :, :HD]
                    if end == 2 * HD:
                        value_out[at, cols] = source[second, high, :, end - begin - HD :]


def queries_kernel(query_parts, after, *refs):
    del after
    query_out = refs[-1]
    refs = list(refs[:-1])
    for head_index, begin, end, terms in query_parts:
        cols = slice(head_index * HD, (head_index + 1) * HD)
        total = refs.pop(0)[0]
        for _ in range(terms - 1):
            total = total + refs.pop(0)[0]
        query_out[begin:end, :, cols] = total


def shape_of(shape, dtype=jnp.float32):
    return jax.ShapeDtypeStruct(shape, dtype)


def add_kernel(mine, theirs, after, total):
    del after
    total[...] = mine[...] + theirs[...]


def on_device(row_devices, head_devices, inputs, key_weight, value_weight, queries, out_grad):
    reads, latents, columns = queries.shape
    head_count = columns // HD
    row_count, features = inputs.shape
    low = row_devices // GROUPS
    tile = latents // (GROUPS // 2)
    piece = features // GROUPS
    operands = (inputs, key_weight, value_weight, queries, out_grad)
    block_work = pl.CostEstimate(
        flops=8 * reads * row_count * latents * HD,
        bytes_accessed=4 * 2**20,
        transcendentals=reads * row_count * latents,
    )

    projected = []
    for head_index in range(head_count):
        first = head_index == 0
        loaded = [
            pltpu.VMEM(item.shape[:-1] + ((HD,) if place else item.shape[-1:]), item.dtype)
            for place, item in enumerate(operands)
        ]
        projected.append(
            pl.pallas_call(
                functools.partial(first_kernel, tile)
                if first
                else functools.partial(later_kernel, latents // 2, head_index),
                out_shape=(
                    shape_of((row_count, HD), jnp.bfloat16),
                    shape_of((row_count, HD), jnp.bfloat16),
                    shape_of((2 * reads, latents)),
                ),
                in_specs=[HBM if first else VMEM] * 5,
                out_specs=(VMEM,) * 3,
                scratch_shapes=loaded + [pltpu.SemaphoreType.DMA((5,))] if first else [],
                compiler_params=params(57 if first else 16),
                cost_estimate=block_work,
                name="project",
            )(*operands)
        )

    stats_parts = []
    for head_index in range(head_count):
        stats = projected[head_index][2]
        for bit in bits_of(row_devices)[:-1]:
            theirs = swap(stats, "rows", row_devices, bit)
            stats = pl.pallas_call(
                merge_kernel,
                out_shape=shape_of(stats.shape),
                in_specs=[VMEM] * 2,
                out_specs=VMEM,
                compiler_params=params(2),
                name="merge",
            )(stats, theirs)
        stats_parts.append((stats, swap(stats, "rows", row_devices, bits_of(row_devices)[-1])))

    order_low = (lax.axis_index("rows") % low) ^ jnp.arange(low, dtype=jnp.int32)
    low_bits = [bit for bit in bits_of(row_devices) if bit < low]

    def scatter_low(block, axis):
        if low == 1:
            return block
        parts = jnp.moveaxis(
            block.reshape(block.shape[:axis] + (low, -1) + block.shape[axis + 1 :]), axis, 0
        )
        parts = jnp.take(parts, order_low, axis=0)
        for bit in low_bits:
            parts = parts.reshape((-1, 2) + parts.shape[1:])
            parts = parts[:, 0] + swap(parts[:, 1], "rows", row_devices, bit)
        return parts[0]

    def sum_low(block):
        for bit in low_bits:
            block = block + row_swap(block, bit=bit)
        return block

    row_swap = functools.partial(row_swap_of, count=row_devices)

    def kernel_call(kernel, shapes, operands, scratch, limit, name):
        return pl.pallas_call(
            kernel,
            out_shape=[shape_of(*item) for item in shapes],
            in_specs=[ANY] + [VMEM] * (len(operands) - 1),
            out_specs=[VMEM] * len(shapes),
            scratch_shapes=scratch,
            compiler_params=params(limit),
            cost_estimate=block_work,
            name=name,
        )(*operands)

    grads_out, weight_steps, marks = [], [], {}
    for head_index in range(head_count):
        keys, values, _ = projected[head_index]
        results = kernel_call(
            functools.partial(grads_kernel, head_index, "rows", low),
            [((row_count, 2 * HD), jnp.bfloat16), ((reads, row_count, latents), jnp.bfloat16)]
            + [
                ((2, 2, piece, end - begin),)
                for begin, end, _ in WEIGHT_PARTS[head_index]
                for _ in range(2)
            ],
            [
                grads_out[-1][0] if grads_out else stats_parts[0][0],
                *(inputs, keys, values, queries, out_grad),
                *stats_parts[head_index],
            ],
            [
                pltpu.VMEM((row_count, HD), jnp.float32),
                pltpu.VMEM((row_count, HD), jnp.float32),
                pltpu.VMEM((features, 2 * HD), jnp.float32),
                pltpu.VMEM((2 * reads, latents), jnp.float32),
            ],
            20,
            "grads",
        )
        grads_out.append(results)
        marks[f"A{head_index}"] = results[0]
        for part, (begin, end, bits) in enumerate(WEIGHT_PARTS[head_index]):
            keep, send = results[2 + 2 * part : 4 + 2 * part]
            theirs = row_swap(send, bit=bits[0] * low)
            send = keep[1:] + theirs[1:]
            mine = keep[:1] + theirs[:1]
            marks[f"w{head_index}.1"] = send
            weight_steps.append((mine, row_swap(send, bit=bits[1] * low)))

    query_terms, query_list = [], []
    for head_index in range(head_count):
        results = kernel_call(
            functools.partial(query_kernel, QUERY_PARTS[head_index], "rows", low),
            [
                ((GROUPS // 2, end - begin, latents // GROUPS, HD),)
                for begin, end, _ in QUERY_PARTS[head_index]
                for _ in range(2)
            ],
            [
                marks[AFTER.get(f"B{head_index}", f"A{head_index}")],
                grads_out[head_index][1],
                projected[head_index][0],
            ],
            [pltpu.VMEM((GROUPS // 2 * reads, tile, HD), jnp.float32)],
            16,
            "query",
        )
        marks[f"B{head_index}"] = results[0]
        for part, (begin, end, bits) in enumerate(QUERY_PARTS[head_index]):
            keep, send = results[2 * part : 2 * part + 2]
            for place, bit in enumerate(bits):
                theirs = row_swap(send, bit=bit * low)
                if place + 1 < len(bits):
                    middle = keep.shape[0] // 2
                    send = keep[middle:] + theirs[middle:]
                    keep = keep[:middle] + theirs[:middle]
                    marks[f"q{head_index}.{place + 1}"] = send
            terms = [keep, theirs]
            if low > 1:
                terms = [scatter_low((keep + theirs)[0], 1)[None]]
            query_terms += terms
            query_list.append((head_index, begin, end, len(terms)))

    def added(kernel, shape, mine, theirs, after):
        return pl.pallas_call(
            kernel,
            out_shape=shape_of(shape),
            in_specs=[VMEM, VMEM, ANY],
            out_specs=VMEM,
            compiler_params=params(4),
            cost_estimate=pl.CostEstimate(flops=1024, bytes_accessed=1024, transcendentals=0),
            name="added",
        )(mine, theirs, after)

    weight_terms, weight_list = [], []
    for head_index in range(head_count):
        for begin, end, bits in WEIGHT_PARTS[head_index]:
            mine, theirs = weight_steps.pop(0)
            first, second = (bit * low for bit in bits)
            for place, bit in ((2, LAST_BIT * low), (3, second)):
                after = AFTER.get(f"w{head_index}.{place}")
                if after:
                    mine = added(add_kernel, mine.shape, mine, theirs, marks[after])
                else:
                    mine = mine + theirs
                if place == 3:
                    mine = sum_low(mine)
                theirs = row_swap(mine, bit=bit)
                marks[f"w{head_index}.{place}"] = mine
            near = jnp.concatenate([mine, theirs], axis=0)
            weight_terms += [near, row_swap(near, bit=first)]
            weight_list.append((head_index, begin, end, bits))

    share = ((head_devices // 2, row_count, features // head_devices),)
    after = marks[AFTER.get("i.0", "B1")]
    input_keep, input_send = pl.pallas_call(
        functools.partial(input_kernel, "heads"),
        out_shape=[shape_of(*share)] * 2,
        in_specs=[VMEM] * (2 + head_count) + [ANY],
        out_specs=[VMEM] * 2,
        scratch_shapes=[pltpu.VMEM((row_count, features), jnp.float32)],
        compiler_params=params(16),
        cost_estimate=block_work,
        name="input",
    )(key_weight, value_weight, *(item[0] for item in grads_out), after)
    head_bits = bits_of(head_devices)[::-1]
    keep, theirs = input_keep, swap(input_send, "heads", head_devices, head_bits[0])
    for bit in head_bits[1:]:
        send = keep[bit:] + theirs[bit:]
        keep, theirs = keep[:bit] + theirs[:bit], swap(send, "heads", head_devices, bit)
    input_terms = (keep, theirs)

    key_weight_grad, value_weight_grad, input_grad, done = pl.pallas_call(
        functools.partial(weights_kernel, weight_list, "rows", low),
        out_shape=(shape_of((features, columns)),) * 2
        + (shape_of((row_count, features // head_devices)), shape_of((8, 128))),
        in_specs=[VMEM] * (2 + len(weight_terms)),
        out_specs=(VMEM,) * 4,
        compiler_params=params(8),
        name="weights",
    )(*input_terms, *weight_terms)
    query_grad = pl.pallas_call(
        functools.partial(queries_kernel, query_list),
        out_shape=shape_of((reads, latents // row_devices, columns)),
        in_specs=[ANY] + [VMEM] * len(query_terms),
        out_specs=VMEM,
        compiler_params=params(4),
        name="queries",
    )(done, *query_terms)
    return (query_grad, key_weight_grad, value_weight_grad, input_grad)


def solution(mesh):
    in_specs = (
        P("rows", None),
        P(None, "heads"),
        P(None, "heads"),
        P(None, None, "heads"),
        P(None, None, "heads"),
    )
    out_specs = (P(None, "rows", "heads"), P(None, "heads"), P(None, "heads"), P("rows", "heads"))

    def body(*args):
        return on_device(mesh.shape["rows"], mesh.shape["heads"], *args)

    return jax.shard_map(body, mesh=mesh, in_specs=in_specs, out_specs=out_specs, check_vma=False)
```
